512 devices in a mesh: blk: 2 (over core), ctx: 32 (over y, x), tp: 8 (over z).
Axes of the slice: x: 4, y: 8, z: 8, core: 2. Of those that a mesh axis runs over, the one named last changes fastest.
Arguments:
- queries: bfloat16 [8192, 5120], P(('blk', 'ctx'), 'tp'), may hold values from -5 to 5
- keys: bfloat16 [8192, 5120], P(('blk', 'ctx'), 'tp'), may hold values from -5 to 5
- values: bfloat16 [8192, 5120], P(('blk', 'ctx'), 'tp'), may hold values from -6 to 6
- lengths: int32 [32], replicated, may hold values from 1 to 5120, 8192 in all
Outputs:
- attended: bfloat16 [8192, 5120], P(('blk', 'ctx'), 'tp')
The draws below stay inside these ranges and needn't reach their ends.
Inputs may be any that keep to these rules, and one draw needn't show every extreme that they name: The lengths sum to 8192.
All inputs are finite; a program needn't handle non-finite values.
Results may differ from the reference program's by a relative error of at most 0.006.
Values may be sent and summed in bfloat16 or wider, within the bound.
No kernel may reach another device: no remote copies, remote signals or barrier semaphores. Data moves between devices by JAX's collectives and lax.ppermute only.
A program may use at most 64 MiB of HBM per device.

```python
import math
import jax
import jax.numpy as jnp
import numpy as np
from jax import lax

HEAD_DIM = 128
HEADS = 40
DOCS = 32
TOKENS = 8192
LONGEST = 5120


def draw_queries(key, part):
    key = jax.random.fold_in(key, 1)
    shape_full = (TOKENS, HEADS * HEAD_DIM)
    return jnp.clip(jax.random.normal(key, shape_full, jnp.float32), -4.0, 4.0).astype(jnp.bfloat16)


def draw_keys(key, part):
    key = jax.random.fold_in(key, 2)
    shape_full = (TOKENS, HEADS * HEAD_DIM)
    return jnp.clip(jax.random.normal(key, shape_full, jnp.float32), -4.0, 4.0).astype(jnp.bfloat16)


def draw_values(key, part):
    key = jax.random.fold_in(key, 3)
    shape_full = (TOKENS, HEADS * HEAD_DIM)
    return jnp.clip(jax.random.normal(key, shape_full, jnp.float32), -6.0, 6.0).astype(jnp.bfloat16)


def split_up(amount, total, most, slope):
    weights = [(1 << 20) // math.isqrt(rank ** slope) + 1 for rank in range(2, amount + 1)]
    surplus, given = total - most - (amount - 1), [1] * (amount - 1)
    while surplus > 0:
        candidates = [i for i in range(amount - 1) if given[i] < most]
        pool, remaining = sum([weights[i] for i in candidates]), surplus
        for i in candidates:
            extra = min(most - given[i], max(1, remaining * weights[i] // pool), surplus)
            given[i] = given[i] + extra
            surplus = surplus - extra
    return np.array([most] + given)


def ragged(stream_key, amount, total, most, slope):
    if amount == 2:
        one = jax.random.randint(stream_key, (), max(1, total - most), min(most, total - 1) + 1)
        return jnp.stack([one, total - one])
    sizes = jnp.asarray(split_up(amount, total, most, slope), jnp.int32)
    pairs = (amount - 1) // 2
    giver, sink = sizes[1:1 + 2 * pairs:2], sizes[2:2 + 2 * pairs:2]
    margin = jnp.minimum(giver - 1, most - sink)
    shifted = jax.random.randint(jax.random.fold_in(stream_key, 1), (pairs,), 0, 1 << 20) % (margin + 1)
    sizes = sizes.at[1:1 + 2 * pairs:2].set(giver - shifted).at[2:2 + 2 * pairs:2].set(sink + shifted)
    return sizes[jax.random.permutation(jax.random.fold_in(stream_key, 2), amount)]


def setup_inputs(seed: int = 0) -> dict:
    streams_of = jax.random.split(jax.random.key(seed), 5)
    return {
        "queries": draw_queries(jax.random.fold_in(streams_of[4], 71), 0),
        "keys": draw_keys(jax.random.fold_in(streams_of[4], 71), 0),
        "values": draw_values(jax.random.fold_in(streams_of[4], 71), 0),
        "lengths": ragged(streams_of[3], DOCS, TOKENS, LONGEST, 2).astype(jnp.int32),
    }


NEG = -1.0e30


def reference(queries, keys, values, lengths):
    doc_ends = jnp.cumsum(lengths).astype(jnp.int32)
    doc_starts = (doc_ends - lengths).astype(jnp.int32)
    positions = jnp.arange(TOKENS, dtype=jnp.int32)
    inside = (positions[:, None] >= doc_starts[None, :]) & (positions[:, None] < doc_ends[None, :])
    first = jnp.sum(jnp.where(inside, doc_starts[None, :], 0), axis=1).astype(jnp.int32)
    block_size = min(1024, TOKENS)
    block_count = TOKENS // block_size
    scale = 1.0 / (HEAD_DIM ** 0.5)
    heads_for_query = queries.reshape(TOKENS, HEADS, HEAD_DIM).transpose(1, 0, 2)
    heads_for_key = keys.reshape(TOKENS, HEADS, HEAD_DIM).transpose(1, 0, 2)
    value_heads = values.reshape(TOKENS, HEADS, HEAD_DIM).transpose(1, 0, 2)

    def one_head(inputs):
        query_one, key_one, value_one = inputs

        def one_block(block_index):
            begin = (block_index * block_size).astype(jnp.int32)
            query_rows = lax.dynamic_slice_in_dim(query_one, begin, block_size, 0)
            row_position = lax.dynamic_slice_in_dim(positions, begin, block_size, 0)
            row_first = lax.dynamic_slice_in_dim(first, begin, block_size, 0)
            scores = jnp.dot(query_rows, key_one.T, preferred_element_type=jnp.float32) * scale
            allowed = (positions[None, :] >= row_first[:, None]) & (positions[None, :] <= row_position[:, None])
            scores = jnp.where(allowed, scores, NEG)
            peak = jnp.max(scores, axis=1, keepdims=True)
            weights = jnp.where(allowed, jnp.exp(scores - peak), 0.0)
            total = jnp.sum(weights, axis=1, keepdims=True)
            weighted = jnp.dot(weights.astype(jnp.bfloat16), value_one, preferred_element_type=jnp.float32)
            return (weighted / total).astype(jnp.bfloat16)

        blocks = lax.map(one_block, jnp.arange(block_count, dtype=jnp.int32))
        return blocks.reshape(TOKENS, HEAD_DIM)

    result = lax.map(one_head, (heads_for_query, heads_for_key, value_heads))
    return result.transpose(1, 0, 2).reshape(TOKENS, HEADS * HEAD_DIM)
```

```python
import math

import jax
import jax.numpy as jnp
from jax import lax
from jax.experimental import pallas as pl
from jax.experimental.pallas import tpu as pltpu
from jax.sharding import Mesh, PartitionSpec as P

HEAD_DIM = 128
ROWS = 128
X = 4
Y = 8
HEADS = 5
DOCS = 32
KEY_BLOCK = X * ROWS
GROUP = Y * KEY_BLOCK
NEG = -1e30
C = math.log2(math.e) / math.sqrt(HEAD_DIM)


def pack_kernel(q_ref, k_ref, v_ref, kv_out, q_out):
    for h in range(HEADS):
        cols = slice(h * HEAD_DIM, (h + 1) * HEAD_DIM)
        kv_out[h, :ROWS, :] = k_ref[:, cols]
        kv_out[h, ROWS:, :] = v_ref[:, cols].T
        q_out[h] = q_ref[:, cols]


def pack(q, k, v):
    return pl.pallas_call(
        pack_kernel,
        out_shape=(
            jax.ShapeDtypeStruct((Y, ROWS + HEAD_DIM, HEAD_DIM), jnp.bfloat16),
            jax.ShapeDtypeStruct((Y, ROWS, HEAD_DIM), jnp.bfloat16),
        ),
        name="pack",
    )(q, k, v)


def unpack_kernel(o_ref, out_ref):
    for h in range(HEADS):
        out_ref[:, h * HEAD_DIM : (h + 1) * HEAD_DIM] = o_ref[h]


def unpack(o):
    return pl.pallas_call(
        unpack_kernel,
        out_shape=jax.ShapeDtypeStruct((ROWS, HEADS * HEAD_DIM), jnp.bfloat16),
        name="unpack",
    )(o)


def attend_kernel(place_ref, len_ref, q_ref, own_ref, prev_ref, o_ref, first_ref, lo_ref):
    blk, x, slot = place_ref[0], place_ref[1], place_ref[2]
    base = blk * GROUP
    off = base + x * ROWS

    @pl.when(slot < HEADS)
    def _():
        pos = (
            off
            + lax.broadcasted_iota(jnp.int32, (Y, ROWS), 0) * KEY_BLOCK
            + lax.broadcasted_iota(jnp.int32, (Y, ROWS), 1)
        )
        first = jnp.zeros((Y, ROWS), jnp.int32)
        los = [jnp.int32(0)] * Y
        start = jnp.int32(0)
        for j in range(DOCS - 1):
            start = start + len_ref[j]
            first = jnp.where(pos >= start, start, first)
            los = [jnp.where(off + y * KEY_BLOCK >= start, start, los[y]) for y in range(Y)]
        first_ref[...] = first
        for y in range(Y):
            lo_ref[y] = los[y]

        def chunk(y, _):
            q = q_ref[y]
            first_row = first_ref[pl.ds(y, 1), :]
            t_row = off + y * KEY_BLOCK + lax.broadcasted_iota(jnp.int32, (1, ROWS), 1)
            lo = lo_ref[y]
            rows = lax.broadcasted_iota(jnp.int32, (KEY_BLOCK, ROWS), 0)

            def step(ref, j, key_base, carry):
                m, l, acc = carry
                s = jnp.concatenate(
                    [
                        lax.dot_general(
                            ref[i, j, :ROWS, :],
                            q,
                            (((1,), (1,)), ((), ())),
                            preferred_element_type=jnp.float32,
                        )
                        for i in range(X)
                    ],
                    axis=0,
                )
                u = rows + (key_base + j * KEY_BLOCK)
                s = jnp.where((u >= first_row) & (u <= t_row), s * C, NEG)
                m_new = jnp.maximum(m, jnp.max(s, axis=0, keepdims=True))
                alpha = jnp.exp2(m - m_new)
                p = jnp.exp2(s - m_new)
                l = l * alpha + jnp.sum(p, axis=0, keepdims=True)
                pb = p.astype(jnp.bfloat16)
                acc = acc * alpha
                for i in range(X):
                    acc = acc + jnp.dot(
                        ref[i, j, ROWS:, :],
                        pb[i * ROWS : (i + 1) * ROWS],
                        preferred_element_type=jnp.float32,
                    )
                return m_new, l, acc

            carry = (
                jnp.full((1, ROWS), NEG, jnp.float32),
                jnp.zeros((1, ROWS), jnp.float32),
                jnp.zeros((HEAD_DIM, ROWS), jnp.float32),
            )
            own_count = y + 1 - lax.shift_right_logical(jnp.maximum(lo - base, 0), 9)
            carry = lax.fori_loop(
                0, own_count, lambda n, c: step(own_ref, y - n, base, c), carry
            )
            prev_count = jnp.where(
                blk > 0, jnp.maximum(Y - lax.shift_right_logical(lo, 9), 0), 0
            )
            carry = lax.fori_loop(
                0, prev_count, lambda n, c: step(prev_ref, Y - 1 - n, 0, c), carry
            )
            m, l, acc = carry
            o_ref[y] = (acc / l).T.astype(jnp.bfloat16)
            return 0

        lax.fori_loop(0, Y, chunk, 0)


def attend(place, lengths, q, own, prev):
    smem = pl.BlockSpec(memory_space=pltpu.SMEM)
    vmem = pl.BlockSpec(memory_space=pltpu.VMEM)
    return pl.pallas_call(
        attend_kernel,
        out_shape=jax.ShapeDtypeStruct((Y, ROWS, HEAD_DIM), jnp.bfloat16),
        in_specs=[smem, smem, vmem, vmem, vmem],
        out_specs=vmem,
        scratch_shapes=[pltpu.VMEM((Y, ROWS), jnp.int32), pltpu.SMEM((Y,), jnp.int32)],
        compiler_params=pltpu.CompilerParams(vmem_limit_bytes=24 << 20),
        name="attend",
    )(place, lengths, q, own, prev)


def body(queries, keys, values, lengths):
    place = jnp.stack([lax.axis_index("blk"), lax.axis_index("x"), lax.axis_index("y")])
    kv, q = pack(queries, keys, values)
    kv = lax.all_to_all(kv, "y", 0, 0, tiled=True)
    own = lax.all_gather(kv, "x")
    q = lax.all_to_all(q, "y", 0, 0, tiled=True)
    prev = lax.ppermute(own, "blk", [(0, 1)])
    o = attend(place.astype(jnp.int32), lengths, q, own, prev)
    o = lax.all_to_all(o, "y", 0, 0, tiled=True)
    return unpack(o)


def solution(mesh):
    devices = mesh.devices.reshape(2, Y, X, mesh.devices.shape[2])
    fine = Mesh(devices, ("blk", "y", "x", "tp"))
    rows = P(("blk", "y", "x"), "tp")
    return jax.shard_map(
        body, mesh=fine, in_specs=(rows, rows, rows, P()), out_specs=rows, check_vma=False
    )
```

```python
import math

import jax
import jax.numpy as jnp
from jax import lax
from jax.experimental import pallas as pl
from jax.experimental.pallas import tpu as pltpu
from jax.sharding import Mesh, PartitionSpec as P

HEAD_DIM = 128
ROWS = 128
X = 4
Y = 8
HEADS = 5
DOCS = 32
KEY_BLOCK = X * ROWS
BLOCK_SHIFT = 9
GROUP = Y * KEY_BLOCK
TILE = 2 * ROWS
HALF = Y // 2
NEG = -1e30
C = math.log2(math.e) / math.sqrt(HEAD_DIM)


def pack_kernel(q_ref, k_ref, v_ref, out_ref):
    for h in range(HEADS):
        cols = slice(h * HEAD_DIM, (h + 1) * HEAD_DIM)
        out_ref[h, :ROWS, :] = q_ref[:, cols]
        out_ref[h, ROWS : 2 * ROWS, :] = k_ref[:, cols]
        out_ref[h, 2 * ROWS :, :] = v_ref[:, cols].T


def pack(q, k, v):
    return pl.pallas_call(
        pack_kernel,
        out_shape=jax.ShapeDtypeStruct((Y, 2 * ROWS + HEAD_DIM, HEAD_DIM), jnp.bfloat16),
        name="pack",
    )(q, k, v)


def unpack_kernel(o_ref, out_ref):
    for h in range(HEADS):
        out_ref[:, h * HEAD_DIM : (h + 1) * HEAD_DIM] = o_ref[h]


def unpack(o):
    return pl.pallas_call(
        unpack_kernel,
        out_shape=jax.ShapeDtypeStruct((ROWS, HEADS * HEAD_DIM), jnp.bfloat16),
        name="unpack",
    )(o)


def attend_kernel(
    place_ref, len_ref, q_ref, *refs
):
    parts, prev_parts = refs[:5], refs[5:10]
    o_ref, first_ref, lo_ref, hi_ref, kv_ref, s_ref, sems = refs[10:]
    blk, x, slot = place_ref[0], place_ref[1], place_ref[2]
    off = blk * GROUP + x * ROWS

    def copies(sources, group, sem):
        back, ahead, far = (x + X - 1) & (X - 1), (x + 1) & (X - 1), (x + 2) & (X - 1)
        lower, upper = pl.ds(0, HALF), pl.ds(HALF, HALF)
        places = [
            kv_ref.at[group, x],
            kv_ref.at[group, back],
            kv_ref.at[group, ahead],
            kv_ref.at[group, far, lower],
            kv_ref.at[group, far, upper],
        ]
        return [
            pltpu.make_async_copy(source, place, sems.at[sem + n])
            for n, (source, place) in enumerate(zip(sources, places))
        ]

    @pl.when(slot < HEADS)
    def _():
        for copy in copies(parts, blk, 0):
            copy.start()

        @pl.when(blk > 0)
        def _():
            for copy in copies(prev_parts, 0, 5):
                copy.start()

        pos = (
            off
            + lax.broadcasted_iota(jnp.int32, (Y, ROWS), 0) * KEY_BLOCK
            + lax.broadcasted_iota(jnp.int32, (Y, ROWS), 1)
        )
        first = jnp.zeros((Y, ROWS), jnp.int32)
        los = [jnp.int32(0)] * (Y // 2)
        his = [jnp.int32(0)] * (Y // 2)
        start = jnp.int32(0)
        for j in range(DOCS - 1):
            start = start + len_ref[j]
            first = jnp.where(pos >= start, start, first)
            for i in range(Y // 2):
                lowest = off + 2 * i * KEY_BLOCK
                highest = lowest + KEY_BLOCK + ROWS - 1
                los[i] = jnp.where(lowest >= start, start, los[i])
                his[i] = jnp.where(highest >= start, start, his[i])
        first_ref[...] = first
        for i in range(Y // 2):
            lo_ref[i] = los[i]
            hi_ref[i] = his[i]

        for copy in copies(parts, blk, 0):
            copy.wait()

        @pl.when(blk > 0)
        def _():
            for copy in copies(prev_parts, 0, 5):
                copy.wait()

        def tile(i, _):
            q = jnp.concatenate([q_ref[2 * i], q_ref[2 * i + 1]], axis=0)
            first_row = jnp.concatenate(
                [first_ref[pl.ds(2 * i, 1), :], first_ref[pl.ds(2 * i + 1, 1), :]], axis=1
            )
            lane = lax.broadcasted_iota(jnp.int32, (1, TILE), 1)
            t_row = (
                off
                + 2 * i * KEY_BLOCK
                + lax.shift_right_logical(lane, 7) * KEY_BLOCK
                + (lane & (ROWS - 1))
            )
            diagonal = blk * Y + 2 * i
            lo_block = lax.shift_right_logical(lo_ref[i], BLOCK_SHIFT)
            end_block = diagonal + 2
            hi = hi_ref[i]
            rows = lax.broadcasted_iota(jnp.int32, (ROWS, TILE), 0)

            def score(g, m):
                group, j = lax.shift_right_logical(g, 3), g & (Y - 1)

                def part(n):
                    return lax.dot_general(
                        kv_ref[group, n, j, :ROWS, :],
                        q,
                        (((1,), (1,)), ((), ())),
                        preferred_element_type=jnp.float32,
                    )

                def keep(n, s, m):
                    s_ref[g, n * ROWS : (n + 1) * ROWS, :] = s
                    return jnp.maximum(m, jnp.max(s.reshape(ROWS // 8, 8, TILE), axis=0))

                def masked(m):
                    for n in range(X):
                        u = rows + (g * KEY_BLOCK + n * ROWS)
                        s = jnp.where((u >= first_row) & (u <= t_row), part(n), NEG)
                        m = keep(n, s, m)
                    return m

                def whole(m):
                    for n in range(X):
                        m = keep(n, part(n), m)
                    return m

                edge = (g >= diagonal) | (g * KEY_BLOCK < hi)
                return lax.cond(edge, masked, whole, m)

            m = lax.fori_loop(
                lo_block, end_block, score, jnp.full((8, TILE), NEG, jnp.float32)
            )
            shift = jnp.max(m, axis=0, keepdims=True) * C

            def mix(g, carry):
                l, acc = carry
                group, j = lax.shift_right_logical(g, 3), g & (Y - 1)
                for n in range(0, X, 2):
                    p = jnp.exp2(s_ref[g, n * ROWS : (n + 2) * ROWS, :] * C - shift)
                    l = l + jnp.sum(p.reshape(2 * ROWS // 8, 8, TILE), axis=0)
                    v = jnp.concatenate(
                        [kv_ref[group, n, j, ROWS:, :], kv_ref[group, n + 1, j, ROWS:, :]],
                        axis=1,
                    )
                    acc = acc + jnp.dot(
                        v, p.astype(jnp.bfloat16), preferred_element_type=jnp.float32
                    )
                return l, acc

            l, acc = lax.fori_loop(
                lo_block,
                end_block,
                mix,
                (
                    jnp.zeros((8, TILE), jnp.float32),
                    jnp.zeros((HEAD_DIM, TILE), jnp.float32),
                ),
            )
            o = acc / jnp.sum(l, axis=0, keepdims=True)
            o_ref[2 * i] = o[:, :ROWS].T.astype(jnp.bfloat16)
            o_ref[2 * i + 1] = o[:, ROWS:].T.astype(jnp.bfloat16)
            return 0

        lax.fori_loop(0, Y // 2, tile, 0)


def attend(place, lengths, q, parts, prev_parts):
    smem = pl.BlockSpec(memory_space=pltpu.SMEM)
    vmem = pl.BlockSpec(memory_space=pltpu.VMEM)
    anywhere = pl.BlockSpec(memory_space=pl.ANY)
    return pl.pallas_call(
        attend_kernel,
        out_shape=jax.ShapeDtypeStruct((Y, ROWS, HEAD_DIM), jnp.bfloat16),
        in_specs=[smem, smem, vmem] + [anywhere] * 10,
        out_specs=vmem,
        scratch_shapes=[
            pltpu.VMEM((Y, ROWS), jnp.int32),
            pltpu.SMEM((Y // 2,), jnp.int32),
            pltpu.SMEM((Y // 2,), jnp.int32),
            pltpu.VMEM((2, X, Y, ROWS + HEAD_DIM, HEAD_DIM), jnp.bfloat16),
            pltpu.VMEM((2 * Y, KEY_BLOCK, TILE), jnp.float32),
            pltpu.SemaphoreType.DMA((10,)),
        ],
        compiler_params=pltpu.CompilerParams(vmem_limit_bytes=32 << 20),
        name="attend",
    )(place, lengths, q, *parts, *prev_parts)


def body(queries, keys, values, lengths):
    place = jnp.stack([lax.axis_index("blk"), lax.axis_index("x"), lax.axis_index("y")])
    packed = pack(queries, keys, values)
    got = lax.all_to_all(packed, "y", 0, 0, tiled=True)
    q, own = got[:, :ROWS], got[:, ROWS:]
    ahead = [(n, (n + 1) % X) for n in range(X)]
    back = [(n, (n - 1) % X) for n in range(X)]
    from_back = lax.ppermute(own, "x", ahead)
    from_ahead = lax.ppermute(own, "x", back)
    far_lower = lax.ppermute(from_back[:HALF], "x", ahead)
    far_upper = lax.ppermute(from_ahead[HALF:], "x", back)
    parts = (own, from_back, from_ahead, far_lower, far_upper)
    prev_parts = tuple(lax.ppermute(part, "blk", [(0, 1)]) for part in parts)
    o = attend(place.astype(jnp.int32), lengths, q, parts, prev_parts)
    o = lax.all_to_all(o, "y", 0, 0, tiled=True)
    return unpack(o)


def solution(mesh):
    devices = mesh.devices.reshape(2, Y, X, mesh.devices.shape[2])
    fine = Mesh(devices, ("blk", "y", "x", "tp"))
    rows = P(("blk", "y", "x"), "tp")
    return jax.shard_map(
        body, mesh=fine, in_specs=(rows, rows, rows, P()), out_specs=rows, check_vma=False
    )
```

```python
import math

import jax
import jax.numpy as jnp
from jax import lax
from jax.experimental import pallas as pl
from jax.experimental.pallas import tpu as pltpu
from jax.sharding import PartitionSpec as P

HEAD_DIM = 128
ROWS = 128
X = 4
Y = 8
CHIPS = X * Y
HEADS = 5
DOCS = 32
PARTS = 4
PART = ROWS // 2
SPAN = X * ROWS
SPAN_SHIFT = 9
GROUP = Y * SPAN
TILE = X * PART
STATS = 16
NEG = -1e30
LOG2E = math.log2(math.e)
C = LOG2E / math.sqrt(HEAD_DIM)


def pack_kernel(q_ref, k_ref, v_ref, out_ref):
    for chip in range(HEADS * PARTS):
        h, k_part, q_part = chip // PARTS, chip // 2 % 2, chip % 2
        cols = slice(h * HEAD_DIM, (h + 1) * HEAD_DIM)
        k_rows = slice(k_part * PART, (k_part + 1) * PART)
        q_rows = slice(q_part * PART, (q_part + 1) * PART)
        out_ref[chip, :PART, :] = q_ref[q_rows, cols]
        out_ref[chip, PART : 2 * PART, :] = k_ref[k_rows, cols]
        out_ref[chip, 2 * PART :, :] = v_ref[k_rows, cols]


def pack(q, k, v):
    return pl.pallas_call(
        pack_kernel,
        out_shape=jax.ShapeDtypeStruct((CHIPS, 3 * PART, HEAD_DIM), jnp.bfloat16),
        name="pack",
    )(q, k, v)


def combine_kernel(place_ref, in_ref, out_ref):
    odd = (place_ref[1] & 1) == 1
    rows = []
    for chip in range(HEADS * PARTS):
        terms = in_ref[chip, PART:, :].astype(jnp.float32)
        row = terms[0:1] + terms[1:2] + terms[2:3]
        rows.append(jnp.where(odd, pltpu.roll(row, PART, 1), row))
    shares = []
    for h in range(HEADS):
        for q_part in range(2):
            a, b = rows[h * PARTS + q_part], rows[h * PARTS + 2 + q_part]
            top = jnp.maximum(a, b)
            a, b = jnp.exp2(a - top), jnp.exp2(b - top)
            shares += [a / (a + b), b / (a + b)]
    shares = jnp.concatenate(shares + [jnp.zeros((12, ROWS), jnp.float32)], axis=0).T
    for h in range(HEADS):
        for q_part in range(2):
            n = 2 * (2 * h + q_part)
            a = in_ref[h * PARTS + q_part, :PART, :].astype(jnp.float32)
            b = in_ref[h * PARTS + 2 + q_part, :PART, :].astype(jnp.float32)
            o = a * shares[:PART, n : n + 1] + b * shares[:PART, n + 1 : n + 2]
            out_ref[
                q_part * PART : (q_part + 1) * PART, h * HEAD_DIM : (h + 1) * HEAD_DIM
            ] = o.astype(jnp.bfloat16)


def combine(place, parts):
    return pl.pallas_call(
        combine_kernel,
        out_shape=jax.ShapeDtypeStruct((ROWS, HEADS * HEAD_DIM), jnp.bfloat16),
        in_specs=[
            pl.BlockSpec(memory_space=pltpu.SMEM),
            pl.BlockSpec(memory_space=pltpu.VMEM),
        ],
        name="combine",
    )(place, parts)


def attend_kernel(
    place_ref,
    len_ref,
    own_ref,
    prev_ref,
    o_ref,
    first_ref,
    lo_ref,
    k_ref,
    vt_ref,
    even_ref,
    odd_ref,
):
    blk, chip = place_ref[0], place_ref[1]
    k_off = (lax.shift_right_logical(chip, 1) & 1) * PART
    off = blk * GROUP + (chip & 1) * PART

    def spread(n):
        return lax.shift_right_logical(n, 6) * ROWS + (n & (PART - 1))

    def load(ref, j, group):
        for n in range(X):
            k_ref[group, j, n * PART : (n + 1) * PART, :] = ref[j * X + n, PART : 2 * PART, :]
        v = jnp.concatenate([ref[j * X + n, 2 * PART :, :] for n in range(X)], axis=0)
        vt_ref[group, j] = v.T

    @pl.when(chip < HEADS * PARTS)
    def _():
        pos = (
            off
            + lax.broadcasted_iota(jnp.int32, (Y, TILE), 0) * SPAN
            + spread(lax.broadcasted_iota(jnp.int32, (Y, TILE), 1))
        )
        first = jnp.zeros((Y, TILE), jnp.int32)
        los = [jnp.int32(0)] * Y
        start = jnp.int32(0)
        for j in range(DOCS - 1):
            start = start + len_ref[j]
            first = jnp.where(pos >= start, start, first)
            los = [jnp.where(off + i * SPAN >= start, start, los[i]) for i in range(Y)]
        first_ref[...] = first
        for i in range(Y):
            lo_ref[i] = lax.shift_right_logical(los[i], SPAN_SHIFT)

        def load_own(j, _):
            load(own_ref, j, blk)
            return 0

        lax.fori_loop(0, Y, load_own, 0)

        @pl.when(blk > 0)
        def _():
            def load_prev(j, _):
                load(prev_ref, j, 0)
                return 0

            lax.fori_loop(lo_ref[0], Y, load_prev, 0)

        key_rows = k_off + spread(lax.broadcasted_iota(jnp.int32, (TILE, TILE), 0))
        lane = spread(lax.broadcasted_iota(jnp.int32, (1, TILE), 1))

        def queries(i):
            return jnp.concatenate([own_ref[i * X + n, :PART, :] for n in range(X)], axis=0)

        def score(s_ref, i, q, g, m, diagonal):
            s = lax.dot_general(
                k_ref[lax.shift_right_logical(g, 3), g & (Y - 1)],
                q,
                (((1,), (1,)), ((), ())),
                preferred_element_type=jnp.float32,
            )
            kept = key_rows >= first_ref[pl.ds(i, 1), :] - g * SPAN
            if diagonal:
                kept &= key_rows <= off - blk * GROUP + lane
            s = jnp.where(kept, s, NEG)
            s_ref[g] = s
            return jnp.maximum(m, jnp.max(s.reshape(TILE // 8, 8, TILE), axis=0))

        def mix(s_ref, g, shift, l, acc):
            p = jnp.exp2(s_ref[g] * C - shift)
            l = l + jnp.sum(p.reshape(TILE // 8, 8, TILE), axis=0)
            acc = acc + jnp.dot(
                vt_ref[lax.shift_right_logical(g, 3), g & (Y - 1)],
                p.astype(jnp.bfloat16),
                preferred_element_type=jnp.float32,
            )
            return l, acc

        def pairs(begin, end, step, carry):
            count = end - begin
            carry = lax.fori_loop(
                0,
                lax.shift_right_logical(count, 1),
                lambda n, c: step(begin + 2 * n + 1, step(begin + 2 * n, c)),
                carry,
            )
            return lax.fori_loop(0, count & 1, lambda n, c: step(end - 1, c), carry)

        none = jnp.full((8, TILE), NEG, jnp.float32)
        diagonal = blk * Y
        q = queries(0)
        m = score(even_ref, 0, q, diagonal, none, True)
        m = pairs(lo_ref[0], diagonal, lambda g, m: score(even_ref, 0, q, g, m, False), m)

        def tile(i, s_ref, later_ref, m):
            top = jnp.max(m, axis=0, keepdims=True)
            shift = jnp.where(top > 0.5 * NEG, top * C, 0.0)
            later = jnp.minimum(i + 1, Y - 1)
            q = queries(later)
            diagonal = blk * Y + later
            zeros = jnp.zeros((8, TILE), jnp.float32)

            def step(g, carry):
                m, l, acc = carry
                l, acc = mix(s_ref, g, shift, l, acc)
                return score(later_ref, later, q, g, m, False), l, acc

            m, l, acc = pairs(
                lo_ref[i],
                blk * Y + i + 1,
                step,
                (none, zeros, jnp.zeros((HEAD_DIM, TILE), jnp.float32)),
            )
            m = score(later_ref, later, q, diagonal, m, True)
            l = jnp.sum(l, axis=0, keepdims=True)
            some = l > 0.0
            o = (acc / jnp.where(some, l, 1.0)).T.astype(jnp.bfloat16)
            log = jnp.where(some, shift + jnp.log(jnp.where(some, l, 1.0)) * LOG2E, NEG)
            high = log.astype(jnp.bfloat16).astype(jnp.float32)
            middle = (log - high).astype(jnp.bfloat16).astype(jnp.float32)
            low = log - high - middle
            row = lax.broadcasted_iota(jnp.int32, (STATS, TILE), 0)
            stats = jnp.where(row == 0, high, jnp.where(row == 1, middle, low))
            stats = stats.astype(jnp.bfloat16)
            for n in range(X):
                o_ref[i * X + n, :PART, :] = o[n * PART : (n + 1) * PART]
                half = n // 2 * ROWS
                o_ref[i * X + n, PART:, :] = stats[:, half : half + ROWS]
            return m

        def two_tiles(i, m):
            m = tile(2 * i, even_ref, odd_ref, m)
            return tile(2 * i + 1, odd_ref, even_ref, m)

        lax.fori_loop(0, Y // 2, two_tiles, m)


def attend(place, lengths, own, prev):
    smem = pl.BlockSpec(memory_space=pltpu.SMEM)
    vmem = pl.BlockSpec(memory_space=pltpu.VMEM)
    return pl.pallas_call(
        attend_kernel,
        out_shape=jax.ShapeDtypeStruct((CHIPS, PART + STATS, HEAD_DIM), jnp.bfloat16),
        in_specs=[smem, smem, vmem, vmem],
        out_specs=vmem,
        scratch_shapes=[
            pltpu.VMEM((Y, TILE), jnp.int32),
            pltpu.SMEM((Y,), jnp.int32),
            pltpu.VMEM((2, Y, TILE, HEAD_DIM), jnp.bfloat16),
            pltpu.VMEM((2, Y, HEAD_DIM, TILE), jnp.bfloat16),
            pltpu.VMEM((2 * Y, TILE, TILE), jnp.float32),
            pltpu.VMEM((2 * Y, TILE, TILE), jnp.float32),
        ],
        compiler_params=pltpu.CompilerParams(vmem_limit_bytes=32 << 20),
        name="attend",
    )(place, lengths, own, prev)


def body(queries, keys, values, lengths):
    place = jnp.stack([lax.axis_index("blk"), lax.axis_index("ctx")]).astype(jnp.int32)
    own = lax.all_to_all(pack(queries, keys, values), "ctx", 0, 0, tiled=True)
    prev = lax.ppermute(own, "blk", [(0, 1)])
    parts = attend(place, lengths, own, prev)
    return combine(place, lax.all_to_all(parts, "ctx", 0, 0, tiled=True))


def solution(mesh):
    rows = P(("blk", "ctx"), "tp")
    return jax.shard_map(
        body, mesh=mesh, in_specs=(rows, rows, rows, P()), out_specs=rows, check_vma=False
    )
```

```python
import functools
import math

import jax
import jax.numpy as jnp
from jax import lax
from jax.experimental import pallas as pl
from jax.experimental.pallas import tpu as pltpu
from jax.sharding import Mesh, PartitionSpec as P

HEAD_DIM = 128
ROWS = 128
X = 4
Y = 8
HEADS = 5
DOCS = 32
SPAN = X * ROWS
SPAN_SHIFT = 9
GROUP = Y * SPAN
TILE = 2 * ROWS
TILES = Y // 2
STATS = 16
NEG = -1e30
LOG2E = math.log2(math.e)
C = LOG2E / math.sqrt(HEAD_DIM)
KEY_PAIRS = [(0, 1), (1, 0), (2, 3), (3, 2)]
QUERY_PAIRS = [(0, 3), (3, 0), (1, 2), (2, 1)]


def pack_kernel(q_ref, k_ref, v_ref, out_ref):
    for h in range(HEADS):
        cols = slice(h * HEAD_DIM, (h + 1) * HEAD_DIM)
        out_ref[h, :ROWS, :] = q_ref[:, cols]
        out_ref[h, ROWS : 2 * ROWS, :] = k_ref[:, cols]
        out_ref[h, 2 * ROWS :, :] = v_ref[:, cols].T


def pack(q, k, v):
    return pl.pallas_call(
        pack_kernel,
        out_shape=jax.ShapeDtypeStruct((Y, 2 * ROWS + HEAD_DIM, HEAD_DIM), jnp.bfloat16),
        name="pack",
    )(q, k, v)


def unpack_kernel(o_ref, out_ref):
    for h in range(HEADS):
        out_ref[:, h * HEAD_DIM : (h + 1) * HEAD_DIM] = o_ref[h]


def unpack(o):
    return pl.pallas_call(
        unpack_kernel,
        out_shape=jax.ShapeDtypeStruct((ROWS, HEADS * HEAD_DIM), jnp.bfloat16),
        name="unpack",
    )(o)


def merge_kernel(place_ref, a_ref, b_ref, out_ref):
    @pl.when(place_ref[2] < HEADS)
    def _():
        terms = [b_ref[y, ROWS:, :].astype(jnp.float32) for y in range(Y)]
        a = jnp.concatenate([a_ref[y, ROWS : ROWS + 1, :] for y in range(Y)], axis=0)
        b = jnp.concatenate([t[0:1] + t[1:2] + t[2:3] for t in terms], axis=0)
        top = jnp.maximum(a, b)
        a, b = jnp.exp2(a - top), jnp.exp2(b - top)
        shares = jnp.concatenate([a / (a + b), b / (a + b)], axis=0).T
        for y in range(Y):
            o = a_ref[y, :ROWS, :] * shares[:, y : y + 1] + b_ref[y, :ROWS, :].astype(
                jnp.float32
            ) * shares[:, Y + y : Y + y + 1]
            out_ref[y] = o.astype(jnp.bfloat16)


def merge(place, a, b):
    vmem = pl.BlockSpec(memory_space=pltpu.VMEM)
    return pl.pallas_call(
        merge_kernel,
        out_shape=jax.ShapeDtypeStruct((Y, ROWS, HEAD_DIM), jnp.bfloat16),
        in_specs=[pl.BlockSpec(memory_space=pltpu.SMEM), vmem, vmem],
        out_specs=vmem,
        name="merge",
    )(place, a, b)


def attend_kernel(
    partner,
    place_ref,
    len_ref,
    q_ref,
    own_ref,
    pair_ref,
    prev_own_ref,
    prev_pair_ref,
    o_ref,
    first_ref,
    lo_ref,
    k_ref,
    vt_ref,
    even_ref,
    odd_ref,
):
    blk, x, slot = place_ref[0], place_ref[1], place_ref[2]
    x_of_queries = (X - 1) - x if partner else x
    off = blk * GROUP + x_of_queries * ROWS

    def load(own, pair, j, group):
        k_ref[group, j, :ROWS, :] = own[j, :ROWS, :]
        k_ref[group, j, ROWS:, :] = pair[j, :ROWS, :]
        vt_ref[group, j, :, :ROWS] = own[j, ROWS:, :]
        vt_ref[group, j, :, ROWS:] = pair[j, ROWS:, :]

    @pl.when(slot < HEADS)
    def _():
        lane = lax.broadcasted_iota(jnp.int32, (Y, TILE), 1)
        pos = (
            off
            + lax.broadcasted_iota(jnp.int32, (Y, TILE), 0) * (2 * SPAN)
            + lax.shift_right_logical(lane, 7) * SPAN
            + (lane & (ROWS - 1))
        )
        first = jnp.zeros((Y, TILE), jnp.int32)
        los = [jnp.int32(0)] * TILES
        start = jnp.int32(0)
        for j in range(DOCS - 1):
            start = start + len_ref[j]
            first = jnp.where(pos >= start, start, first)
            los = [jnp.where(off + 2 * i * SPAN >= start, start, los[i]) for i in range(TILES)]
        first_ref[...] = first
        for i in range(TILES):
            lo_ref[i] = lax.shift_right_logical(los[i], SPAN_SHIFT)

        def load_own(j, _):
            load(own_ref, pair_ref, j, blk)
            return 0

        lax.fori_loop(0, Y, load_own, 0)

        @pl.when(blk > 0)
        def _():
            def load_prev(j, _):
                load(prev_own_ref, prev_pair_ref, j, 0)
                return 0

            lax.fori_loop(lo_ref[0], Y, load_prev, 0)

        row = lax.broadcasted_iota(jnp.int32, (TILE, TILE), 0)
        key_rows = jnp.where(row < ROWS, x * ROWS, (x ^ 1) * ROWS) + (row & (ROWS - 1))

        def queries(i):
            return jnp.concatenate([q_ref[2 * i], q_ref[2 * i + 1]], axis=0)

        def score(s_ref, i, q, g, m, diagonal):
            s = lax.dot_general(
                k_ref[lax.shift_right_logical(g, 3), g & (Y - 1)],
                q,
                (((1,), (1,)), ((), ())),
                preferred_element_type=jnp.float32,
            )
            kept = key_rows >= first_ref[pl.ds(i, 1), :] - g * SPAN
            if diagonal:
                n = lax.broadcasted_iota(jnp.int32, (1, TILE), 1)
                t = off + 2 * i * SPAN + lax.shift_right_logical(n, 7) * SPAN + (n & (ROWS - 1))
                kept &= key_rows <= t - g * SPAN
            s = jnp.where(kept, s, NEG)
            s_ref[g] = s
            return jnp.maximum(m, jnp.max(s.reshape(TILE // 8, 8, TILE), axis=0))

        def mix(s_ref, g, shift, l, acc):
            p = jnp.exp2(s_ref[g] * C - shift)
            l = l + jnp.sum(p.reshape(TILE // 8, 8, TILE), axis=0)
            acc = acc + jnp.dot(
                vt_ref[lax.shift_right_logical(g, 3), g & (Y - 1)],
                p.astype(jnp.bfloat16),
                preferred_element_type=jnp.float32,
            )
            return l, acc

        def pairs(begin, end, step, carry):
            count = end - begin
            carry = lax.fori_loop(
                0,
                lax.shift_right_logical(count, 1),
                lambda n, c: step(begin + 2 * n + 1, step(begin + 2 * n, c)),
                carry,
            )
            return lax.fori_loop(0, count & 1, lambda n, c: step(end - 1, c), carry)

        def score_diagonal(s_ref, i, q, m):
            g = blk * Y + 2 * i
            m = score(s_ref, i, q, g, m, True)
            return score(s_ref, i, q, g + 1, m, True)

        none = jnp.full((8, TILE), NEG, jnp.float32)
        q = queries(0)
        m = score_diagonal(even_ref, 0, q, none)
        m = pairs(
            lo_ref[0], blk * Y, lambda g, m: score(even_ref, 0, q, g, m, False), m
        )

        def tile(i, s_ref, later_ref, m):
            top = jnp.max(m, axis=0, keepdims=True)
            shift = jnp.where(top > 0.5 * NEG, top * C, 0.0)
            later = jnp.minimum(i + 1, TILES - 1)
            q = queries(later)
            zeros = jnp.zeros((8, TILE), jnp.float32)

            def step(g, carry):
                m, l, acc = carry
                l, acc = mix(s_ref, g, shift, l, acc)
                return score(later_ref, later, q, g, m, False), l, acc

            m, l, acc = pairs(
                lo_ref[i],
                blk * Y + 2 * i + 2,
                step,
                (none, zeros, jnp.zeros((HEAD_DIM, TILE), jnp.float32)),
            )
            m = score_diagonal(later_ref, later, q, m)
            l = jnp.sum(l, axis=0, keepdims=True)
            some = l > 0.0
            o = (acc / jnp.where(some, l, 1.0)).T.astype(o_ref.dtype)
            log = jnp.where(some, shift + jnp.log(jnp.where(some, l, 1.0)) * LOG2E, NEG)
            if partner:
                high = log.astype(jnp.bfloat16).astype(jnp.float32)
                middle = (log - high).astype(jnp.bfloat16).astype(jnp.float32)
                low = log - high - middle
                row = lax.broadcasted_iota(jnp.int32, (STATS, TILE), 0)
                stats = jnp.where(row == 0, high, jnp.where(row == 1, middle, low))
            else:
                stats = jnp.broadcast_to(log, (STATS, TILE))
            stats = stats.astype(o_ref.dtype)
            for n in range(2):
                part = slice(n * ROWS, (n + 1) * ROWS)
                o_ref[2 * i + n, :ROWS, :] = o[part]
                o_ref[2 * i + n, ROWS:, :] = stats[:, part]
            return m

        def two_tiles(i, m):
            m = tile(2 * i, even_ref, odd_ref, m)
            return tile(2 * i + 1, odd_ref, even_ref, m)

        lax.fori_loop(0, TILES // 2, two_tiles, m)


def attend(partner, place, lengths, q, own, pair, prev_own, prev_pair):
    smem = pl.BlockSpec(memory_space=pltpu.SMEM)
    vmem = pl.BlockSpec(memory_space=pltpu.VMEM)
    return pl.pallas_call(
        functools.partial(attend_kernel, partner),
        out_shape=jax.ShapeDtypeStruct(
            (Y, ROWS + STATS, HEAD_DIM), jnp.bfloat16 if partner else jnp.float32
        ),
        in_specs=[smem, smem] + [vmem] * 5,
        out_specs=vmem,
        scratch_shapes=[
            pltpu.VMEM((Y, TILE), jnp.int32),
            pltpu.SMEM((TILES,), jnp.int32),
            pltpu.VMEM((2, Y, TILE, HEAD_DIM), jnp.bfloat16),
            pltpu.VMEM((2, Y, HEAD_DIM, TILE), jnp.bfloat16),
            pltpu.VMEM((2 * Y, TILE, TILE), jnp.float32),
            pltpu.VMEM((2 * Y, TILE, TILE), jnp.float32),
        ],
        compiler_params=pltpu.CompilerParams(vmem_limit_bytes=24 << 20),
        cost_estimate=pl.CostEstimate(
            flops=1 << 30, bytes_accessed=4 << 20, transcendentals=2 << 20
        ),
        name="attend_partner" if partner else "attend_own",
    )(place, lengths, q, own, pair, prev_own, prev_pair)


def body(queries, keys, values, lengths):
    place = jnp.stack([lax.axis_index("blk"), lax.axis_index("x"), lax.axis_index("y")])
    place = place.astype(jnp.int32)
    got = lax.all_to_all(pack(queries, keys, values), "y", 0, 0, tiled=True)
    own_queries, own = got[:, :ROWS], got[:, ROWS:]
    pair = lax.ppermute(own, "x", KEY_PAIRS)
    partner_queries = lax.ppermute(own_queries, "x", QUERY_PAIRS)
    prev_own = lax.ppermute(own, "blk", [(0, 1)])
    pair, partner_queries = lax.optimization_barrier((pair, partner_queries))
    prev_pair = lax.ppermute(pair, "blk", [(0, 1)])
    keys_and_values = (own, pair, prev_own, prev_pair)
    partial = attend(True, place, lengths, partner_queries, *keys_and_values)
    partial = lax.ppermute(partial, "x", QUERY_PAIRS)
    mine = attend(False, place, lengths, own_queries, *keys_and_values)
    return unpack(lax.all_to_all(merge(place, mine, partial), "y", 0, 0, tiled=True))


def solution(mesh):
    devices = mesh.devices.reshape(2, Y, X, mesh.devices.shape[2])
    fine = Mesh(devices, ("blk", "y", "x", "tp"))
    rows = P(("blk", "y", "x"), "tp")
    return jax.shard_map(
        body, mesh=fine, in_specs=(rows, rows, rows, P()), out_specs=rows, check_vma=False
    )
```

```python
import math

import jax
import jax.numpy as jnp
from jax import lax
from jax.experimental import pallas as pl
from jax.experimental.pallas import tpu as pltpu
from jax.sharding import Mesh, PartitionSpec as P

HEAD_DIM = 128
ROWS = 128
X = 4
Y = 8
HEADS = 5
DOCS = 32
SPAN = X * ROWS
WIDE = 2 * SPAN
WIDE_SHIFT = 10
TILE = 4 * ROWS
TILES = Y // 2
GROUP = Y * SPAN
STATS = 16
NEG = -1e30
LOG2E = math.log2(math.e)
C = LOG2E / math.sqrt(HEAD_DIM)
KEY_PAIRS = [(x, X - 1 - x) for x in range(X)]
QUERY_PAIRS = [(0, 1), (1, 0)]


def pack_kernel(q_ref, k_ref, v_ref, out_ref):
    for h in range(HEADS):
        cols = slice(h * HEAD_DIM, (h + 1) * HEAD_DIM)
        out_ref[h, :ROWS, :] = q_ref[:, cols]
        out_ref[h, ROWS : 2 * ROWS, :] = k_ref[:, cols]
        out_ref[h, 2 * ROWS :, :] = v_ref[:, cols].T


def pack(q, k, v):
    return pl.pallas_call(
        pack_kernel,
        out_shape=jax.ShapeDtypeStruct((Y, 2 * ROWS + HEAD_DIM, HEAD_DIM), jnp.bfloat16),
        name="pack",
    )(q, k, v)


def combine_kernel(in_ref, out_ref):
    logs = []
    for h in range(HEADS):
        for n in range(2):
            terms = in_ref[h, n, ROWS:, :].astype(jnp.float32)
            logs.append(terms[0:1] + terms[1:2] + terms[2:3])
    a = jnp.concatenate(logs[::2] + logs[:1] * (8 - HEADS), axis=0)
    b = jnp.concatenate(logs[1::2] + logs[1:2] * (8 - HEADS), axis=0)
    top = jnp.maximum(a, b)
    a, b = jnp.exp2(a - top), jnp.exp2(b - top)
    total = a + b
    shares = jnp.concatenate([a / total, b / total], axis=0).T
    for h in range(HEADS):
        a = in_ref[h, 0, :ROWS, :].astype(jnp.float32) * shares[:, h : h + 1]
        b = in_ref[h, 1, :ROWS, :].astype(jnp.float32) * shares[:, 8 + h : 9 + h]
        out_ref[:, h * HEAD_DIM : (h + 1) * HEAD_DIM] = (a + b).astype(jnp.bfloat16)


def combine(parts):
    return pl.pallas_call(
        combine_kernel,
        out_shape=jax.ShapeDtypeStruct((ROWS, HEADS * HEAD_DIM), jnp.bfloat16),
        name="combine",
    )(parts)


def attend_kernel(
    place_ref,
    len_ref,
    q_own_ref,
    q_pair_ref,
    own_ref,
    pair_ref,
    prev_own_ref,
    prev_pair_ref,
    o_ref,
    first_ref,
    lo_ref,
    k_ref,
    vt_ref,
    even_ref,
    odd_ref,
):
    blk, x, slot = place_ref[0], place_ref[1], place_ref[2]
    base = blk * GROUP

    def load(own, pair, j, group):
        block = group * TILES + j
        for n, ref in enumerate((own, pair, own, pair)):
            y = 2 * j + n // 2
            part = slice(n * ROWS, (n + 1) * ROWS)
            k_ref[block, part, :] = ref[y, :ROWS, :]
            vt_ref[block, :, part] = ref[y, ROWS:, :]

    @pl.when(slot < HEADS)
    def _():
        def places(shape):
            n = lax.broadcasted_iota(jnp.int32, shape, 1)
            return (
                jnp.where(n < 2 * ROWS, x, x ^ 1) * ROWS
                + (lax.shift_right_logical(n, 7) & 1) * SPAN
                + (n & (ROWS - 1))
            )

        pos = base + places((8, TILE)) + lax.broadcasted_iota(jnp.int32, (8, TILE), 0) * WIDE
        lowest = base + jnp.minimum(x, x ^ 1) * ROWS
        first = jnp.zeros((8, TILE), jnp.int32)
        los = [jnp.int32(0)] * TILES
        start = jnp.int32(0)
        for j in range(DOCS - 1):
            start = start + len_ref[j]
            first = jnp.where(pos >= start, start, first)
            los = [jnp.where(lowest + i * WIDE >= start, start, los[i]) for i in range(TILES)]
        first_ref[...] = first
        for i in range(TILES):
            lo_ref[i] = lax.shift_right_logical(los[i], WIDE_SHIFT)

        def load_own(j, _):
            load(own_ref, pair_ref, j, blk)
            return 0

        lax.fori_loop(0, TILES, load_own, 0)

        @pl.when(blk > 0)
        def _():
            def load_prev(j, _):
                load(prev_own_ref, prev_pair_ref, j, 0)
                return 0

            lax.fori_loop(lo_ref[0], TILES, load_prev, 0)

        row = lax.broadcasted_iota(jnp.int32, (TILE, TILE), 0)
        key_rows = (
            jnp.where((row & ROWS) == 0, x, X - 1 - x) * ROWS
            + lax.shift_right_logical(row, 8) * SPAN
            + (row & (ROWS - 1))
        )

        def queries(i):
            return jnp.concatenate(
                [q_own_ref[2 * i], q_own_ref[2 * i + 1], q_pair_ref[2 * i], q_pair_ref[2 * i + 1]],
                axis=0,
            )

        def score(s_ref, i, q, g, m, diagonal):
            s = lax.dot_general(
                k_ref[g], q, (((1,), (1,)), ((), ())), preferred_element_type=jnp.float32
            )
            kept = key_rows >= first_ref[pl.ds(i, 1), :] - g * WIDE
            if diagonal:
                kept &= key_rows <= places((1, TILE))
            s = jnp.where(kept, s, NEG)
            s_ref[g] = s
            return jnp.maximum(m, jnp.max(s.reshape(TILE // 8, 8, TILE), axis=0))

        def mix(s_ref, g, shift, l, acc):
            p = jnp.exp2(s_ref[g] * C - shift)
            l = l + jnp.sum(p.reshape(TILE // 8, 8, TILE), axis=0)
            acc = acc + jnp.dot(
                vt_ref[g], p.astype(jnp.bfloat16), preferred_element_type=jnp.float32
            )
            return l, acc

        none = jnp.full((8, TILE), NEG, jnp.float32)
        q = queries(0)
        m = score(even_ref, 0, q, blk * TILES, none, True)
        m = lax.fori_loop(
            lo_ref[0], blk * TILES, lambda g, m: score(even_ref, 0, q, g, m, False), m
        )

        def tile(i, s_ref, later_ref, m):
            top = jnp.max(m, axis=0, keepdims=True)
            shift = jnp.where(top > 0.5 * NEG, top * C, 0.0)
            later = jnp.minimum(i + 1, TILES - 1)
            q = queries(later)
            zeros = jnp.zeros((8, TILE), jnp.float32)

            def step(g, carry):
                m, l, acc = carry
                l, acc = mix(s_ref, g, shift, l, acc)
                return score(later_ref, later, q, g, m, False), l, acc

            m, l, acc = lax.fori_loop(
                lo_ref[i],
                blk * TILES + i + 1,
                step,
                (none, zeros, jnp.zeros((HEAD_DIM, TILE), jnp.float32)),
            )
            m = score(later_ref, later, q, blk * TILES + later, m, True)
            l = jnp.sum(l, axis=0, keepdims=True)
            some = l > 0.0
            l = jnp.where(some, l, 1.0)
            o = acc / l
            log = jnp.where(some, shift + jnp.log(l) * LOG2E, NEG)
            high = log.astype(jnp.bfloat16).astype(jnp.float32)
            middle = (log - high).astype(jnp.bfloat16).astype(jnp.float32)
            low = log - high - middle
            row = lax.broadcasted_iota(jnp.int32, (STATS, TILE), 0)
            stats = jnp.where(row == 0, high, jnp.where(row == 1, middle, low))
            stats = stats.astype(jnp.bfloat16)
            for n in range(4):
                part = slice(n * ROWS, (n + 1) * ROWS)
                y, to = 2 * i + (n & 1), (x & 1) ^ (n >> 1)
                o_ref[y, to, :ROWS, :] = o[:, part].T.astype(jnp.bfloat16)
                o_ref[y, to, ROWS:, :] = stats[:, part]
            return m

        def two_tiles(i, m):
            m = tile(2 * i, even_ref, odd_ref, m)
            return tile(2 * i + 1, odd_ref, even_ref, m)

        lax.fori_loop(0, TILES // 2, two_tiles, m)


def attend(place, lengths, *operands):
    smem = pl.BlockSpec(memory_space=pltpu.SMEM)
    vmem = pl.BlockSpec(memory_space=pltpu.VMEM)
    return pl.pallas_call(
        attend_kernel,
        out_shape=jax.ShapeDtypeStruct((Y, 2, ROWS + STATS, HEAD_DIM), jnp.bfloat16),
        in_specs=[smem, smem] + [vmem] * 6,
        out_specs=vmem,
        scratch_shapes=[
            pltpu.VMEM((8, TILE), jnp.int32),
            pltpu.SMEM((TILES,), jnp.int32),
            pltpu.VMEM((2 * TILES, TILE, HEAD_DIM), jnp.bfloat16),
            pltpu.VMEM((2 * TILES, HEAD_DIM, TILE), jnp.bfloat16),
            pltpu.VMEM((2 * TILES, TILE, TILE), jnp.float32),
            pltpu.VMEM((2 * TILES, TILE, TILE), jnp.float32),
        ],
        compiler_params=pltpu.CompilerParams(vmem_limit_bytes=28 << 20),
        cost_estimate=pl.CostEstimate(
            flops=1 << 30, bytes_accessed=4 << 20, transcendentals=2 << 20
        ),
        name="attend",
    )(place, lengths, *operands)


def body(queries, keys, values, lengths):
    x = 2 * lax.axis_index("xh") + lax.axis_index("xl")
    place = jnp.stack([lax.axis_index("blk"), x, lax.axis_index("y")]).astype(jnp.int32)
    got = lax.all_to_all(pack(queries, keys, values), "y", 0, 0, tiled=True)
    own_queries, own = got[:, :ROWS], got[:, ROWS:]
    pair = lax.ppermute(own, ("xh", "xl"), KEY_PAIRS)
    pair_queries = lax.ppermute(own_queries, "xl", QUERY_PAIRS)
    prev_own = lax.ppermute(own, "blk", [(0, 1)])
    pair, pair_queries = lax.optimization_barrier((pair, pair_queries))
    prev_pair = lax.ppermute(pair, "blk", [(0, 1)])
    parts = attend(place, lengths, own_queries, pair_queries, own, pair, prev_own, prev_pair)
    parts = parts.reshape(2 * Y, ROWS + STATS, HEAD_DIM)
    parts = lax.all_to_all(parts, ("y", "xl"), 0, 0, tiled=True)
    return combine(parts.reshape(Y, 2, ROWS + STATS, HEAD_DIM))


def solution(mesh):
    devices = mesh.devices.reshape(2, Y, 2, 2, mesh.devices.shape[2])
    fine = Mesh(devices, ("blk", "y", "xh", "xl", "tp"))
    rows = P(("blk", "y", "xh", "xl"), "tp")
    return jax.shard_map(
        body, mesh=fine, in_specs=(rows, rows, rows, P()), out_specs=rows, check_vma=False
    )
```

```python
import functools
import math

import jax
import jax.numpy as jnp
from jax import lax
from jax.experimental import pallas as pl
from jax.experimental.pallas import tpu as pltpu
from jax.sharding import Mesh, PartitionSpec as P

HEAD_DIM = 128
ROWS = 128
X = 4
Y = 8
HEADS = 5
DOCS = 32
SPAN = X * ROWS
WIDE = 2 * SPAN
WIDE_SHIFT = 10
TILE = 4 * ROWS
TILES = Y // 2
GROUP = Y * SPAN
STATS = 16
NEG = -1e30
LOG2E = math.log2(math.e)
C = LOG2E / math.sqrt(HEAD_DIM)
KEY_PAIRS = [(x, X - 1 - x) for x in range(X)]
QUERY_PAIRS = [(0, 1), (1, 0)]


def pack_kernel(q_ref, k_ref, v_ref, out_ref):
    for h in range(HEADS):
        cols = slice(h * HEAD_DIM, (h + 1) * HEAD_DIM)
        out_ref[h, :ROWS, :] = q_ref[:, cols]
        out_ref[h, ROWS : 2 * ROWS, :] = k_ref[:, cols]
        out_ref[h, 2 * ROWS :, :] = v_ref[:, cols].T


def pack(q, k, v):
    return pl.pallas_call(
        pack_kernel,
        out_shape=jax.ShapeDtypeStruct((Y, 2 * ROWS + HEAD_DIM, HEAD_DIM), jnp.bfloat16),
        name="pack",
    )(q, k, v)


def combine_kernel(in_ref, out_ref):
    logs = []
    for h in range(HEADS):
        for n in range(2):
            terms = in_ref[h, n, ROWS:, :].astype(jnp.float32)
            logs.append(terms[0:1] + terms[1:2] + terms[2:3])
    a = jnp.concatenate(logs[::2] + logs[:1] * (8 - HEADS), axis=0)
    b = jnp.concatenate(logs[1::2] + logs[1:2] * (8 - HEADS), axis=0)
    top = jnp.maximum(a, b)
    a, b = jnp.exp2(a - top), jnp.exp2(b - top)
    total = a + b
    shares = jnp.concatenate([a / total, b / total], axis=0).T
    for h in range(HEADS):
        a = in_ref[h, 0, :ROWS, :].astype(jnp.float32) * shares[:, h : h + 1]
        b = in_ref[h, 1, :ROWS, :].astype(jnp.float32) * shares[:, 8 + h : 9 + h]
        out_ref[:, h * HEAD_DIM : (h + 1) * HEAD_DIM] = (a + b).astype(jnp.bfloat16)


def combine(parts):
    return pl.pallas_call(
        combine_kernel,
        out_shape=jax.ShapeDtypeStruct((ROWS, HEADS * HEAD_DIM), jnp.bfloat16),
        name="combine",
    )(parts)


def attend_kernel(
    place_ref,
    len_ref,
    q_own_ref,
    q_pair_ref,
    own_ref,
    pair_ref,
    prev_own_ref,
    prev_pair_ref,
    o_ref,
    first_ref,
    lo_ref,
    hi_ref,
    k_ref,
    vt_ref,
    even_ref,
    odd_ref,
):
    blk, x, slot = place_ref[0], place_ref[1], place_ref[2]
    base = blk * GROUP

    def load(own, pair, j, group):
        block = group * TILES + j
        for n, ref in enumerate((own, pair, own, pair)):
            y = 2 * j + n // 2
            part = slice(n * ROWS, (n + 1) * ROWS)
            k_ref[block, part, :] = ref[y, :ROWS, :]
            vt_ref[block, :, part] = ref[y, ROWS:, :]

    @pl.when(slot < HEADS)
    def _():
        def places(shape):
            n = lax.broadcasted_iota(jnp.int32, shape, 1)
            return (
                jnp.where(n < 2 * ROWS, x, x ^ 1) * ROWS
                + (lax.shift_right_logical(n, 7) & 1) * SPAN
                + (n & (ROWS - 1))
            )

        pos = base + places((8, TILE)) + lax.broadcasted_iota(jnp.int32, (8, TILE), 0) * WIDE
        lowest = base + jnp.minimum(x, x ^ 1) * ROWS
        first = jnp.zeros((8, TILE), jnp.int32)
        highest = base + SPAN + jnp.maximum(x, x ^ 1) * ROWS + ROWS - 1
        los = [jnp.int32(0)] * TILES
        his = [jnp.int32(0)] * TILES
        start = jnp.int32(0)
        for j in range(DOCS - 1):
            start = start + len_ref[j]
            first = jnp.where(pos >= start, start, first)
            los = [jnp.where(lowest + i * WIDE >= start, start, los[i]) for i in range(TILES)]
            his = [jnp.where(highest + i * WIDE >= start, start, his[i]) for i in range(TILES)]
        first_ref[...] = first
        for i in range(TILES):
            lo_ref[i] = lax.shift_right_logical(los[i], WIDE_SHIFT)
            hi_ref[i] = lax.shift_right_logical(his[i], WIDE_SHIFT)

        def load_own(j, _):
            load(own_ref, pair_ref, j, blk)
            return 0

        lax.fori_loop(0, TILES, load_own, 0)

        @pl.when(blk > 0)
        def _():
            def load_prev(j, _):
                load(prev_own_ref, prev_pair_ref, j, 0)
                return 0

            lax.fori_loop(lo_ref[0], TILES, load_prev, 0)

        row = lax.broadcasted_iota(jnp.int32, (TILE, TILE), 0)
        key_rows = (
            jnp.where((row & ROWS) == 0, x, X - 1 - x) * ROWS
            + lax.shift_right_logical(row, 8) * SPAN
            + (row & (ROWS - 1))
        )

        def queries(i):
            return jnp.concatenate(
                [q_own_ref[2 * i], q_own_ref[2 * i + 1], q_pair_ref[2 * i], q_pair_ref[2 * i + 1]],
                axis=0,
            )

        def score(s_ref, i, q, g, m, masked, diagonal):
            s = lax.dot_general(
                k_ref[g], q, (((1,), (1,)), ((), ())), preferred_element_type=jnp.float32
            )
            if masked:
                kept = key_rows >= first_ref[i : i + 1, :] - g * WIDE
                if diagonal:
                    kept &= key_rows <= places((1, TILE))
                s = jnp.where(kept, s, NEG)
            s_ref[g] = s
            return jnp.maximum(m, jnp.max(s.reshape(TILE // 8, 8, TILE), axis=0))

        def mix(s_ref, g, shift, l, acc):
            p = jnp.exp2(s_ref[g] * C - shift)
            l = l + jnp.sum(p.reshape(TILE // 8, 8, TILE), axis=0)
            acc = acc + jnp.dot(
                vt_ref[g], p.astype(jnp.bfloat16), preferred_element_type=jnp.float32
            )
            return l, acc

        def edge(i, begin, end):
            return jnp.clip(hi_ref[i] + 1, begin, end)

        none = jnp.full((8, TILE), NEG, jnp.float32)
        buffers = (even_ref, odd_ref)
        q = queries(0)
        m = score(even_ref, 0, q, blk * TILES, none, True, True)
        begin, end = lo_ref[0], blk * TILES
        middle = edge(0, begin, end)
        m = lax.fori_loop(begin, middle, lambda g, m: score(even_ref, 0, q, g, m, True, False), m)
        m = lax.fori_loop(middle, end, lambda g, m: score(even_ref, 0, q, g, m, False, False), m)

        for i in range(TILES):
            s_ref, later_ref = buffers[i % 2], buffers[(i + 1) % 2]
            top = jnp.max(m, axis=0, keepdims=True)
            shift = jnp.where(top > 0.5 * NEG, top * C, 0.0)
            begin, end = lo_ref[i], blk * TILES + i
            sums = (
                jnp.zeros((8, TILE), jnp.float32),
                jnp.zeros((HEAD_DIM, TILE), jnp.float32),
            )
            if i + 1 < TILES:
                q = queries(i + 1)

                def step(masked, g, carry, i=i, q=q, shift=shift, s_ref=s_ref, later_ref=later_ref):
                    m, l, acc = carry
                    l, acc = mix(s_ref, g, shift, l, acc)
                    return score(later_ref, i + 1, q, g, m, masked, False), l, acc

                middle = edge(i + 1, begin, end)
                carry = lax.fori_loop(begin, middle, functools.partial(step, True), (none,) + sums)
                carry = lax.fori_loop(middle, end, functools.partial(step, False), carry)
                m, l, acc = step(True, end, carry)
                m = score(later_ref, i + 1, q, end + 1, m, True, True)
            else:
                l, acc = lax.fori_loop(
                    begin,
                    end + 1,
                    lambda g, c, s_ref=s_ref, shift=shift: mix(s_ref, g, shift, *c),
                    sums,
                )
            l = jnp.sum(l, axis=0, keepdims=True)
            some = l > 0.0
            l = jnp.where(some, l, 1.0)
            o = acc / l
            log = jnp.where(some, shift + jnp.log(l) * LOG2E, NEG)
            high = log.astype(jnp.bfloat16).astype(jnp.float32)
            middle = (log - high).astype(jnp.bfloat16).astype(jnp.float32)
            low = log - high - middle
            row = lax.broadcasted_iota(jnp.int32, (STATS, TILE), 0)
            stats = jnp.where(row == 0, high, jnp.where(row == 1, middle, low))
            stats = stats.astype(jnp.bfloat16)
            for n in range(4):
                part = slice(n * ROWS, (n + 1) * ROWS)
                y, to = 2 * i + (n & 1), (x & 1) ^ (n >> 1)
                o_ref[y, to, :ROWS, :] = o[:, part].T.astype(jnp.bfloat16)
                o_ref[y, to, ROWS:, :] = stats[:, part]


def attend(place, lengths, *operands):
    smem = pl.BlockSpec(memory_space=pltpu.SMEM)
    vmem = pl.BlockSpec(memory_space=pltpu.VMEM)
    return pl.pallas_call(
        attend_kernel,
        out_shape=jax.ShapeDtypeStruct((Y, 2, ROWS + STATS, HEAD_DIM), jnp.bfloat16),
        in_specs=[smem, smem] + [vmem] * 6,
        out_specs=vmem,
        scratch_shapes=[
            pltpu.VMEM((8, TILE), jnp.int32),
            pltpu.SMEM((TILES,), jnp.int32),
            pltpu.SMEM((TILES,), jnp.int32),
            pltpu.VMEM((2 * TILES, TILE, HEAD_DIM), jnp.bfloat16),
            pltpu.VMEM((2 * TILES, HEAD_DIM, TILE), jnp.bfloat16),
            pltpu.VMEM((2 * TILES, TILE, TILE), jnp.float32),
            pltpu.VMEM((2 * TILES, TILE, TILE), jnp.float32),
        ],
        compiler_params=pltpu.CompilerParams(vmem_limit_bytes=28 << 20),
        cost_estimate=pl.CostEstimate(
            flops=1 << 30, bytes_accessed=4 << 20, transcendentals=2 << 20
        ),
        name="attend",
    )(place, lengths, *operands)


def body(queries, keys, values, lengths):
    x = 2 * lax.axis_index("xh") + lax.axis_index("xl")
    place = jnp.stack([lax.axis_index("blk"), x, lax.axis_index("y")]).astype(jnp.int32)
    got = lax.all_to_all(pack(queries, keys, values), "y", 0, 0, tiled=True)
    own_queries, own = got[:, :ROWS], got[:, ROWS:]
    pair = lax.ppermute(own, ("xh", "xl"), KEY_PAIRS)
    pair_queries = lax.ppermute(own_queries, "xl", QUERY_PAIRS)
    prev_own = lax.ppermute(own, "blk", [(0, 1)])
    pair, pair_queries = lax.optimization_barrier((pair, pair_queries))
    prev_pair = lax.ppermute(pair, "blk", [(0, 1)])
    parts = attend(place, lengths, own_queries, pair_queries, own, pair, prev_own, prev_pair)
    parts = parts.reshape(2 * Y, ROWS + STATS, HEAD_DIM)
    parts = lax.all_to_all(parts, ("y", "xl"), 0, 0, tiled=True)
    return combine(parts.reshape(Y, 2, ROWS + STATS, HEAD_DIM))


def solution(mesh):
    devices = mesh.devices.reshape(2, Y, 2, 2, mesh.devices.shape[2])
    fine = Mesh(devices, ("blk", "y", "xh", "xl", "tp"))
    rows = P(("blk", "y", "xh", "xl"), "tp")
    return jax.shard_map(
        body, mesh=fine, in_specs=(rows, rows, rows, P()), out_specs=rows, check_vma=False
    )
```

```python
import functools
import math

import jax
import jax.numpy as jnp
from jax import lax
from jax.experimental import pallas as pl
from jax.experimental.pallas import tpu as pltpu
from jax.sharding import Mesh, PartitionSpec as P

HEAD_DIM = 128
ROWS = 128
X = 4
Y = 8
HEADS = 5
DOCS = 32
SPAN = X * ROWS
WIDE = 2 * SPAN
WIDE_SHIFT = 10
TILE = 4 * ROWS
TILES = Y // 2
GROUP = Y * SPAN
STATS = 16
NEG = -1e30
LOG2E = math.log2(math.e)
C = LOG2E / math.sqrt(HEAD_DIM)
KEY_PAIRS = [(x, X - 1 - x) for x in range(X)]
QUERY_PAIRS = [(0, 1), (1, 0)]


def pack_kernel(q_ref, k_ref, v_ref, out_ref):
    for h in range(HEADS):
        cols = slice(h * HEAD_DIM, (h + 1) * HEAD_DIM)
        out_ref[h, :ROWS, :] = q_ref[:, cols]
        out_ref[h, ROWS : 2 * ROWS, :] = k_ref[:, cols]
        out_ref[h, 2 * ROWS :, :] = v_ref[:, cols].T


def pack(q, k, v):
    return pl.pallas_call(
        pack_kernel,
        out_shape=jax.ShapeDtypeStruct((Y, 2 * ROWS + HEAD_DIM, HEAD_DIM), jnp.bfloat16),
        name="pack",
    )(q, k, v)


def combine_kernel(in_ref, out_ref):
    logs = []
    for h in range(HEADS):
        for n in range(2):
            terms = in_ref[h, n, ROWS:, :].astype(jnp.float32)
            logs.append(terms[0:1] + terms[1:2] + terms[2:3])
    a = jnp.concatenate(logs[::2] + logs[:1] * (8 - HEADS), axis=0)
    b = jnp.concatenate(logs[1::2] + logs[1:2] * (8 - HEADS), axis=0)
    top = jnp.maximum(a, b)
    a, b = jnp.exp2(a - top), jnp.exp2(b - top)
    total = a + b
    shares = jnp.concatenate([a / total, b / total], axis=0).T
    for h in range(HEADS):
        a = in_ref[h, 0, :ROWS, :].astype(jnp.float32) * shares[:, h : h + 1]
        b = in_ref[h, 1, :ROWS, :].astype(jnp.float32) * shares[:, 8 + h : 9 + h]
        out_ref[:, h * HEAD_DIM : (h + 1) * HEAD_DIM] = (a + b).astype(jnp.bfloat16)


def combine(parts):
    return pl.pallas_call(
        combine_kernel,
        out_shape=jax.ShapeDtypeStruct((ROWS, HEADS * HEAD_DIM), jnp.bfloat16),
        name="combine",
    )(parts)


def places(x, shape):
    n = lax.broadcasted_iota(jnp.int32, shape, 1)
    return (
        jnp.where(n < 2 * ROWS, x, x ^ 1) * ROWS
        + (lax.shift_right_logical(n, 7) & 1) * SPAN
        + (n & (ROWS - 1))
    )


def find_documents(blk, x, len_ref, first_ref, lo_ref, hi_ref):
    base = blk * GROUP
    pos = places(x, (8, TILE)) + lax.broadcasted_iota(jnp.int32, (8, TILE), 0) * WIDE
    lowest = jnp.minimum(x, x ^ 1) * ROWS
    highest = SPAN + jnp.maximum(x, x ^ 1) * ROWS + ROWS - 1
    start = -base
    first = jnp.zeros((8, TILE), jnp.int32) - base
    los = [start] * TILES
    his = [start] * TILES
    for j in range(DOCS - 1):
        start = start + len_ref[j]
        first = jnp.where(pos >= start, start, first)
        los = [jnp.where(lowest + i * WIDE >= start, start, los[i]) for i in range(TILES)]
        his = [jnp.where(highest + i * WIDE >= start, start, his[i]) for i in range(TILES)]
    first_ref[...] = first
    for i in range(TILES):
        lo_ref[i] = lax.shift_right_arithmetic(los[i], WIDE_SHIFT)
        hi_ref[i] = lax.shift_right_arithmetic(his[i], WIDE_SHIFT)


def load_block(own_ref, pair_ref, k_ref, vt_ref, j):
    for n, ref in enumerate((own_ref, pair_ref, own_ref, pair_ref)):
        y = 2 * j + n // 2
        part = slice(n * ROWS, (n + 1) * ROWS)
        k_ref[j, part, :] = ref[y, :ROWS, :]
        vt_ref[j, :, part] = ref[y, ROWS:, :]


def key_places(x):
    row = lax.broadcasted_iota(jnp.int32, (TILE, TILE), 0)
    return (
        jnp.where((row & ROWS) == 0, x, X - 1 - x) * ROWS
        + lax.shift_right_logical(row, 8) * SPAN
        + (row & (ROWS - 1))
    )


def load_queries(q_own_ref, q_pair_ref, i):
    return jnp.concatenate(
        [q_own_ref[2 * i], q_own_ref[2 * i + 1], q_pair_ref[2 * i], q_pair_ref[2 * i + 1]],
        axis=0,
    )


def scores_of(k_ref, s_ref, q, g, m, kept):
    s = lax.dot_general(
        k_ref[g], q, (((1,), (1,)), ((), ())), preferred_element_type=jnp.float32
    )
    if kept is not None:
        s = jnp.where(kept, s, NEG)
    s_ref[g] = s
    return jnp.maximum(m, jnp.max(s.reshape(TILE // 8, 8, TILE), axis=0))


def mix(vt_ref, s_ref, g, shift, l, acc):
    p = jnp.exp2(s_ref[g] * C - shift)
    l = l + jnp.sum(p.reshape(TILE // 8, 8, TILE), axis=0)
    acc = acc + jnp.dot(vt_ref[g], p.astype(jnp.bfloat16), preferred_element_type=jnp.float32)
    return l, acc


def shift_of(top):
    return jnp.where(top > 0.5 * NEG, top * C, 0.0)


def own_kernel(
    place_ref,
    len_ref,
    q_own_ref,
    q_pair_ref,
    own_ref,
    pair_ref,
    acc_ref,
    state_ref,
    first_ref,
    lo_ref,
    hi_ref,
    k_ref,
    vt_ref,
    even_ref,
    odd_ref,
):
    blk, x, slot = place_ref[0], place_ref[1], place_ref[2]

    @pl.when(slot < HEADS)
    def _():
        find_documents(blk, x, len_ref, first_ref, lo_ref, hi_ref)

        def load(j, _):
            load_block(own_ref, pair_ref, k_ref, vt_ref, j)
            return 0

        lax.fori_loop(0, TILES, load, 0)
        key_rows = key_places(x)

        def score(s_ref, i, q, g, m, masked, diagonal):
            kept = None
            if masked:
                kept = key_rows >= first_ref[i : i + 1, :] - g * WIDE
                if diagonal:
                    kept &= key_rows <= places(x, (1, TILE))
            return scores_of(k_ref, s_ref, q, g, m, kept)

        none = jnp.full((8, TILE), NEG, jnp.float32)
        zeros = jnp.zeros((8, TILE), jnp.float32)
        buffers = (even_ref, odd_ref)
        q = load_queries(q_own_ref, q_pair_ref, 0)
        m = score(even_ref, 0, q, 0, none, True, True)
        for i in range(TILES):
            s_ref, later_ref = buffers[i % 2], buffers[(i + 1) % 2]
            top = jnp.max(m, axis=0, keepdims=True)
            shift = shift_of(top)
            begin = jnp.maximum(lo_ref[i], 0)
            sums = (zeros, jnp.zeros((HEAD_DIM, TILE), jnp.float32))
            if i + 1 < TILES:
                q = load_queries(q_own_ref, q_pair_ref, i + 1)

                def step(masked, g, carry, i=i, q=q, shift=shift, s_ref=s_ref, later_ref=later_ref):
                    m, l, acc = carry
                    l, acc = mix(vt_ref, s_ref, g, shift, l, acc)
                    return score(later_ref, i + 1, q, g, m, masked, False), l, acc

                carry = (none,) + sums
                if i > 0:
                    middle = jnp.clip(hi_ref[i + 1] + 1, begin, i)
                    carry = lax.fori_loop(begin, middle, functools.partial(step, True), carry)
                    carry = lax.fori_loop(middle, i, functools.partial(step, False), carry)
                m, l, acc = step(True, i, carry)
                m = score(later_ref, i + 1, q, i + 1, m, True, True)
            else:
                l, acc = lax.fori_loop(
                    begin,
                    i + 1,
                    lambda g, c, s_ref=s_ref, shift=shift: mix(vt_ref, s_ref, g, shift, *c),
                    sums,
                )
            l = jnp.sum(l, axis=0, keepdims=True)
            row = lax.broadcasted_iota(jnp.int32, (8, TILE), 0)
            acc_ref[i] = acc
            state_ref[i] = jnp.where(row == 0, l, top)


def prev_kernel(
    place_ref,
    len_ref,
    q_own_ref,
    q_pair_ref,
    prev_own_ref,
    prev_pair_ref,
    acc_ref,
    state_ref,
    o_ref,
    first_ref,
    lo_ref,
    hi_ref,
    k_ref,
    vt_ref,
    even_ref,
    odd_ref,
    held_ref,
    sem,
):
    blk, x, slot = place_ref[0], place_ref[1], place_ref[2]

    @pl.when(slot < HEADS)
    def _():
        fetch = pltpu.make_async_copy(acc_ref, held_ref, sem)
        fetch.start()
        find_documents(blk, x, len_ref, first_ref, lo_ref, hi_ref)

        def begin_of(i):
            return jnp.where(blk > 0, jnp.clip(lo_ref[i] + TILES, 0, TILES), TILES)

        def load(j, _):
            load_block(prev_own_ref, prev_pair_ref, k_ref, vt_ref, j)
            return 0

        lax.fori_loop(begin_of(0), TILES, load, 0)
        key_rows = key_places(x)

        def score(s_ref, i, q, g, m, masked):
            kept = key_rows >= first_ref[i : i + 1, :] - (g - TILES) * WIDE if masked else None
            return scores_of(k_ref, s_ref, q, g, m, kept)

        def middle_of(i, begin):
            return jnp.clip(hi_ref[i] + TILES + 1, begin, TILES)

        none = jnp.full((8, TILE), NEG, jnp.float32)
        zeros = jnp.zeros((8, TILE), jnp.float32)
        buffers = (even_ref, odd_ref)
        q = load_queries(q_own_ref, q_pair_ref, 0)
        begin = begin_of(0)
        middle = middle_of(0, begin)
        m = lax.fori_loop(begin, middle, lambda g, m: score(even_ref, 0, q, g, m, True), none)
        m = lax.fori_loop(middle, TILES, lambda g, m: score(even_ref, 0, q, g, m, False), m)
        fetch.wait()
        for i in range(TILES):
            s_ref, later_ref = buffers[i % 2], buffers[(i + 1) % 2]
            own_l, own_top = state_ref[i, 0:1, :], state_ref[i, 1:2, :]
            top = jnp.maximum(jnp.max(m, axis=0, keepdims=True), own_top)
            shift = shift_of(top)
            scale = jnp.where(own_top > 0.5 * NEG, jnp.exp2(own_top * C - shift), 0.0)
            begin = begin_of(i)
            sums = (zeros, held_ref[i] * scale)
            if i + 1 < TILES:
                q = load_queries(q_own_ref, q_pair_ref, i + 1)

                def step(masked, g, carry, i=i, q=q, shift=shift, s_ref=s_ref, later_ref=later_ref):
                    m, l, acc = carry
                    l, acc = mix(vt_ref, s_ref, g, shift, l, acc)
                    return score(later_ref, i + 1, q, g, m, masked), l, acc

                middle = middle_of(i + 1, begin)
                carry = (none,) + sums
                carry = lax.fori_loop(begin, middle, functools.partial(step, True), carry)
                m, l, acc = lax.fori_loop(middle, TILES, functools.partial(step, False), carry)
            else:
                l, acc = lax.fori_loop(
                    begin,
                    TILES,
                    lambda g, c, s_ref=s_ref, shift=shift: mix(vt_ref, s_ref, g, shift, *c),
                    sums,
                )
            l = jnp.sum(l, axis=0, keepdims=True) + own_l * scale
            some = l > 0.0
            l = jnp.where(some, l, 1.0)
            o = acc / l
            log = jnp.where(some, shift + jnp.log(l) * LOG2E, NEG)
            high = log.astype(jnp.bfloat16).astype(jnp.float32)
            middle = (log - high).astype(jnp.bfloat16).astype(jnp.float32)
            low = log - high - middle
            row = lax.broadcasted_iota(jnp.int32, (STATS, TILE), 0)
            stats = jnp.where(row == 0, high, jnp.where(row == 1, middle, low))
            stats = stats.astype(jnp.bfloat16)
            for n in range(4):
                part = slice(n * ROWS, (n + 1) * ROWS)
                y, to = 2 * i + (n & 1), (x & 1) ^ (n >> 1)
                o_ref[y, to, :ROWS, :] = o[:, part].T.astype(jnp.bfloat16)
                o_ref[y, to, ROWS:, :] = stats[:, part]


SCRATCH = [
    pltpu.VMEM((8, TILE), jnp.int32),
    pltpu.SMEM((TILES,), jnp.int32),
    pltpu.SMEM((TILES,), jnp.int32),
    pltpu.VMEM((TILES, TILE, HEAD_DIM), jnp.bfloat16),
    pltpu.VMEM((TILES, HEAD_DIM, TILE), jnp.bfloat16),
    pltpu.VMEM((TILES, TILE, TILE), jnp.float32),
    pltpu.VMEM((TILES, TILE, TILE), jnp.float32),
]
SMEM = pl.BlockSpec(memory_space=pltpu.SMEM)
VMEM = pl.BlockSpec(memory_space=pltpu.VMEM)
ACC = (TILES, HEAD_DIM, TILE)


def attend_own(place, lengths, q_own, q_pair, own, pair):
    return pl.pallas_call(
        own_kernel,
        out_shape=(
            jax.ShapeDtypeStruct(ACC, jnp.float32),
            jax.ShapeDtypeStruct((TILES, 8, TILE), jnp.float32),
        ),
        in_specs=[SMEM, SMEM] + [VMEM] * 4,
        out_specs=(VMEM, VMEM),
        scratch_shapes=SCRATCH,
        compiler_params=pltpu.CompilerParams(vmem_limit_bytes=20 << 20),
        cost_estimate=pl.CostEstimate(
            flops=1 << 30, bytes_accessed=4 << 20, transcendentals=2 << 20
        ),
        name="attend_own",
    )(place, lengths, q_own, q_pair, own, pair)


def attend_prev(place, lengths, q_own, q_pair, prev_own, prev_pair, acc, state):
    return pl.pallas_call(
        prev_kernel,
        out_shape=jax.ShapeDtypeStruct((Y, 2, ROWS + STATS, HEAD_DIM), jnp.bfloat16),
        in_specs=[SMEM, SMEM] + [VMEM] * 4 + [pl.BlockSpec(memory_space=pl.ANY), VMEM],
        out_specs=VMEM,
        scratch_shapes=SCRATCH + [pltpu.VMEM(ACC, jnp.float32), pltpu.SemaphoreType.DMA],
        compiler_params=pltpu.CompilerParams(vmem_limit_bytes=20 << 20),
        cost_estimate=pl.CostEstimate(
            flops=1 << 29, bytes_accessed=4 << 20, transcendentals=1 << 20
        ),
        name="attend_prev",
    )(place, lengths, q_own, q_pair, prev_own, prev_pair, acc, state)


def body(queries, keys, values, lengths):
    x = 2 * lax.axis_index("xh") + lax.axis_index("xl")
    place = jnp.stack([lax.axis_index("blk"), x, lax.axis_index("y")]).astype(jnp.int32)
    got = lax.all_to_all(pack(queries, keys, values), "y", 0, 0, tiled=True)
    own_queries, own = got[:, :ROWS], got[:, ROWS:]
    pair = lax.ppermute(own, ("xh", "xl"), KEY_PAIRS)
    pair_queries = lax.ppermute(own_queries, "xl", QUERY_PAIRS)
    prev_own = lax.ppermute(own, "blk", [(0, 1)])
    pair, pair_queries = lax.optimization_barrier((pair, pair_queries))
    prev_pair = lax.ppermute(pair, "blk", [(0, 1)])
    state = attend_own(place, lengths, own_queries, pair_queries, own, pair)
    parts = attend_prev(place, lengths, own_queries, pair_queries, prev_own, prev_pair, *state)
    parts = parts.reshape(2 * Y, ROWS + STATS, HEAD_DIM)
    parts = lax.all_to_all(parts, ("y", "xl"), 0, 0, tiled=True)
    return combine(parts.reshape(Y, 2, ROWS + STATS, HEAD_DIM))


def solution(mesh):
    devices = mesh.devices.reshape(2, Y, 2, 2, mesh.devices.shape[2])
    fine = Mesh(devices, ("blk", "y", "xh", "xl", "tp"))
    rows = P(("blk", "y", "xh", "xl"), "tp")
    return jax.shard_map(
        body, mesh=fine, in_specs=(rows, rows, rows, P()), out_specs=rows, check_vma=False
    )
```

```python
import functools
import math

import jax
import jax.numpy as jnp
from jax import lax
from jax.experimental import pallas as pl
from jax.experimental.pallas import tpu as pltpu
from jax.sharding import Mesh, PartitionSpec as P

HEAD_DIM = 128
ROWS = 128
X = 4
Y = 8
HEADS = 5
DOCS = 32
SPAN = X * ROWS
WIDE = 2 * SPAN
WIDE_SHIFT = 10
TILE = 4 * ROWS
HALF = TILE // 2
TILES = Y // 2
GROUP = Y * SPAN
STATS = 16
NEG = -1e30
LOG2E = math.log2(math.e)
C = LOG2E / math.sqrt(HEAD_DIM)
KEY_PAIRS = [(x, X - 1 - x) for x in range(X)]
QUERY_PAIRS = [(0, 1), (1, 0)]


def pack_kernel(q_ref, k_ref, v_ref, out_ref):
    for h in range(HEADS):
        cols = slice(h * HEAD_DIM, (h + 1) * HEAD_DIM)
        out_ref[h, :ROWS, :] = q_ref[:, cols].T
        out_ref[h, ROWS : 2 * ROWS, :] = k_ref[:, cols]
        out_ref[h, 2 * ROWS :, :] = v_ref[:, cols].T


def pack(q, k, v):
    return pl.pallas_call(
        pack_kernel,
        out_shape=jax.ShapeDtypeStruct((Y, 2 * ROWS + HEAD_DIM, HEAD_DIM), jnp.bfloat16),
        name="pack",
    )(q, k, v)


def combine_kernel(in_ref, out_ref):
    logs = []
    for h in range(HEADS):
        for n in range(2):
            terms = in_ref[h, n, ROWS:, :].astype(jnp.float32)
            logs.append(terms[0:1] + terms[1:2] + terms[2:3])
    a = jnp.concatenate(logs[::2] + logs[:1] * (8 - HEADS), axis=0)
    b = jnp.concatenate(logs[1::2] + logs[1:2] * (8 - HEADS), axis=0)
    top = jnp.maximum(a, b)
    a, b = jnp.exp2(a - top), jnp.exp2(b - top)
    total = a + b
    shares = jnp.concatenate([a / total, b / total], axis=0).T
    for h in range(HEADS):
        a = in_ref[h, 0, :ROWS, :].astype(jnp.float32) * shares[:, h : h + 1]
        b = in_ref[h, 1, :ROWS, :].astype(jnp.float32) * shares[:, 8 + h : 9 + h]
        out_ref[:, h * HEAD_DIM : (h + 1) * HEAD_DIM] = (a + b).astype(jnp.bfloat16)


def combine(parts):
    return pl.pallas_call(
        combine_kernel,
        out_shape=jax.ShapeDtypeStruct((ROWS, HEADS * HEAD_DIM), jnp.bfloat16),
        name="combine",
    )(parts)


def places(x, shape):
    n = lax.broadcasted_iota(jnp.int32, shape, 1)
    return (
        jnp.where(n < 2 * ROWS, x, x ^ 1) * ROWS
        + (lax.shift_right_logical(n, 7) & 1) * SPAN
        + (n & (ROWS - 1))
    )


def find_documents(blk, x, len_ref, first_ref, lo_ref, hi_ref):
    base = blk * GROUP
    pos = places(x, (8, TILE)) + lax.broadcasted_iota(jnp.int32, (8, TILE), 0) * WIDE
    lowest = jnp.minimum(x, x ^ 1) * ROWS
    highest = SPAN + jnp.maximum(x, x ^ 1) * ROWS + ROWS - 1
    start = -base
    first = jnp.zeros((8, TILE), jnp.int32) - base
    los = [start] * TILES
    his = [start] * TILES
    for j in range(DOCS - 1):
        start = start + len_ref[j]
        first = jnp.where(pos >= start, start, first)
        los = [jnp.where(lowest + i * WIDE >= start, start, los[i]) for i in range(TILES)]
        his = [jnp.where(highest + i * WIDE >= start, start, his[i]) for i in range(TILES)]
    first_ref[...] = first
    for i in range(TILES):
        lo_ref[i] = lax.shift_right_arithmetic(los[i], WIDE_SHIFT)
        hi_ref[i] = lax.shift_right_arithmetic(his[i], WIDE_SHIFT)


def load_block(own_ref, pair_ref, k_ref, vt_ref, j):
    for n, ref in enumerate((own_ref, pair_ref, own_ref, pair_ref)):
        y = 2 * j + n // 2
        part = slice(n * ROWS, (n + 1) * ROWS)
        k_ref[j, part, :] = ref[y, :ROWS, :]
        vt_ref[j, :, part] = ref[y, ROWS:, :]


def key_places(x):
    row = lax.broadcasted_iota(jnp.int32, (HALF, TILE), 0)
    return jnp.where(row < ROWS, x, X - 1 - x) * ROWS + (row & (ROWS - 1))


def load_queries(q_own_ref, q_pair_ref, i):
    return jnp.concatenate(
        [q_own_ref[2 * i], q_own_ref[2 * i + 1], q_pair_ref[2 * i], q_pair_ref[2 * i + 1]],
        axis=1,
    )


def scores_of(k_ref, s_ref, q, g, n, m, kept):
    part = slice(n * HALF, (n + 1) * HALF)
    s = jnp.dot(k_ref[g, part, :], q, preferred_element_type=jnp.float32)
    if kept is not None:
        s = jnp.where(kept, s, NEG)
    s_ref[g, part, :] = s
    return jnp.maximum(m, jnp.max(s.reshape(HALF // 8, 8, TILE), axis=0))


def mix(vt_ref, s_ref, g, n, shift, l, acc):
    part = slice(n * HALF, (n + 1) * HALF)
    p = jnp.exp2(s_ref[g, part, :] * C - shift)
    l = l + jnp.sum(p.reshape(HALF // 8, 8, TILE), axis=0)
    acc = acc + jnp.dot(
        vt_ref[g, :, part], p.astype(jnp.bfloat16), preferred_element_type=jnp.float32
    )
    return l, acc


def mix_block(vt_ref, s_ref, g, shift, l, acc):
    for n in range(2):
        l, acc = mix(vt_ref, s_ref, g, n, shift, l, acc)
    return l, acc


def shift_of(top):
    return jnp.where(top > 0.5 * NEG, top * C, 0.0)


def own_kernel(
    place_ref,
    len_ref,
    q_own_ref,
    q_pair_ref,
    own_ref,
    pair_ref,
    acc_ref,
    state_ref,
    first_ref,
    lo_ref,
    hi_ref,
    k_ref,
    vt_ref,
    even_ref,
    odd_ref,
):
    blk, x, slot = place_ref[0], place_ref[1], place_ref[2]

    @pl.when(slot < HEADS)
    def _():
        find_documents(blk, x, len_ref, first_ref, lo_ref, hi_ref)

        def load(j, _):
            load_block(own_ref, pair_ref, k_ref, vt_ref, j)
            return 0

        lax.fori_loop(0, TILES, load, 0)
        key_rows = key_places(x)

        def score(s_ref, i, q, g, n, m, masked, diagonal):
            kept = None
            if masked:
                kept = key_rows >= first_ref[i : i + 1, :] - (g * WIDE + n * SPAN)
                if diagonal:
                    kept &= key_rows <= places(x, (1, TILE)) - n * SPAN
            return scores_of(k_ref, s_ref, q, g, n, m, kept)

        def score_diagonal(s_ref, i, q, m):
            for n in range(2):
                m = score(s_ref, i, q, i, n, m, True, True)
            return m

        none = jnp.full((8, TILE), NEG, jnp.float32)
        zeros = jnp.zeros((8, TILE), jnp.float32)
        buffers = (even_ref, odd_ref)
        q = load_queries(q_own_ref, q_pair_ref, 0)
        m = score_diagonal(even_ref, 0, q, none)
        for i in range(TILES):
            s_ref, later_ref = buffers[i % 2], buffers[(i + 1) % 2]
            top = jnp.max(m, axis=0, keepdims=True)
            shift = shift_of(top)
            begin = jnp.maximum(lo_ref[i], 0)
            sums = (zeros, jnp.zeros((HEAD_DIM, TILE), jnp.float32))
            if i + 1 < TILES:
                q = load_queries(q_own_ref, q_pair_ref, i + 1)

                def step(masked, g, carry, i=i, q=q, shift=shift, s_ref=s_ref, later_ref=later_ref):
                    m, l, acc = carry
                    for n in range(2):
                        l, acc = mix(vt_ref, s_ref, g, n, shift, l, acc)
                        m = score(later_ref, i + 1, q, g, n, m, masked, False)
                    return m, l, acc

                carry = (none,) + sums
                if i > 0:
                    middle = jnp.clip(hi_ref[i + 1] + 1, begin, i)
                    carry = lax.fori_loop(begin, middle, functools.partial(step, True), carry)
                    carry = lax.fori_loop(middle, i, functools.partial(step, False), carry)
                m, l, acc = step(True, i, carry)
                m = score_diagonal(later_ref, i + 1, q, m)
            else:
                l, acc = lax.fori_loop(
                    begin,
                    i + 1,
                    lambda g, c, s_ref=s_ref, shift=shift: mix_block(vt_ref, s_ref, g, shift, *c),
                    sums,
                )
            l = jnp.sum(l, axis=0, keepdims=True)
            row = lax.broadcasted_iota(jnp.int32, (8, TILE), 0)
            acc_ref[i] = acc
            state_ref[i] = jnp.where(row == 0, l, top)


def prev_kernel(
    place_ref,
    len_ref,
    q_own_ref,
    q_pair_ref,
    prev_own_ref,
    prev_pair_ref,
    acc_ref,
    state_ref,
    o_ref,
    first_ref,
    lo_ref,
    hi_ref,
    k_ref,
    vt_ref,
    even_ref,
    odd_ref,
):
    blk, x, slot = place_ref[0], place_ref[1], place_ref[2]

    @pl.when(slot < HEADS)
    def _():
        find_documents(blk, x, len_ref, first_ref, lo_ref, hi_ref)

        def begin_of(i):
            return jnp.where(blk > 0, jnp.clip(lo_ref[i] + TILES, 0, TILES), TILES)

        def load(j, _):
            load_block(prev_own_ref, prev_pair_ref, k_ref, vt_ref, j)
            return 0

        lax.fori_loop(begin_of(0), TILES, load, 0)
        key_rows = key_places(x)

        def score(s_ref, i, q, g, n, m, masked):
            kept = None
            if masked:
                kept = key_rows >= first_ref[i : i + 1, :] - ((g - TILES) * WIDE + n * SPAN)
            return scores_of(k_ref, s_ref, q, g, n, m, kept)

        def score_first(masked, g, m):
            for n in range(2):
                m = score(even_ref, 0, q, g, n, m, masked)
            return m

        def middle_of(i, begin):
            return jnp.clip(hi_ref[i] + TILES + 1, begin, TILES)

        none = jnp.full((8, TILE), NEG, jnp.float32)
        zeros = jnp.zeros((8, TILE), jnp.float32)
        buffers = (even_ref, odd_ref)
        q = load_queries(q_own_ref, q_pair_ref, 0)
        begin = begin_of(0)
        middle = middle_of(0, begin)
        m = lax.fori_loop(begin, middle, functools.partial(score_first, True), none)
        m = lax.fori_loop(middle, TILES, functools.partial(score_first, False), m)
        for i in range(TILES):
            s_ref, later_ref = buffers[i % 2], buffers[(i + 1) % 2]
            own_l, own_top = state_ref[i, 0:1, :], state_ref[i, 1:2, :]
            top = jnp.maximum(jnp.max(m, axis=0, keepdims=True), own_top)
            shift = shift_of(top)
            scale = jnp.where(own_top > 0.5 * NEG, jnp.exp2(own_top * C - shift), 0.0)
            begin = begin_of(i)
            sums = (zeros, acc_ref[i] * scale)
            if i + 1 < TILES:
                q = load_queries(q_own_ref, q_pair_ref, i + 1)

                def step(masked, g, carry, i=i, q=q, shift=shift, s_ref=s_ref, later_ref=later_ref):
                    m, l, acc = carry
                    for n in range(2):
                        l, acc = mix(vt_ref, s_ref, g, n, shift, l, acc)
                        m = score(later_ref, i + 1, q, g, n, m, masked)
                    return m, l, acc

                middle = middle_of(i + 1, begin)
                carry = (none,) + sums
                carry = lax.fori_loop(begin, middle, functools.partial(step, True), carry)
                m, l, acc = lax.fori_loop(middle, TILES, functools.partial(step, False), carry)
            else:
                l, acc = lax.fori_loop(
                    begin,
                    TILES,
                    lambda g, c, s_ref=s_ref, shift=shift: mix_block(vt_ref, s_ref, g, shift, *c),
                    sums,
                )
            l = jnp.sum(l, axis=0, keepdims=True) + own_l * scale
            some = l > 0.0
            l = jnp.where(some, l, 1.0)
            o = acc / l
            log = jnp.where(some, shift + jnp.log(l) * LOG2E, NEG)
            high = log.astype(jnp.bfloat16).astype(jnp.float32)
            middle = (log - high).astype(jnp.bfloat16).astype(jnp.float32)
            low = log - high - middle
            row = lax.broadcasted_iota(jnp.int32, (STATS, TILE), 0)
            stats = jnp.where(row == 0, high, jnp.where(row == 1, middle, low))
            stats = stats.astype(jnp.bfloat16)
            for n in range(4):
                part = slice(n * ROWS, (n + 1) * ROWS)
                y, to = 2 * i + (n & 1), (x & 1) ^ (n >> 1)
                o_ref[y, to, :ROWS, :] = o[:, part].T.astype(jnp.bfloat16)
                o_ref[y, to, ROWS:, :] = stats[:, part]


SCRATCH = [
    pltpu.VMEM((8, TILE), jnp.int32),
    pltpu.SMEM((TILES,), jnp.int32),
    pltpu.SMEM((TILES,), jnp.int32),
    pltpu.VMEM((TILES, TILE, HEAD_DIM), jnp.bfloat16),
    pltpu.VMEM((TILES, HEAD_DIM, TILE), jnp.bfloat16),
    pltpu.VMEM((TILES, TILE, TILE), jnp.float32),
    pltpu.VMEM((TILES, TILE, TILE), jnp.float32),
]
SMEM = pl.BlockSpec(memory_space=pltpu.SMEM)
VMEM = pl.BlockSpec(memory_space=pltpu.VMEM)
ACC = (TILES, HEAD_DIM, TILE)


def attend_own(place, lengths, q_own, q_pair, own, pair):
    return pl.pallas_call(
        own_kernel,
        out_shape=(
            jax.ShapeDtypeStruct(ACC, jnp.float32),
            jax.ShapeDtypeStruct((TILES, 8, TILE), jnp.float32),
        ),
        in_specs=[SMEM, SMEM] + [VMEM] * 4,
        out_specs=(VMEM, VMEM),
        scratch_shapes=SCRATCH,
        compiler_params=pltpu.CompilerParams(vmem_limit_bytes=20 << 20),
        cost_estimate=pl.CostEstimate(
            flops=1 << 30, bytes_accessed=4 << 20, transcendentals=2 << 20
        ),
        name="attend_own",
    )(place, lengths, q_own, q_pair, own, pair)


def attend_prev(place, lengths, q_own, q_pair, prev_own, prev_pair, acc, state):
    return pl.pallas_call(
        prev_kernel,
        out_shape=jax.ShapeDtypeStruct((Y, 2, ROWS + STATS, HEAD_DIM), jnp.bfloat16),
        in_specs=[SMEM, SMEM] + [VMEM] * 6,
        out_specs=VMEM,
        scratch_shapes=SCRATCH,
        compiler_params=pltpu.CompilerParams(vmem_limit_bytes=20 << 20),
        cost_estimate=pl.CostEstimate(
            flops=1 << 29, bytes_accessed=4 << 20, transcendentals=1 << 20
        ),
        name="attend_prev",
    )(place, lengths, q_own, q_pair, prev_own, prev_pair, acc, state)


def body(queries, keys, values, lengths):
    x = 2 * lax.axis_index("xh") + lax.axis_index("xl")
    place = jnp.stack([lax.axis_index("blk"), x, lax.axis_index("y")]).astype(jnp.int32)
    got = lax.all_to_all(pack(queries, keys, values), "y", 0, 0, tiled=True)
    own_queries, own = got[:, :ROWS], got[:, ROWS:]
    pair = lax.ppermute(own, ("xh", "xl"), KEY_PAIRS)
    pair_queries = lax.ppermute(own_queries, "xl", QUERY_PAIRS)
    prev_own = lax.ppermute(own, "blk", [(0, 1)])
    pair, pair_queries = lax.optimization_barrier((pair, pair_queries))
    prev_pair = lax.ppermute(pair, "blk", [(0, 1)])
    state = attend_own(place, lengths, own_queries, pair_queries, own, pair)
    parts = attend_prev(place, lengths, own_queries, pair_queries, prev_own, prev_pair, *state)
    parts = parts.reshape(2 * Y, ROWS + STATS, HEAD_DIM)
    parts = lax.all_to_all(parts, ("y", "xl"), 0, 0, tiled=True)
    return combine(parts.reshape(Y, 2, ROWS + STATS, HEAD_DIM))


def solution(mesh):
    devices = mesh.devices.reshape(2, Y, 2, 2, mesh.devices.shape[2])
    fine = Mesh(devices, ("blk", "y", "xh", "xl", "tp"))
    rows = P(("blk", "y", "xh", "xl"), "tp")
    return jax.shard_map(
        body, mesh=fine, in_specs=(rows, rows, rows, P()), out_specs=rows, check_vma=False
    )
```

```python
import functools
import math

import jax
import jax.numpy as jnp
from jax import lax
from jax.experimental import pallas as pl
from jax.experimental.pallas import tpu as pltpu
from jax.sharding import Mesh, PartitionSpec as P

HEAD_DIM = 128
ROWS = 128
X = 4
Y = 8
HEADS = 5
DOCS = 32
SPAN = X * ROWS
WIDE = 2 * SPAN
WIDE_SHIFT = 10
TILE = 4 * ROWS
HALF = TILE // 2
TILES = Y // 2
GROUP = Y * SPAN
STATS = 16
PLACE = 3
NEG = -1e30
LOG2E = math.log2(math.e)
C = LOG2E / math.sqrt(HEAD_DIM)
KEY_PAIRS = [(x, X - 1 - x) for x in range(X)]
QUERY_PAIRS = [(0, 1), (1, 0)]


def pack_kernel(q_ref, k_ref, v_ref, out_ref):
    for h in range(HEADS):
        cols = slice(h * HEAD_DIM, (h + 1) * HEAD_DIM)
        out_ref[h, :ROWS, :] = q_ref[:, cols].T
        out_ref[h, ROWS : 2 * ROWS, :] = k_ref[:, cols]
        out_ref[h, 2 * ROWS :, :] = v_ref[:, cols].T


def pack(q, k, v):
    return pl.pallas_call(
        pack_kernel,
        out_shape=jax.ShapeDtypeStruct((Y, 2 * ROWS + HEAD_DIM, HEAD_DIM), jnp.bfloat16),
        name="pack",
    )(q, k, v)


def combine_kernel(in_ref, out_ref):
    for h in range(HEADS):
        logs = []
        for n in range(2):
            terms = in_ref[h, n, ROWS:, :].astype(jnp.float32)
            logs.append(terms[0:1] + terms[1:2] + terms[2:3])
        top = jnp.maximum(logs[0], logs[1])
        a, b = jnp.exp2(logs[0] - top), jnp.exp2(logs[1] - top)
        o = in_ref[h, 0, :ROWS, :].astype(jnp.float32) * (a / (a + b))
        o += in_ref[h, 1, :ROWS, :].astype(jnp.float32) * (b / (a + b))
        out_ref[:, h * HEAD_DIM : (h + 1) * HEAD_DIM] = o.T.astype(jnp.bfloat16)


def combine(parts):
    shape = (HEADS, 2, ROWS + STATS, HEAD_DIM)
    return pl.pallas_call(
        combine_kernel,
        grid=(1,),
        out_shape=jax.ShapeDtypeStruct((ROWS, HEADS * HEAD_DIM), jnp.bfloat16),
        in_specs=[pl.BlockSpec(shape, lambda i: (0, 0, 0, 0))],
        out_specs=pl.BlockSpec((ROWS, HEADS * HEAD_DIM), lambda i: (0, 0)),
        name="combine",
    )(parts)


def places(x, shape):
    n = lax.broadcasted_iota(jnp.int32, shape, 1)
    return (
        jnp.where(n < 2 * ROWS, x, x ^ 1) * ROWS
        + (lax.shift_right_logical(n, 7) & 1) * SPAN
        + (n & (ROWS - 1))
    )


def find_documents(blk, x, int_ref, first_ref, lo_ref, hi_ref):
    base = blk * GROUP
    pos = places(x, (8, TILE)) + lax.broadcasted_iota(jnp.int32, (8, TILE), 0) * WIDE
    lowest = jnp.minimum(x, x ^ 1) * ROWS
    highest = SPAN + jnp.maximum(x, x ^ 1) * ROWS + ROWS - 1
    start = -base
    first = jnp.zeros((8, TILE), jnp.int32) - base
    los = [start] * TILES
    his = [start] * TILES
    for j in range(DOCS - 1):
        start = start + int_ref[PLACE + j]
        first = jnp.where(pos >= start, start, first)
        los = [jnp.where(lowest + i * WIDE >= start, start, los[i]) for i in range(TILES)]
        his = [jnp.where(highest + i * WIDE >= start, start, his[i]) for i in range(TILES)]
    first_ref[...] = first
    for i in range(TILES):
        lo_ref[i] = lax.shift_right_arithmetic(los[i], WIDE_SHIFT)
        hi_ref[i] = lax.shift_right_arithmetic(his[i], WIDE_SHIFT)


def key_places(x):
    row = lax.broadcasted_iota(jnp.int32, (HALF, TILE), 0)
    return jnp.where(row < ROWS, x, X - 1 - x) * ROWS + (row & (ROWS - 1))


def load_queries(q_own_ref, q_pair_ref, i):
    return jnp.concatenate(
        [q_own_ref[2 * i], q_own_ref[2 * i + 1], q_pair_ref[2 * i], q_pair_ref[2 * i + 1]],
        axis=1,
    )


def scores_of(refs, s_ref, q, g, n, m, kept):
    part = slice(n * HALF, (n + 1) * HALF)
    k = jnp.concatenate([ref[2 * g + n, :ROWS, :] for ref in refs], axis=0)
    s = jnp.dot(k, q, preferred_element_type=jnp.float32)
    if kept is not None:
        s = jnp.where(kept, s, NEG)
    s_ref[g, part, :] = s
    return jnp.maximum(m, jnp.max(s.reshape(HALF // 8, 8, TILE), axis=0))


def mix(refs, s_ref, g, n, shift, l, acc):
    part = slice(n * HALF, (n + 1) * HALF)
    p = jnp.exp2(s_ref[g, part, :] * C - shift)
    l = l + jnp.sum(p.reshape(HALF // 8, 8, TILE), axis=0)
    vt = jnp.concatenate([ref[2 * g + n, ROWS:, :] for ref in refs], axis=1)
    acc = acc + jnp.dot(vt, p.astype(jnp.bfloat16), preferred_element_type=jnp.float32)
    return l, acc


def mix_block(refs, s_ref, g, shift, l, acc):
    for n in range(2):
        l, acc = mix(refs, s_ref, g, n, shift, l, acc)
    return l, acc


def shift_of(top):
    return jnp.where(top > 0.5 * NEG, top * C, 0.0)


def own_kernel(
    int_ref,
    q_own_ref,
    q_pair_ref,
    own_ref,
    pair_ref,
    acc_ref,
    state_ref,
    first_ref,
    lo_ref,
    hi_ref,
    even_ref,
    odd_ref,
):
    blk, x, slot = int_ref[0], int_ref[1], int_ref[2]

    @pl.when(slot < HEADS)
    def _():
        find_documents(blk, x, int_ref, first_ref, lo_ref, hi_ref)

        refs = (own_ref, pair_ref)
        key_rows = key_places(x)

        def score(s_ref, i, q, g, n, m, masked, diagonal):
            kept = None
            if masked:
                kept = key_rows >= first_ref[i : i + 1, :] - (g * WIDE + n * SPAN)
                if diagonal:
                    kept &= key_rows <= places(x, (1, TILE)) - n * SPAN
            return scores_of(refs, s_ref, q, g, n, m, kept)

        def score_diagonal(s_ref, i, q, m):
            for n in range(2):
                m = score(s_ref, i, q, i, n, m, True, True)
            return m

        none = jnp.full((8, TILE), NEG, jnp.float32)
        zeros = jnp.zeros((8, TILE), jnp.float32)
        buffers = (even_ref, odd_ref)
        q = load_queries(q_own_ref, q_pair_ref, 0)
        m = score_diagonal(even_ref, 0, q, none)
        for i in range(TILES):
            s_ref, later_ref = buffers[i % 2], buffers[(i + 1) % 2]
            top = jnp.max(m, axis=0, keepdims=True)
            shift = shift_of(top)
            begin = jnp.maximum(lo_ref[i], 0)
            sums = (zeros, jnp.zeros((HEAD_DIM, TILE), jnp.float32))
            if i + 1 < TILES:
                q = load_queries(q_own_ref, q_pair_ref, i + 1)

                def step(masked, g, carry, i=i, q=q, shift=shift, s_ref=s_ref, later_ref=later_ref):
                    m, l, acc = carry
                    for n in range(2):
                        l, acc = mix(refs, s_ref, g, n, shift, l, acc)
                        m = score(later_ref, i + 1, q, g, n, m, masked, False)
                    return m, l, acc

                carry = (none,) + sums
                if i > 0:
                    middle = jnp.clip(hi_ref[i + 1] + 1, begin, i)
                    carry = lax.fori_loop(begin, middle, functools.partial(step, True), carry)
                    carry = lax.fori_loop(middle, i, functools.partial(step, False), carry)
                m, l, acc = step(True, i, carry)
                m = score_diagonal(later_ref, i + 1, q, m)
            else:
                l, acc = lax.fori_loop(
                    begin,
                    i + 1,
                    lambda g, c, s_ref=s_ref, shift=shift: mix_block(refs, s_ref, g, shift, *c),
                    sums,
                )
            l = jnp.sum(l, axis=0, keepdims=True)
            row = lax.broadcasted_iota(jnp.int32, (8, TILE), 0)
            acc_ref[i] = acc
            state_ref[i] = jnp.where(row == 0, l, top)


def prev_kernel(
    int_ref,
    q_own_ref,
    q_pair_ref,
    prev_own_ref,
    prev_pair_ref,
    acc_ref,
    state_ref,
    o_ref,
    first_ref,
    lo_ref,
    hi_ref,
    even_ref,
    odd_ref,
):
    blk, x, slot = int_ref[0], int_ref[1], int_ref[2]

    @pl.when(slot < HEADS)
    def _():
        find_documents(blk, x, int_ref, first_ref, lo_ref, hi_ref)

        def begin_of(i):
            return jnp.where(blk > 0, jnp.clip(lo_ref[i] + TILES, 0, TILES), TILES)

        refs = (prev_own_ref, prev_pair_ref)
        key_rows = key_places(x)

        def score(s_ref, i, q, g, n, m, masked):
            kept = None
            if masked:
                kept = key_rows >= first_ref[i : i + 1, :] - ((g - TILES) * WIDE + n * SPAN)
            return scores_of(refs, s_ref, q, g, n, m, kept)

        def score_first(masked, g, m):
            for n in range(2):
                m = score(even_ref, 0, q, g, n, m, masked)
            return m

        def middle_of(i, begin):
            return jnp.clip(hi_ref[i] + TILES + 1, begin, TILES)

        none = jnp.full((8, TILE), NEG, jnp.float32)
        zeros = jnp.zeros((8, TILE), jnp.float32)
        buffers = (even_ref, odd_ref)
        q = load_queries(q_own_ref, q_pair_ref, 0)
        begin = begin_of(0)
        middle = middle_of(0, begin)
        m = lax.fori_loop(begin, middle, functools.partial(score_first, True), none)
        m = lax.fori_loop(middle, TILES, functools.partial(score_first, False), m)
        for i in range(TILES):
            s_ref, later_ref = buffers[i % 2], buffers[(i + 1) % 2]
            own_l, own_top = state_ref[i, 0:1, :], state_ref[i, 1:2, :]
            top = jnp.maximum(jnp.max(m, axis=0, keepdims=True), own_top)
            shift = shift_of(top)
            scale = jnp.where(own_top > 0.5 * NEG, jnp.exp2(own_top * C - shift), 0.0)
            begin = begin_of(i)
            sums = (zeros, acc_ref[i] * scale)
            if i + 1 < TILES:
                q = load_queries(q_own_ref, q_pair_ref, i + 1)

                def step(masked, g, carry, i=i, q=q, shift=shift, s_ref=s_ref, later_ref=later_ref):
                    m, l, acc = carry
                    for n in range(2):
                        l, acc = mix(refs, s_ref, g, n, shift, l, acc)
                        m = score(later_ref, i + 1, q, g, n, m, masked)
                    return m, l, acc

                middle = middle_of(i + 1, begin)
                carry = (none,) + sums
                carry = lax.fori_loop(begin, middle, functools.partial(step, True), carry)
                m, l, acc = lax.fori_loop(middle, TILES, functools.partial(step, False), carry)
            else:
                l, acc = lax.fori_loop(
                    begin,
                    TILES,
                    lambda g, c, s_ref=s_ref, shift=shift: mix_block(refs, s_ref, g, shift, *c),
                    sums,
                )
            l = jnp.sum(l, axis=0, keepdims=True) + own_l * scale
            some = l > 0.0
            l = jnp.where(some, l, 1.0)
            o = (acc * (1.0 / l)).astype(jnp.bfloat16)
            log = jnp.where(some, shift + jnp.log(l) * LOG2E, NEG)
            high = log.astype(jnp.bfloat16).astype(jnp.float32)
            middle = (log - high).astype(jnp.bfloat16).astype(jnp.float32)
            low = log - high - middle
            row = lax.broadcasted_iota(jnp.int32, (STATS, TILE), 0)
            stats = jnp.where(row == 0, high, jnp.where(row == 1, middle, low))
            stats = stats.astype(jnp.bfloat16)
            for n in range(4):
                part = slice(n * ROWS, (n + 1) * ROWS)
                y, to = 2 * i + (n & 1), (x & 1) ^ (n >> 1)
                o_ref[y, to, :ROWS, :] = o[:, part]
                o_ref[y, to, ROWS:, :] = stats[:, part]


SCRATCH = [
    pltpu.VMEM((8, TILE), jnp.int32),
    pltpu.SMEM((TILES,), jnp.int32),
    pltpu.SMEM((TILES,), jnp.int32),
    pltpu.VMEM((TILES, TILE, TILE), jnp.float32),
    pltpu.VMEM((TILES, TILE, TILE), jnp.float32),
]
SMEM = pl.BlockSpec(memory_space=pltpu.SMEM)
VMEM = pl.BlockSpec(memory_space=pltpu.VMEM)
ACC = (TILES, HEAD_DIM, TILE)


def attend_own(ints, q_own, q_pair, own, pair):
    return pl.pallas_call(
        own_kernel,
        out_shape=(
            jax.ShapeDtypeStruct(ACC, jnp.float32),
            jax.ShapeDtypeStruct((TILES, 8, TILE), jnp.float32),
        ),
        in_specs=[SMEM] + [VMEM] * 4,
        out_specs=(VMEM, VMEM),
        scratch_shapes=SCRATCH,
        compiler_params=pltpu.CompilerParams(vmem_limit_bytes=16 << 20),
        cost_estimate=pl.CostEstimate(
            flops=1 << 30, bytes_accessed=4 << 20, transcendentals=2 << 20
        ),
        name="attend_own",
    )(ints, q_own, q_pair, own, pair)


def attend_prev(ints, q_own, q_pair, prev_own, prev_pair, acc, state):
    return pl.pallas_call(
        prev_kernel,
        out_shape=jax.ShapeDtypeStruct((Y, 2, ROWS + STATS, HEAD_DIM), jnp.bfloat16),
        in_specs=[SMEM] + [VMEM] * 6,
        out_specs=VMEM,
        scratch_shapes=SCRATCH,
        compiler_params=pltpu.CompilerParams(vmem_limit_bytes=16 << 20),
        cost_estimate=pl.CostEstimate(
            flops=1 << 29, bytes_accessed=4 << 20, transcendentals=1 << 20
        ),
        name="attend_prev",
    )(ints, q_own, q_pair, prev_own, prev_pair, acc, state)


def body(queries, keys, values, lengths):
    x = 2 * lax.axis_index("xh") + lax.axis_index("xl")
    place = jnp.stack([lax.axis_index("blk"), x, lax.axis_index("y")]).astype(jnp.int32)
    ints = jnp.concatenate([place, lengths])
    got = lax.all_to_all(pack(queries, keys, values), "y", 0, 0, tiled=True)
    own_queries, own = got[:, :ROWS], got[:, ROWS:]
    pair = lax.ppermute(own, ("xh", "xl"), KEY_PAIRS)
    pair_queries = lax.ppermute(own_queries, "xl", QUERY_PAIRS)
    prev_own = lax.ppermute(own, "blk", [(0, 1)])
    pair, pair_queries, ints = lax.optimization_barrier((pair, pair_queries, ints))
    prev_pair = lax.ppermute(pair, "blk", [(0, 1)])
    state = attend_own(ints, own_queries, pair_queries, own, pair)
    parts = attend_prev(ints, own_queries, pair_queries, prev_own, prev_pair, *state)
    parts = parts.reshape(2 * Y, ROWS + STATS, HEAD_DIM)
    parts = lax.all_to_all(parts, ("y", "xl"), 0, 0, tiled=True)
    return combine(parts.reshape(Y, 2, ROWS + STATS, HEAD_DIM))


def solution(mesh):
    devices = mesh.devices.reshape(2, Y, 2, 2, mesh.devices.shape[2])
    fine = Mesh(devices, ("blk", "y", "xh", "xl", "tp"))
    rows = P(("blk", "y", "xh", "xl"), "tp")
    return jax.shard_map(
        body, mesh=fine, in_specs=(rows, rows, rows, P()), out_specs=rows, check_vma=False
    )
```

```python
import functools
import math

import jax
import jax.numpy as jnp
from jax import lax
from jax.experimental import pallas as pl
from jax.experimental.pallas import tpu as pltpu
from jax.sharding import Mesh, PartitionSpec as P

HEAD_DIM = 128
ROWS = 128
X = 4
Y = 8
HEADS = 5
DOCS = 32
SPAN = X * ROWS
WIDE = 2 * SPAN
WIDE_SHIFT = 10
TILE = 4 * ROWS
HALF = TILE // 2
TILES = Y // 2
GROUP = Y * SPAN
PLACE = 3
NEG = -1e30
C = math.log2(math.e) / math.sqrt(HEAD_DIM)
KEY_PAIRS = [(x, X - 1 - x) for x in range(X)]
QUERY_PAIRS = [(0, 1), (1, 0)]


def pack_kernel(q_ref, k_ref, v_ref, out_ref):
    for h in range(HEADS):
        cols = slice(h * HEAD_DIM, (h + 1) * HEAD_DIM)
        out_ref[h, :ROWS, :] = q_ref[:, cols].T
        out_ref[h, ROWS : 2 * ROWS, :] = k_ref[:, cols]
        out_ref[h, 2 * ROWS :, :] = v_ref[:, cols].T


def pack(q, k, v):
    return pl.pallas_call(
        pack_kernel,
        out_shape=jax.ShapeDtypeStruct((Y, 2 * ROWS + HEAD_DIM, HEAD_DIM), jnp.bfloat16),
        name="pack",
    )(q, k, v)


def combine_kernel(in_ref, out_ref):
    for h in range(HEADS):
        o = in_ref[h, 0].astype(jnp.float32) + in_ref[h, 1].astype(jnp.float32)
        out_ref[:, h * HEAD_DIM : (h + 1) * HEAD_DIM] = o.T.astype(jnp.bfloat16)


def combine(parts):
    shape = (HEADS, 2, HEAD_DIM, ROWS)
    return pl.pallas_call(
        combine_kernel,
        grid=(1,),
        out_shape=jax.ShapeDtypeStruct((ROWS, HEADS * HEAD_DIM), jnp.bfloat16),
        in_specs=[pl.BlockSpec(shape, lambda i: (0, 0, 0, 0))],
        out_specs=pl.BlockSpec((ROWS, HEADS * HEAD_DIM), lambda i: (0, 0)),
        name="combine",
    )(parts)


def weigh_kernel(int_ref, acc_ref, state_ref, other_ref, o_ref):
    x, slot = int_ref[1], int_ref[2]

    @pl.when(slot < HEADS)
    def _():
        other = pltpu.roll(other_ref[...], TILE // 2, 1)
        for i in range(TILES):
            l, top = state_ref[2 * i : 2 * i + 1, :], state_ref[2 * i + 1 : 2 * i + 2, :]
            other_l, other_top = other[2 * i : 2 * i + 1], other[2 * i + 1 : 2 * i + 2]
            most = jnp.maximum(top, other_top)
            share = jnp.exp2((top - most) * C)
            total = l * share + other_l * jnp.exp2((other_top - most) * C)
            o = (acc_ref[i] * (share / total)).astype(jnp.bfloat16)
            for n in range(4):
                y, to = 2 * i + (n & 1), (x & 1) ^ (n >> 1)
                o_ref[y, to] = o[:, n * ROWS : (n + 1) * ROWS]


def places(x, shape):
    n = lax.broadcasted_iota(jnp.int32, shape, 1)
    return (
        jnp.where(n < 2 * ROWS, x, x ^ 1) * ROWS
        + (lax.shift_right_logical(n, 7) & 1) * SPAN
        + (n & (ROWS - 1))
    )


def find_documents(blk, x, int_ref, first_ref, lo_ref, hi_ref):
    base = blk * GROUP
    pos = places(x, (8, TILE)) + lax.broadcasted_iota(jnp.int32, (8, TILE), 0) * WIDE
    lowest = jnp.minimum(x, x ^ 1) * ROWS
    highest = SPAN + jnp.maximum(x, x ^ 1) * ROWS + ROWS - 1
    start = -base
    first = jnp.zeros((8, TILE), jnp.int32) - base
    los = [start] * TILES
    his = [start] * TILES
    for j in range(DOCS - 1):
        start = start + int_ref[PLACE + j]
        first = jnp.where(pos >= start, start, first)
        los = [jnp.where(lowest + i * WIDE >= start, start, los[i]) for i in range(TILES)]
        his = [jnp.where(highest + i * WIDE >= start, start, his[i]) for i in range(TILES)]
    first_ref[...] = first
    for i in range(TILES):
        lo_ref[i] = lax.shift_right_arithmetic(los[i], WIDE_SHIFT)
        hi_ref[i] = lax.shift_right_arithmetic(his[i], WIDE_SHIFT)


def key_places(x):
    row = lax.broadcasted_iota(jnp.int32, (HALF, TILE), 0)
    return jnp.where(row < ROWS, x, X - 1 - x) * ROWS + (row & (ROWS - 1))


def load_queries(q_own_ref, q_pair_ref, i):
    return jnp.concatenate(
        [q_own_ref[2 * i], q_own_ref[2 * i + 1], q_pair_ref[2 * i], q_pair_ref[2 * i + 1]],
        axis=1,
    )


def scores_of(refs, s_ref, q, g, n, m, kept):
    part = slice(n * HALF, (n + 1) * HALF)
    k = jnp.concatenate([ref[2 * g + n, :ROWS, :] for ref in refs], axis=0)
    s = jnp.dot(k, q, preferred_element_type=jnp.float32)
    if kept is not None:
        s = jnp.where(kept, s, NEG)
    s_ref[g, part, :] = s
    return jnp.maximum(m, jnp.max(s.reshape(HALF // 8, 8, TILE), axis=0))


def mix(refs, s_ref, g, n, shift, l, acc):
    part = slice(n * HALF, (n + 1) * HALF)
    p = jnp.exp2(s_ref[g, part, :] * C - shift)
    l = l + jnp.sum(p.reshape(HALF // 8, 8, TILE), axis=0)
    vt = jnp.concatenate([ref[2 * g + n, ROWS:, :] for ref in refs], axis=1)
    acc = acc + jnp.dot(vt, p.astype(jnp.bfloat16), preferred_element_type=jnp.float32)
    return l, acc


def mix_block(refs, s_ref, g, shift, l, acc):
    for n in range(2):
        l, acc = mix(refs, s_ref, g, n, shift, l, acc)
    return l, acc


def shift_of(top):
    return jnp.where(top > 0.5 * NEG, top * C, 0.0)


def own_kernel(
    int_ref,
    q_own_ref,
    q_pair_ref,
    own_ref,
    pair_ref,
    acc_ref,
    state_ref,
    first_ref,
    lo_ref,
    hi_ref,
    even_ref,
    odd_ref,
):
    blk, x, slot = int_ref[0], int_ref[1], int_ref[2]

    @pl.when(slot < HEADS)
    def _():
        find_documents(blk, x, int_ref, first_ref, lo_ref, hi_ref)

        refs = (own_ref, pair_ref)
        key_rows = key_places(x)

        def score(s_ref, i, q, g, n, m, masked, diagonal):
            kept = None
            if masked:
                kept = key_rows >= first_ref[i : i + 1, :] - (g * WIDE + n * SPAN)
                if diagonal:
                    kept &= key_rows <= places(x, (1, TILE)) - n * SPAN
            return scores_of(refs, s_ref, q, g, n, m, kept)

        def score_diagonal(s_ref, i, q, m):
            for n in range(2):
                m = score(s_ref, i, q, i, n, m, True, True)
            return m

        none = jnp.full((8, TILE), NEG, jnp.float32)
        zeros = jnp.zeros((8, TILE), jnp.float32)
        buffers = (even_ref, odd_ref)
        q = load_queries(q_own_ref, q_pair_ref, 0)
        m = score_diagonal(even_ref, 0, q, none)
        for i in range(TILES):
            s_ref, later_ref = buffers[i % 2], buffers[(i + 1) % 2]
            top = jnp.max(m, axis=0, keepdims=True)
            shift = shift_of(top)
            begin = jnp.maximum(lo_ref[i], 0)
            sums = (zeros, jnp.zeros((HEAD_DIM, TILE), jnp.float32))
            if i + 1 < TILES:
                q = load_queries(q_own_ref, q_pair_ref, i + 1)

                def step(masked, g, carry, i=i, q=q, shift=shift, s_ref=s_ref, later_ref=later_ref):
                    m, l, acc = carry
                    for n in range(2):
                        l, acc = mix(refs, s_ref, g, n, shift, l, acc)
                        m = score(later_ref, i + 1, q, g, n, m, masked, False)
                    return m, l, acc

                carry = (none,) + sums
                if i > 0:
                    middle = jnp.clip(hi_ref[i + 1] + 1, begin, i)
                    carry = lax.fori_loop(begin, middle, functools.partial(step, True), carry)
                    carry = lax.fori_loop(middle, i, functools.partial(step, False), carry)
                m, l, acc = step(True, i, carry)
                m = score_diagonal(later_ref, i + 1, q, m)
            else:
                l, acc = lax.fori_loop(
                    begin,
                    i + 1,
                    lambda g, c, s_ref=s_ref, shift=shift: mix_block(refs, s_ref, g, shift, *c),
                    sums,
                )
            l = jnp.sum(l, axis=0, keepdims=True)
            acc_ref[i] = acc
            state_ref[2 * i : 2 * i + 1, :] = l
            state_ref[2 * i + 1 : 2 * i + 2, :] = top


def prev_kernel(
    int_ref,
    q_own_ref,
    q_pair_ref,
    prev_own_ref,
    prev_pair_ref,
    old_acc_ref,
    old_state_ref,
    acc_ref,
    state_ref,
    first_ref,
    lo_ref,
    hi_ref,
    even_ref,
    odd_ref,
):
    blk, x, slot = int_ref[0], int_ref[1], int_ref[2]

    @pl.when((slot < HEADS) & (blk == 0))
    def _():
        acc_ref[...] = old_acc_ref[...]
        state_ref[...] = old_state_ref[...]

    @pl.when((slot < HEADS) & (blk > 0))
    def _():
        find_documents(blk, x, int_ref, first_ref, lo_ref, hi_ref)

        def begin_of(i):
            return jnp.clip(lo_ref[i] + TILES, 0, TILES)

        refs = (prev_own_ref, prev_pair_ref)
        key_rows = key_places(x)

        def score(s_ref, i, q, g, n, m, masked):
            kept = None
            if masked:
                kept = key_rows >= first_ref[i : i + 1, :] - ((g - TILES) * WIDE + n * SPAN)
            return scores_of(refs, s_ref, q, g, n, m, kept)

        def score_first(masked, g, m):
            for n in range(2):
                m = score(even_ref, 0, q, g, n, m, masked)
            return m

        def middle_of(i, begin):
            return jnp.clip(hi_ref[i] + TILES + 1, begin, TILES)

        none = jnp.full((8, TILE), NEG, jnp.float32)
        zeros = jnp.zeros((8, TILE), jnp.float32)
        buffers = (even_ref, odd_ref)
        q = load_queries(q_own_ref, q_pair_ref, 0)
        begin = begin_of(0)
        middle = middle_of(0, begin)
        m = lax.fori_loop(begin, middle, functools.partial(score_first, True), none)
        m = lax.fori_loop(middle, TILES, functools.partial(score_first, False), m)
        for i in range(TILES):
            s_ref, later_ref = buffers[i % 2], buffers[(i + 1) % 2]
            own_l, own_top = old_state_ref[2 * i : 2 * i + 1, :], old_state_ref[2 * i + 1 : 2 * i + 2, :]
            top = jnp.maximum(jnp.max(m, axis=0, keepdims=True), own_top)
            shift = shift_of(top)
            scale = jnp.where(own_top > 0.5 * NEG, jnp.exp2(own_top * C - shift), 0.0)
            begin = begin_of(i)
            sums = (zeros, old_acc_ref[i] * scale)
            if i + 1 < TILES:
                q = load_queries(q_own_ref, q_pair_ref, i + 1)

                def step(masked, g, carry, i=i, q=q, shift=shift, s_ref=s_ref, later_ref=later_ref):
                    m, l, acc = carry
                    for n in range(2):
                        l, acc = mix(refs, s_ref, g, n, shift, l, acc)
                        m = score(later_ref, i + 1, q, g, n, m, masked)
                    return m, l, acc

                middle = middle_of(i + 1, begin)
                carry = (none,) + sums
                carry = lax.fori_loop(begin, middle, functools.partial(step, True), carry)
                m, l, acc = lax.fori_loop(middle, TILES, functools.partial(step, False), carry)
            else:
                l, acc = lax.fori_loop(
                    begin,
                    TILES,
                    lambda g, c, s_ref=s_ref, shift=shift: mix_block(refs, s_ref, g, shift, *c),
                    sums,
                )
            l = jnp.sum(l, axis=0, keepdims=True) + own_l * scale
            acc_ref[i] = acc
            state_ref[2 * i : 2 * i + 1, :] = l
            state_ref[2 * i + 1 : 2 * i + 2, :] = top


SCRATCH = [
    pltpu.VMEM((8, TILE), jnp.int32),
    pltpu.SMEM((TILES,), jnp.int32),
    pltpu.SMEM((TILES,), jnp.int32),
    pltpu.VMEM((TILES, TILE, TILE), jnp.float32),
    pltpu.VMEM((TILES, TILE, TILE), jnp.float32),
]
SMEM = pl.BlockSpec(memory_space=pltpu.SMEM)
VMEM = pl.BlockSpec(memory_space=pltpu.VMEM)
ACC = (TILES, HEAD_DIM, TILE)


def attend_own(ints, q_own, q_pair, own, pair):
    return pl.pallas_call(
        own_kernel,
        out_shape=(
            jax.ShapeDtypeStruct(ACC, jnp.float32),
            jax.ShapeDtypeStruct((2 * TILES, TILE), jnp.float32),
        ),
        in_specs=[SMEM] + [VMEM] * 4,
        out_specs=(VMEM, VMEM),
        scratch_shapes=SCRATCH,
        compiler_params=pltpu.CompilerParams(vmem_limit_bytes=16 << 20),
        cost_estimate=pl.CostEstimate(
            flops=1 << 30, bytes_accessed=4 << 20, transcendentals=2 << 20
        ),
        name="attend_own",
    )(ints, q_own, q_pair, own, pair)


def attend_prev(ints, q_own, q_pair, prev_own, prev_pair, acc, state):
    return pl.pallas_call(
        prev_kernel,
        out_shape=(
            jax.ShapeDtypeStruct(ACC, jnp.float32),
            jax.ShapeDtypeStruct((2 * TILES, TILE), jnp.float32),
        ),
        in_specs=[SMEM] + [VMEM] * 6,
        out_specs=(VMEM, VMEM),
        scratch_shapes=SCRATCH,
        compiler_params=pltpu.CompilerParams(vmem_limit_bytes=16 << 20),
        cost_estimate=pl.CostEstimate(
            flops=1 << 29, bytes_accessed=4 << 20, transcendentals=1 << 20
        ),
        name="attend_prev",
    )(ints, q_own, q_pair, prev_own, prev_pair, acc, state)


def weigh(ints, acc, state, other):
    return pl.pallas_call(
        weigh_kernel,
        out_shape=jax.ShapeDtypeStruct((Y, 2, HEAD_DIM, ROWS), jnp.bfloat16),
        in_specs=[SMEM] + [VMEM] * 3,
        out_specs=VMEM,
        name="weigh",
    )(ints, acc, state, other)


def body(queries, keys, values, lengths):
    x = 2 * lax.axis_index("xh") + lax.axis_index("xl")
    place = jnp.stack([lax.axis_index("blk"), x, lax.axis_index("y")]).astype(jnp.int32)
    ints = jnp.concatenate([place, lengths])
    got = lax.all_to_all(pack(queries, keys, values), "y", 0, 0, tiled=True)
    own_queries, own = got[:, :ROWS], got[:, ROWS:]
    pair = lax.ppermute(own, ("xh", "xl"), KEY_PAIRS)
    pair_queries = lax.ppermute(own_queries, "xl", QUERY_PAIRS)
    prev_own = lax.ppermute(own, "blk", [(0, 1)])
    pair, pair_queries, ints = lax.optimization_barrier((pair, pair_queries, ints))
    prev_pair = lax.ppermute(pair, "blk", [(0, 1)])
    state = attend_own(ints, own_queries, pair_queries, own, pair)
    acc, state = attend_prev(ints, own_queries, pair_queries, prev_own, prev_pair, *state)
    other = lax.ppermute(state, "xl", QUERY_PAIRS)
    parts = weigh(ints, acc, state, other).reshape(2 * Y, HEAD_DIM, ROWS)
    parts = lax.all_to_all(parts, ("y", "xl"), 0, 0, tiled=True)
    return combine(parts.reshape(Y, 2, HEAD_DIM, ROWS))


def solution(mesh):
    devices = mesh.devices.reshape(2, Y, 2, 2, mesh.devices.shape[2])
    fine = Mesh(devices, ("blk", "y", "xh", "xl", "tp"))
    rows = P(("blk", "y", "xh", "xl"), "tp")
    return jax.shard_map(
        body, mesh=fine, in_specs=(rows, rows, rows, P()), out_specs=rows, check_vma=False
    )
```

```python
import functools
import math

import jax
import jax.numpy as jnp
from jax import lax
from jax.experimental import pallas as pl
from jax.experimental.pallas import tpu as pltpu
from jax.sharding import Mesh, PartitionSpec as P

HEAD_DIM = 128
ROWS = 128
X = 4
Y = 8
HEADS = 5
DOCS = 32
SPAN = X * ROWS
WIDE = 2 * SPAN
WIDE_SHIFT = 10
TILE = 4 * ROWS
HALF = TILE // 2
TILES = Y // 2
GROUP = Y * SPAN
STATS = 16
PLACE = 3
NEG = -1e30
LOG2E = math.log2(math.e)
C = LOG2E / math.sqrt(HEAD_DIM)
KEY_PAIRS = [(x, X - 1 - x) for x in range(X)]
QUERY_PAIRS = [(0, 1), (1, 0)]


SMEM = pl.BlockSpec(memory_space=pltpu.SMEM)
VMEM = pl.BlockSpec(memory_space=pltpu.VMEM)


def pack_kernel(q_ref, k_ref, v_ref, out_ref):
    for h in range(HEADS):
        cols = slice(h * HEAD_DIM, (h + 1) * HEAD_DIM)
        out_ref[h, :ROWS, :] = q_ref[:, cols].T
        out_ref[h, ROWS : 2 * ROWS, :] = k_ref[:, cols]
        out_ref[h, 2 * ROWS :, :] = v_ref[:, cols].T


def pack(q, k, v):
    return pl.pallas_call(
        pack_kernel,
        out_shape=jax.ShapeDtypeStruct((Y, 2 * ROWS + HEAD_DIM, HEAD_DIM), jnp.bfloat16),
        name="pack",
    )(q, k, v)


def merge_kernel(int_ref, mine_ref, theirs_ref, out_ref):
    @pl.when(int_ref[2] < HEADS)
    def _():
        for y in range(Y):
            logs = []
            for ref in (mine_ref, theirs_ref):
                terms = ref[y, ROWS:, :].astype(jnp.float32)
                logs.append(terms[0:1] + terms[1:2] + terms[2:3])
            top = jnp.maximum(logs[0], logs[1])
            a, b = jnp.exp2(logs[0] - top), jnp.exp2(logs[1] - top)
            o = mine_ref[y, :ROWS, :].astype(jnp.float32) * (a / (a + b))
            o += theirs_ref[y, :ROWS, :].astype(jnp.float32) * (b / (a + b))
            out_ref[y] = o.astype(jnp.bfloat16)


def merge(ints, mine, theirs):
    return pl.pallas_call(
        merge_kernel,
        out_shape=jax.ShapeDtypeStruct((Y, HEAD_DIM, ROWS), jnp.bfloat16),
        in_specs=[SMEM, VMEM, VMEM],
        out_specs=VMEM,
        name="merge",
    )(ints, mine, theirs)


def unpack_kernel(in_ref, out_ref):
    for h in range(HEADS):
        out_ref[:, h * HEAD_DIM : (h + 1) * HEAD_DIM] = in_ref[h].T


def unpack(o):
    shape = (HEADS, HEAD_DIM, ROWS)
    return pl.pallas_call(
        unpack_kernel,
        grid=(1,),
        out_shape=jax.ShapeDtypeStruct((ROWS, HEADS * HEAD_DIM), jnp.bfloat16),
        in_specs=[pl.BlockSpec(shape, lambda i: (0, 0, 0))],
        out_specs=pl.BlockSpec((ROWS, HEADS * HEAD_DIM), lambda i: (0, 0)),
        name="unpack",
    )(o)


def places(x, shape):
    n = lax.broadcasted_iota(jnp.int32, shape, 1)
    return (
        jnp.where(n < 2 * ROWS, x, x ^ 1) * ROWS
        + (lax.shift_right_logical(n, 7) & 1) * SPAN
        + (n & (ROWS - 1))
    )


def find_documents(blk, x, int_ref, first_ref, lo_ref, hi_ref):
    base = blk * GROUP
    pos = places(x, (8, TILE)) + lax.broadcasted_iota(jnp.int32, (8, TILE), 0) * WIDE
    lowest = jnp.minimum(x, x ^ 1) * ROWS
    highest = SPAN + jnp.maximum(x, x ^ 1) * ROWS + ROWS - 1
    start = -base
    first = jnp.zeros((8, TILE), jnp.int32) - base
    los = [start] * TILES
    his = [start] * TILES
    for j in range(DOCS - 1):
        start = start + int_ref[PLACE + j]
        first = jnp.where(pos >= start, start, first)
        los = [jnp.where(lowest + i * WIDE >= start, start, los[i]) for i in range(TILES)]
        his = [jnp.where(highest + i * WIDE >= start, start, his[i]) for i in range(TILES)]
    first_ref[...] = first
    for i in range(TILES):
        lo_ref[i] = lax.shift_right_arithmetic(los[i], WIDE_SHIFT)
        hi_ref[i] = lax.shift_right_arithmetic(his[i], WIDE_SHIFT)


def key_places(x):
    row = lax.broadcasted_iota(jnp.int32, (HALF, TILE), 0)
    return jnp.where(row < ROWS, x, X - 1 - x) * ROWS + (row & (ROWS - 1))


def load_queries(q_own_ref, q_pair_ref, i):
    return jnp.concatenate(
        [q_own_ref[2 * i], q_own_ref[2 * i + 1], q_pair_ref[2 * i], q_pair_ref[2 * i + 1]],
        axis=1,
    )


def scores_of(refs, s_ref, q, g, n, m, kept):
    part = slice(n * HALF, (n + 1) * HALF)
    k = jnp.concatenate([ref[2 * g + n, :ROWS, :] for ref in refs], axis=0)
    s = jnp.dot(k, q, preferred_element_type=jnp.float32)
    if kept is not None:
        s = jnp.where(kept, s, NEG)
    s_ref[g, part, :] = s
    return jnp.maximum(m, jnp.max(s.reshape(HALF // 8, 8, TILE), axis=0))


def mix(refs, s_ref, g, n, shift, l, acc):
    part = slice(n * HALF, (n + 1) * HALF)
    p = jnp.exp2(s_ref[g, part, :] * C - shift)
    l = l + jnp.sum(p.reshape(HALF // 8, 8, TILE), axis=0)
    vt = jnp.concatenate([ref[2 * g + n, ROWS:, :] for ref in refs], axis=1)
    acc = acc + jnp.dot(vt, p.astype(jnp.bfloat16), preferred_element_type=jnp.float32)
    return l, acc


def mix_block(refs, s_ref, g, shift, l, acc):
    for n in range(2):
        l, acc = mix(refs, s_ref, g, n, shift, l, acc)
    return l, acc


def shift_of(top):
    return jnp.where(top > 0.5 * NEG, top * C, 0.0)


def own_kernel(
    int_ref,
    q_own_ref,
    q_pair_ref,
    own_ref,
    pair_ref,
    acc_ref,
    state_ref,
    first_ref,
    lo_ref,
    hi_ref,
    even_ref,
    odd_ref,
):
    blk, x, slot = int_ref[0], int_ref[1], int_ref[2]

    @pl.when(slot < HEADS)
    def _():
        find_documents(blk, x, int_ref, first_ref, lo_ref, hi_ref)

        refs = (own_ref, pair_ref)
        key_rows = key_places(x)

        def score(s_ref, i, q, g, n, m, masked, diagonal):
            kept = None
            if masked:
                kept = key_rows >= first_ref[i : i + 1, :] - (g * WIDE + n * SPAN)
                if diagonal:
                    kept &= key_rows <= places(x, (1, TILE)) - n * SPAN
            return scores_of(refs, s_ref, q, g, n, m, kept)

        def score_diagonal(s_ref, i, q, m):
            for n in range(2):
                m = score(s_ref, i, q, i, n, m, True, True)
            return m

        none = jnp.full((8, TILE), NEG, jnp.float32)
        zeros = jnp.zeros((8, TILE), jnp.float32)
        buffers = (even_ref, odd_ref)
        q = load_queries(q_own_ref, q_pair_ref, 0)
        m = score_diagonal(even_ref, 0, q, none)
        for i in range(TILES):
            s_ref, later_ref = buffers[i % 2], buffers[(i + 1) % 2]
            top = jnp.max(m, axis=0, keepdims=True)
            shift = shift_of(top)
            begin = jnp.maximum(lo_ref[i], 0)
            sums = (zeros, jnp.zeros((HEAD_DIM, TILE), jnp.float32))
            if i + 1 < TILES:
                q = load_queries(q_own_ref, q_pair_ref, i + 1)

                def step(masked, g, carry, i=i, q=q, shift=shift, s_ref=s_ref, later_ref=later_ref):
                    m, l, acc = carry
                    for n in range(2):
                        l, acc = mix(refs, s_ref, g, n, shift, l, acc)
                        m = score(later_ref, i + 1, q, g, n, m, masked, False)
                    return m, l, acc

                carry = (none,) + sums
                if i > 0:
                    middle = jnp.clip(hi_ref[i + 1] + 1, begin, i)
                    carry = lax.fori_loop(begin, middle, functools.partial(step, True), carry)
                    carry = lax.fori_loop(middle, i, functools.partial(step, False), carry)
                m, l, acc = step(True, i, carry)
                m = score_diagonal(later_ref, i + 1, q, m)
            else:
                l, acc = lax.fori_loop(
                    begin,
                    i + 1,
                    lambda g, c, s_ref=s_ref, shift=shift: mix_block(refs, s_ref, g, shift, *c),
                    sums,
                )
            l = jnp.sum(l, axis=0, keepdims=True)
            row = lax.broadcasted_iota(jnp.int32, (8, TILE), 0)
            acc_ref[i] = acc
            state_ref[i] = jnp.where(row == 0, l, top)


def prev_kernel(
    int_ref,
    q_own_ref,
    q_pair_ref,
    prev_own_ref,
    prev_pair_ref,
    acc_ref,
    state_ref,
    mine_ref,
    theirs_ref,
    first_ref,
    lo_ref,
    hi_ref,
    even_ref,
    odd_ref,
):
    blk, x, slot = int_ref[0], int_ref[1], int_ref[2]

    @pl.when(slot < HEADS)
    def _():
        find_documents(blk, x, int_ref, first_ref, lo_ref, hi_ref)

        def begin_of(i):
            return jnp.where(blk > 0, jnp.clip(lo_ref[i] + TILES, 0, TILES), TILES)

        refs = (prev_own_ref, prev_pair_ref)
        key_rows = key_places(x)

        def score(s_ref, i, q, g, n, m, masked):
            kept = None
            if masked:
                kept = key_rows >= first_ref[i : i + 1, :] - ((g - TILES) * WIDE + n * SPAN)
            return scores_of(refs, s_ref, q, g, n, m, kept)

        def score_first(masked, g, m):
            for n in range(2):
                m = score(even_ref, 0, q, g, n, m, masked)
            return m

        def middle_of(i, begin):
            return jnp.clip(hi_ref[i] + TILES + 1, begin, TILES)

        none = jnp.full((8, TILE), NEG, jnp.float32)
        zeros = jnp.zeros((8, TILE), jnp.float32)
        buffers = (even_ref, odd_ref)
        q = load_queries(q_own_ref, q_pair_ref, 0)
        begin = begin_of(0)
        middle = middle_of(0, begin)
        m = lax.fori_loop(begin, middle, functools.partial(score_first, True), none)
        m = lax.fori_loop(middle, TILES, functools.partial(score_first, False), m)
        for i in range(TILES):
            s_ref, later_ref = buffers[i % 2], buffers[(i + 1) % 2]
            own_l, own_top = state_ref[i, 0:1, :], state_ref[i, 1:2, :]
            top = jnp.maximum(jnp.max(m, axis=0, keepdims=True), own_top)
            shift = shift_of(top)
            scale = jnp.where(own_top > 0.5 * NEG, jnp.exp2(own_top * C - shift), 0.0)
            begin = begin_of(i)
            sums = (zeros, acc_ref[i] * scale)
            if i + 1 < TILES:
                q = load_queries(q_own_ref, q_pair_ref, i + 1)

                def step(masked, g, carry, i=i, q=q, shift=shift, s_ref=s_ref, later_ref=later_ref):
                    m, l, acc = carry
                    for n in range(2):
                        l, acc = mix(refs, s_ref, g, n, shift, l, acc)
                        m = score(later_ref, i + 1, q, g, n, m, masked)
                    return m, l, acc

                middle = middle_of(i + 1, begin)
                carry = (none,) + sums
                carry = lax.fori_loop(begin, middle, functools.partial(step, True), carry)
                m, l, acc = lax.fori_loop(middle, TILES, functools.partial(step, False), carry)
            else:
                l, acc = lax.fori_loop(
                    begin,
                    TILES,
                    lambda g, c, s_ref=s_ref, shift=shift: mix_block(refs, s_ref, g, shift, *c),
                    sums,
                )
            l = jnp.sum(l, axis=0, keepdims=True) + own_l * scale
            some = l > 0.0
            l = jnp.where(some, l, 1.0)
            o = (acc * (1.0 / l)).astype(jnp.bfloat16)
            log = jnp.where(some, shift + jnp.log(l) * LOG2E, NEG)
            high = log.astype(jnp.bfloat16).astype(jnp.float32)
            middle = (log - high).astype(jnp.bfloat16).astype(jnp.float32)
            low = log - high - middle
            row = lax.broadcasted_iota(jnp.int32, (STATS, TILE), 0)
            stats = jnp.where(row == 0, high, jnp.where(row == 1, middle, low))
            stats = stats.astype(jnp.bfloat16)
            for n in range(4):
                part = slice(n * ROWS, (n + 1) * ROWS)
                ref = mine_ref if n < 2 else theirs_ref
                ref[2 * i + (n & 1), :ROWS, :] = o[:, part]
                ref[2 * i + (n & 1), ROWS:, :] = stats[:, part]


SCRATCH = [
    pltpu.VMEM((8, TILE), jnp.int32),
    pltpu.SMEM((TILES,), jnp.int32),
    pltpu.SMEM((TILES,), jnp.int32),
    pltpu.VMEM((TILES, TILE, TILE), jnp.float32),
    pltpu.VMEM((TILES, TILE, TILE), jnp.float32),
]
ACC = (TILES, HEAD_DIM, TILE)


def attend_own(ints, q_own, q_pair, own, pair):
    return pl.pallas_call(
        own_kernel,
        out_shape=(
            jax.ShapeDtypeStruct(ACC, jnp.float32),
            jax.ShapeDtypeStruct((TILES, 8, TILE), jnp.float32),
        ),
        in_specs=[SMEM] + [VMEM] * 4,
        out_specs=(VMEM, VMEM),
        scratch_shapes=SCRATCH,
        compiler_params=pltpu.CompilerParams(vmem_limit_bytes=16 << 20),
        cost_estimate=pl.CostEstimate(
            flops=1 << 30, bytes_accessed=4 << 20, transcendentals=2 << 20
        ),
        name="attend_own",
    )(ints, q_own, q_pair, own, pair)


def attend_prev(ints, q_own, q_pair, prev_own, prev_pair, acc, state):
    return pl.pallas_call(
        prev_kernel,
        out_shape=(jax.ShapeDtypeStruct((Y, HEAD_DIM + STATS, ROWS), jnp.bfloat16),) * 2,
        in_specs=[SMEM] + [VMEM] * 6,
        out_specs=(VMEM, VMEM),
        scratch_shapes=SCRATCH,
        compiler_params=pltpu.CompilerParams(vmem_limit_bytes=16 << 20),
        cost_estimate=pl.CostEstimate(
            flops=1 << 29, bytes_accessed=4 << 20, transcendentals=1 << 20
        ),
        name="attend_prev",
    )(ints, q_own, q_pair, prev_own, prev_pair, acc, state)


def body(queries, keys, values, lengths):
    x = 2 * lax.axis_index("xh") + lax.axis_index("xl")
    place = jnp.stack([lax.axis_index("blk"), x, lax.axis_index("y")]).astype(jnp.int32)
    ints = jnp.concatenate([place, lengths])
    got = lax.all_to_all(pack(queries, keys, values), "y", 0, 0, tiled=True)
    own_queries, own = got[:, :ROWS], got[:, ROWS:]
    pair = lax.ppermute(own, ("xh", "xl"), KEY_PAIRS)
    pair_queries = lax.ppermute(own_queries, "xl", QUERY_PAIRS)
    prev_own = lax.ppermute(own, "blk", [(0, 1)])
    pair, pair_queries, ints = lax.optimization_barrier((pair, pair_queries, ints))
    prev_pair = lax.ppermute(pair, "blk", [(0, 1)])
    state = attend_own(ints, own_queries, pair_queries, own, pair)
    mine, theirs = attend_prev(ints, own_queries, pair_queries, prev_own, prev_pair, *state)
    theirs = lax.ppermute(theirs, "xl", QUERY_PAIRS)
    o = merge(ints, mine, theirs)
    return unpack(lax.all_to_all(o, "y", 0, 0, tiled=True))


def solution(mesh):
    devices = mesh.devices.reshape(2, Y, 2, 2, mesh.devices.shape[2])
    fine = Mesh(devices, ("blk", "y", "xh", "xl", "tp"))
    rows = P(("blk", "y", "xh", "xl"), "tp")
    return jax.shard_map(
        body, mesh=fine, in_specs=(rows, rows, rows, P()), out_specs=rows, check_vma=False
    )
```

```python
import functools
import math

import jax
import jax.numpy as jnp
from jax import lax
from jax.experimental import pallas as pl
from jax.experimental.pallas import tpu as pltpu
from jax.sharding import Mesh, PartitionSpec as P

HEAD_DIM = 128
ROWS = 128
X = 4
Y = 8
HEADS = 5
DOCS = 32
SPAN = X * ROWS
WIDE = 2 * SPAN
WIDE_SHIFT = 10
TILE = 4 * ROWS
HALF = TILE // 2
TILES = Y // 2
GROUP = Y * SPAN
STATS = 16
PLACE = 3
NEG = -1e30
LOG2E = math.log2(math.e)
C = LOG2E / math.sqrt(HEAD_DIM)
KEY_PAIRS = [[(g * X + x, g * X + X - 1 - x) for x in range(X)] for g in range(2)]
QUERY_PAIRS = [(0, 1), (1, 0)]


def pack_kernel(q_ref, k_ref, v_ref, out_ref):
    for h in range(HEADS):
        cols = slice(h * HEAD_DIM, (h + 1) * HEAD_DIM)
        out_ref[h, :ROWS, :] = q_ref[:, cols].T
        out_ref[h, ROWS : 2 * ROWS, :] = k_ref[:, cols]
        out_ref[h, 2 * ROWS :, :] = v_ref[:, cols].T


def pack(q, k, v):
    return pl.pallas_call(
        pack_kernel,
        out_shape=jax.ShapeDtypeStruct((Y, 2 * ROWS + HEAD_DIM, HEAD_DIM), jnp.bfloat16),
        name="pack",
    )(q, k, v)


def combine_kernel(in_ref, out_ref):
    for h in range(HEADS):
        logs = []
        for n in range(2):
            terms = in_ref[h, n, ROWS:, :].astype(jnp.float32)
            logs.append(terms[0:1] + terms[1:2] + terms[2:3])
        top = jnp.maximum(logs[0], logs[1])
        a, b = jnp.exp2(logs[0] - top), jnp.exp2(logs[1] - top)
        o = in_ref[h, 0, :ROWS, :].astype(jnp.float32) * (a / (a + b))
        o += in_ref[h, 1, :ROWS, :].astype(jnp.float32) * (b / (a + b))
        out_ref[:, h * HEAD_DIM : (h + 1) * HEAD_DIM] = o.T.astype(jnp.bfloat16)


def combine(parts):
    shape = (HEADS, 2, ROWS + STATS, HEAD_DIM)
    return pl.pallas_call(
        combine_kernel,
        grid=(1,),
        out_shape=jax.ShapeDtypeStruct((ROWS, HEADS * HEAD_DIM), jnp.bfloat16),
        in_specs=[pl.BlockSpec(shape, lambda i: (0, 0, 0, 0))],
        out_specs=pl.BlockSpec((ROWS, HEADS * HEAD_DIM), lambda i: (0, 0)),
        name="combine",
    )(parts)


def places(x, shape):
    n = lax.broadcasted_iota(jnp.int32, shape, 1)
    return (
        jnp.where(n < 2 * ROWS, x, x ^ 1) * ROWS
        + (lax.shift_right_logical(n, 7) & 1) * SPAN
        + (n & (ROWS - 1))
    )


def find_documents(blk, x, int_ref, first_ref, lo_ref, hi_ref):
    base = blk * GROUP
    pos = places(x, (8, TILE)) + lax.broadcasted_iota(jnp.int32, (8, TILE), 0) * WIDE
    lowest = jnp.minimum(x, x ^ 1) * ROWS
    highest = SPAN + jnp.maximum(x, x ^ 1) * ROWS + ROWS - 1
    start = -base
    first = jnp.zeros((8, TILE), jnp.int32) - base
    los = [start] * TILES
    his = [start] * TILES
    for j in range(DOCS - 1):
        start = start + int_ref[PLACE + j]
        first = jnp.where(pos >= start, start, first)
        los = [jnp.where(lowest + i * WIDE >= start, start, los[i]) for i in range(TILES)]
        his = [jnp.where(highest + i * WIDE >= start, start, his[i]) for i in range(TILES)]
    first_ref[...] = first
    for i in range(TILES):
        lo_ref[i] = lax.shift_right_arithmetic(los[i], WIDE_SHIFT)
        hi_ref[i] = lax.shift_right_arithmetic(his[i], WIDE_SHIFT)


def key_places(x):
    row = lax.broadcasted_iota(jnp.int32, (HALF, TILE), 0)
    return jnp.where(row < ROWS, x, X - 1 - x) * ROWS + (row & (ROWS - 1))


def load_queries(q_own_ref, q_pair_ref, i):
    return jnp.concatenate(
        [q_own_ref[2 * i], q_own_ref[2 * i + 1], q_pair_ref[2 * i], q_pair_ref[2 * i + 1]],
        axis=1,
    )


def scores_of(refs, s_ref, q, g, n, m, kept):
    part = slice(n * HALF, (n + 1) * HALF)
    k = jnp.concatenate([ref[2 * g + n, :ROWS, :] for ref in refs], axis=0)
    s = jnp.dot(k, q, preferred_element_type=jnp.float32)
    if kept is not None:
        s = jnp.where(kept, s, NEG)
    s_ref[g, part, :] = s
    return jnp.maximum(m, jnp.max(s.reshape(HALF // 8, 8, TILE), axis=0))


def mix(refs, s_ref, g, n, shift, l, acc):
    part = slice(n * HALF, (n + 1) * HALF)
    p = jnp.exp2(s_ref[g, part, :] * C - shift)
    l = l + jnp.sum(p.reshape(HALF // 8, 8, TILE), axis=0)
    vt = jnp.concatenate([ref[2 * g + n, ROWS:, :] for ref in refs], axis=1)
    acc = acc + jnp.dot(vt, p.astype(jnp.bfloat16), preferred_element_type=jnp.float32)
    return l, acc


def mix_block(refs, s_ref, g, shift, l, acc):
    for n in range(2):
        l, acc = mix(refs, s_ref, g, n, shift, l, acc)
    return l, acc


def shift_of(top):
    return jnp.where(top > 0.5 * NEG, top * C, 0.0)


def own_kernel(
    int_ref,
    q_own_ref,
    q_pair_ref,
    own_ref,
    first_pair_ref,
    second_pair_ref,
    acc_ref,
    state_ref,
    first_ref,
    lo_ref,
    hi_ref,
    even_ref,
    odd_ref,
    pair_ref,
):
    blk, x, slot = int_ref[0], int_ref[1], int_ref[2]

    @pl.when(slot < HEADS)
    def _():
        find_documents(blk, x, int_ref, first_ref, lo_ref, hi_ref)

        @pl.when(blk == 0)
        def _():
            pair_ref[...] = first_pair_ref[...]

        @pl.when(blk > 0)
        def _():
            pair_ref[...] = second_pair_ref[...]

        refs = (own_ref, pair_ref)
        key_rows = key_places(x)

        def score(s_ref, i, q, g, n, m, masked, diagonal):
            kept = None
            if masked:
                kept = key_rows >= first_ref[i : i + 1, :] - (g * WIDE + n * SPAN)
                if diagonal:
                    kept &= key_rows <= places(x, (1, TILE)) - n * SPAN
            return scores_of(refs, s_ref, q, g, n, m, kept)

        def score_diagonal(s_ref, i, q, m):
            for n in range(2):
                m = score(s_ref, i, q, i, n, m, True, True)
            return m

        none = jnp.full((8, TILE), NEG, jnp.float32)
        zeros = jnp.zeros((8, TILE), jnp.float32)
        buffers = (even_ref, odd_ref)
        q = load_queries(q_own_ref, q_pair_ref, 0)
        m = score_diagonal(even_ref, 0, q, none)
        for i in range(TILES):
            s_ref, later_ref = buffers[i % 2], buffers[(i + 1) % 2]
            top = jnp.max(m, axis=0, keepdims=True)
            shift = shift_of(top)
            begin = jnp.maximum(lo_ref[i], 0)
            sums = (zeros, jnp.zeros((HEAD_DIM, TILE), jnp.float32))
            if i + 1 < TILES:
                q = load_queries(q_own_ref, q_pair_ref, i + 1)

                def step(masked, g, carry, i=i, q=q, shift=shift, s_ref=s_ref, later_ref=later_ref):
                    m, l, acc = carry
                    for n in range(2):
                        l, acc = mix(refs, s_ref, g, n, shift, l, acc)
                        m = score(later_ref, i + 1, q, g, n, m, masked, False)
                    return m, l, acc

                carry = (none,) + sums
                if i > 0:
                    middle = jnp.clip(hi_ref[i + 1] + 1, begin, i)
                    carry = lax.fori_loop(begin, middle, functools.partial(step, True), carry)
                    carry = lax.fori_loop(middle, i, functools.partial(step, False), carry)
                m, l, acc = step(True, i, carry)
                m = score_diagonal(later_ref, i + 1, q, m)
            else:
                l, acc = lax.fori_loop(
                    begin,
                    i + 1,
                    lambda g, c, s_ref=s_ref, shift=shift: mix_block(refs, s_ref, g, shift, *c),
                    sums,
                )
            l = jnp.sum(l, axis=0, keepdims=True)
            row = lax.broadcasted_iota(jnp.int32, (8, TILE), 0)
            acc_ref[i] = acc
            state_ref[i] = jnp.where(row == 0, l, top)


def prev_kernel(
    int_ref,
    q_own_ref,
    q_pair_ref,
    prev_own_ref,
    prev_pair_ref,
    acc_ref,
    state_ref,
    o_ref,
    first_ref,
    lo_ref,
    hi_ref,
    even_ref,
    odd_ref,
):
    blk, x, slot = int_ref[0], int_ref[1], int_ref[2]

    @pl.when(slot < HEADS)
    def _():
        find_documents(blk, x, int_ref, first_ref, lo_ref, hi_ref)

        def begin_of(i):
            return jnp.where(blk > 0, jnp.clip(lo_ref[i] + TILES, 0, TILES), TILES)

        refs = (prev_own_ref, prev_pair_ref)
        key_rows = key_places(x)

        def score(s_ref, i, q, g, n, m, masked):
            kept = None
            if masked:
                kept = key_rows >= first_ref[i : i + 1, :] - ((g - TILES) * WIDE + n * SPAN)
            return scores_of(refs, s_ref, q, g, n, m, kept)

        def score_first(masked, g, m):
            for n in range(2):
                m = score(even_ref, 0, q, g, n, m, masked)
            return m

        def middle_of(i, begin):
            return jnp.clip(hi_ref[i] + TILES + 1, begin, TILES)

        none = jnp.full((8, TILE), NEG, jnp.float32)
        zeros = jnp.zeros((8, TILE), jnp.float32)
        buffers = (even_ref, odd_ref)
        q = load_queries(q_own_ref, q_pair_ref, 0)
        begin = begin_of(0)
        middle = middle_of(0, begin)
        m = lax.fori_loop(begin, middle, functools.partial(score_first, True), none)
        m = lax.fori_loop(middle, TILES, functools.partial(score_first, False), m)
        for i in range(TILES):
            s_ref, later_ref = buffers[i % 2], buffers[(i + 1) % 2]
            own_l, own_top = state_ref[i, 0:1, :], state_ref[i, 1:2, :]
            top = jnp.maximum(jnp.max(m, axis=0, keepdims=True), own_top)
            shift = shift_of(top)
            scale = jnp.where(own_top > 0.5 * NEG, jnp.exp2(own_top * C - shift), 0.0)
            begin = begin_of(i)
            sums = (zeros, acc_ref[i] * scale)
            if i + 1 < TILES:
                q = load_queries(q_own_ref, q_pair_ref, i + 1)

                def step(masked, g, carry, i=i, q=q, shift=shift, s_ref=s_ref, later_ref=later_ref):
                    m, l, acc = carry
                    for n in range(2):
                        l, acc = mix(refs, s_ref, g, n, shift, l, acc)
                        m = score(later_ref, i + 1, q, g, n, m, masked)
                    return m, l, acc

                middle = middle_of(i + 1, begin)
                carry = (none,) + sums
                carry = lax.fori_loop(begin, middle, functools.partial(step, True), carry)
                m, l, acc = lax.fori_loop(middle, TILES, functools.partial(step, False), carry)
            else:
                l, acc = lax.fori_loop(
                    begin,
                    TILES,
                    lambda g, c, s_ref=s_ref, shift=shift: mix_block(refs, s_ref, g, shift, *c),
                    sums,
                )
            l = jnp.sum(l, axis=0, keepdims=True) + own_l * scale
            some = l > 0.0
            l = jnp.where(some, l, 1.0)
            o = (acc * (1.0 / l)).astype(jnp.bfloat16)
            log = jnp.where(some, shift + jnp.log(l) * LOG2E, NEG)
            high = log.astype(jnp.bfloat16).astype(jnp.float32)
            middle = (log - high).astype(jnp.bfloat16).astype(jnp.float32)
            low = log - high - middle
            row = lax.broadcasted_iota(jnp.int32, (STATS, TILE), 0)
            stats = jnp.where(row == 0, high, jnp.where(row == 1, middle, low))
            stats = stats.astype(jnp.bfloat16)
            for n in range(4):
                part = slice(n * ROWS, (n + 1) * ROWS)
                y, to = 2 * i + (n & 1), (x & 1) ^ (n >> 1)
                o_ref[y, to, :ROWS, :] = o[:, part]
                o_ref[y, to, ROWS:, :] = stats[:, part]


SCRATCH = [
    pltpu.VMEM((8, TILE), jnp.int32),
    pltpu.SMEM((TILES,), jnp.int32),
    pltpu.SMEM((TILES,), jnp.int32),
    pltpu.VMEM((TILES, TILE, TILE), jnp.float32),
    pltpu.VMEM((TILES, TILE, TILE), jnp.float32),
]
SMEM = pl.BlockSpec(memory_space=pltpu.SMEM)
VMEM = pl.BlockSpec(memory_space=pltpu.VMEM)
ACC = (TILES, HEAD_DIM, TILE)


def attend_own(ints, q_own, q_pair, own, first_pair, second_pair):
    return pl.pallas_call(
        own_kernel,
        out_shape=(
            jax.ShapeDtypeStruct(ACC, jnp.float32),
            jax.ShapeDtypeStruct((TILES, 8, TILE), jnp.float32),
        ),
        in_specs=[SMEM] + [VMEM] * 5,
        out_specs=(VMEM, VMEM),
        scratch_shapes=SCRATCH + [pltpu.VMEM((Y, 2 * ROWS, HEAD_DIM), jnp.bfloat16)],
        compiler_params=pltpu.CompilerParams(vmem_limit_bytes=16 << 20),
        cost_estimate=pl.CostEstimate(
            flops=1 << 30, bytes_accessed=4 << 20, transcendentals=2 << 20
        ),
        name="attend_own",
    )(ints, q_own, q_pair, own, first_pair, second_pair)


def attend_prev(ints, q_own, q_pair, prev_own, prev_pair, acc, state):
    return pl.pallas_call(
        prev_kernel,
        out_shape=jax.ShapeDtypeStruct((Y, 2, ROWS + STATS, HEAD_DIM), jnp.bfloat16),
        in_specs=[SMEM] + [VMEM] * 6,
        out_specs=VMEM,
        scratch_shapes=SCRATCH,
        compiler_params=pltpu.CompilerParams(vmem_limit_bytes=16 << 20),
        cost_estimate=pl.CostEstimate(
            flops=1 << 29, bytes_accessed=4 << 20, transcendentals=1 << 20
        ),
        name="attend_prev",
    )(ints, q_own, q_pair, prev_own, prev_pair, acc, state)


def body(queries, keys, values, lengths):
    x = 2 * lax.axis_index("xh") + lax.axis_index("xl")
    place = jnp.stack([lax.axis_index("blk"), x, lax.axis_index("y")]).astype(jnp.int32)
    ints = jnp.concatenate([place, lengths])
    got = lax.all_to_all(pack(queries, keys, values), "y", 0, 0, tiled=True)
    own_queries, own = got[:, :ROWS], got[:, ROWS:]
    axes = ("blk", "xh", "xl")
    pair_first = lax.ppermute(own, axes, KEY_PAIRS[0])
    pair_queries = lax.ppermute(own_queries, "xl", QUERY_PAIRS)
    prev_own = lax.ppermute(own, "blk", [(0, 1)])
    later, pair_queries, ints = lax.optimization_barrier((own, pair_queries, ints))
    pair_second = lax.ppermute(later, axes, KEY_PAIRS[1])
    prev_pair = lax.ppermute(pair_first, "blk", [(0, 1)])
    state = attend_own(ints, own_queries, pair_queries, own, pair_first, pair_second)
    parts = attend_prev(ints, own_queries, pair_queries, prev_own, prev_pair, *state)
    parts = parts.reshape(2 * Y, ROWS + STATS, HEAD_DIM)
    parts = lax.all_to_all(parts, ("y", "xl"), 0, 0, tiled=True)
    return combine(parts.reshape(Y, 2, ROWS + STATS, HEAD_DIM))


def solution(mesh):
    devices = mesh.devices.reshape(2, Y, 2, 2, mesh.devices.shape[2])
    fine = Mesh(devices, ("blk", "y", "xh", "xl", "tp"))
    rows = P(("blk", "y", "xh", "xl"), "tp")
    return jax.shard_map(
        body, mesh=fine, in_specs=(rows, rows, rows, P()), out_specs=rows, check_vma=False
    )
```

```python
import functools
import math

import jax
import jax.numpy as jnp
from jax import lax
from jax.experimental import pallas as pl
from jax.experimental.pallas import tpu as pltpu
from jax.sharding import Mesh, PartitionSpec as P

HEAD_DIM = 128
ROWS = 128
X = 4
Y = 8
HEADS = 5
DOCS = 32
SPAN = X * ROWS
WIDE = 2 * SPAN
WIDE_SHIFT = 10
TILE = 4 * ROWS
HALF = TILE // 2
TILES = Y // 2
GROUP = Y * SPAN
STATS = 16
PLACE = 3
NEG = -1e30
LOG2E = math.log2(math.e)
C = LOG2E / math.sqrt(HEAD_DIM)
KEY_PAIRS = [[(g * X + x, g * X + X - 1 - x) for x in range(X)] for g in range(2)]
QUERY_PAIRS = [(0, 1), (1, 0)]


def pack_kernel(q_ref, k_ref, v_ref, out_ref):
    for h in range(HEADS):
        cols = slice(h * HEAD_DIM, (h + 1) * HEAD_DIM)
        out_ref[h, :ROWS, :] = q_ref[:, cols].T
        out_ref[h, ROWS : 2 * ROWS, :] = k_ref[:, cols]
        out_ref[h, 2 * ROWS :, :] = v_ref[:, cols].T


def pack(q, k, v):
    return pl.pallas_call(
        pack_kernel,
        out_shape=jax.ShapeDtypeStruct((Y, 2 * ROWS + HEAD_DIM, HEAD_DIM), jnp.bfloat16),
        name="pack",
    )(q, k, v)


def combine_kernel(in_ref, out_ref):
    for h in range(HEADS):
        logs = []
        for n in range(2):
            terms = in_ref[h, n, ROWS:, :].astype(jnp.float32)
            logs.append(terms[0:1] + terms[1:2] + terms[2:3])
        top = jnp.maximum(logs[0], logs[1])
        a, b = jnp.exp2(logs[0] - top), jnp.exp2(logs[1] - top)
        o = in_ref[h, 0, :ROWS, :].astype(jnp.float32) * (a / (a + b))
        o += in_ref[h, 1, :ROWS, :].astype(jnp.float32) * (b / (a + b))
        out_ref[:, h * HEAD_DIM : (h + 1) * HEAD_DIM] = o.T.astype(jnp.bfloat16)


def combine(parts):
    shape = (HEADS, 2, ROWS + STATS, HEAD_DIM)
    return pl.pallas_call(
        combine_kernel,
        grid=(1,),
        out_shape=jax.ShapeDtypeStruct((ROWS, HEADS * HEAD_DIM), jnp.bfloat16),
        in_specs=[pl.BlockSpec(shape, lambda i: (0, 0, 0, 0))],
        out_specs=pl.BlockSpec((ROWS, HEADS * HEAD_DIM), lambda i: (0, 0)),
        name="combine",
    )(parts)


def places(x, shape):
    n = lax.broadcasted_iota(jnp.int32, shape, 1)
    return (
        jnp.where(n < 2 * ROWS, x, x ^ 1) * ROWS
        + (lax.shift_right_logical(n, 7) & 1) * SPAN
        + (n & (ROWS - 1))
    )


def find_documents(blk, x, int_ref, first_ref, lo_ref, hi_ref):
    base = blk * GROUP
    pos = places(x, (8, TILE)) + lax.broadcasted_iota(jnp.int32, (8, TILE), 0) * WIDE
    lowest = jnp.minimum(x, x ^ 1) * ROWS
    highest = SPAN + jnp.maximum(x, x ^ 1) * ROWS + ROWS - 1
    start = -base
    first = jnp.zeros((8, TILE), jnp.int32) - base
    los = [start] * TILES
    his = [start] * TILES
    for j in range(DOCS - 1):
        start = start + int_ref[PLACE + j]
        first = jnp.where(pos >= start, start, first)
        los = [jnp.where(lowest + i * WIDE >= start, start, los[i]) for i in range(TILES)]
        his = [jnp.where(highest + i * WIDE >= start, start, his[i]) for i in range(TILES)]
    first_ref[...] = first
    for i in range(TILES):
        lo_ref[i] = lax.shift_right_arithmetic(los[i], WIDE_SHIFT)
        hi_ref[i] = lax.shift_right_arithmetic(his[i], WIDE_SHIFT)


def key_places(x):
    row = lax.broadcasted_iota(jnp.int32, (HALF, TILE), 0)
    return jnp.where(row < ROWS, x, X - 1 - x) * ROWS + (row & (ROWS - 1))


def load_queries(q_own_ref, q_pair_ref, i):
    return jnp.concatenate(
        [q_own_ref[2 * i], q_own_ref[2 * i + 1], q_pair_ref[2 * i], q_pair_ref[2 * i + 1]],
        axis=1,
    )


def scores_of(refs, s_ref, q, g, n, m, kept):
    part = slice(n * HALF, (n + 1) * HALF)
    k = jnp.concatenate([ref[2 * g + n, :ROWS, :] for ref in refs], axis=0)
    s = jnp.dot(k, q, preferred_element_type=jnp.float32)
    if kept is not None:
        s = jnp.where(kept, s, NEG)
    s_ref[g, part, :] = s
    return jnp.maximum(m, jnp.max(s.reshape(HALF // 8, 8, TILE), axis=0))


def mix(refs, s_ref, g, n, shift, l, acc):
    part = slice(n * HALF, (n + 1) * HALF)
    p = jnp.exp2(s_ref[g, part, :] * C - shift)
    l = l + jnp.sum(p.reshape(HALF // 8, 8, TILE), axis=0)
    vt = jnp.concatenate([ref[2 * g + n, ROWS:, :] for ref in refs], axis=1)
    acc = acc + jnp.dot(vt, p.astype(jnp.bfloat16), preferred_element_type=jnp.float32)
    return l, acc


def mix_block(refs, s_ref, g, shift, l, acc):
    for n in range(2):
        l, acc = mix(refs, s_ref, g, n, shift, l, acc)
    return l, acc


def shift_of(top):
    return jnp.where(top > 0.5 * NEG, top * C, 0.0)


def own_kernel(
    int_ref,
    q_own_ref,
    q_pair_ref,
    own_ref,
    first_pair_ref,
    second_pair_ref,
    acc_ref,
    state_ref,
    first_ref,
    lo_ref,
    hi_ref,
    even_ref,
    odd_ref,
    pair_ref,
):
    blk, x, slot = int_ref[0], int_ref[1], int_ref[2]

    @pl.when(slot < HEADS)
    def _():
        find_documents(blk, x, int_ref, first_ref, lo_ref, hi_ref)

        @pl.when(blk == 0)
        def _():
            pair_ref[...] = first_pair_ref[...]

        @pl.when(blk > 0)
        def _():
            pair_ref[...] = second_pair_ref[...]

        refs = (own_ref, pair_ref)
        key_rows = key_places(x)

        def score(s_ref, i, q, g, n, m, masked, diagonal):
            kept = None
            if masked:
                kept = key_rows >= first_ref[i : i + 1, :] - (g * WIDE + n * SPAN)
                if diagonal:
                    kept &= key_rows <= places(x, (1, TILE)) - n * SPAN
            return scores_of(refs, s_ref, q, g, n, m, kept)

        def score_diagonal(s_ref, i, q, m):
            for n in range(2):
                m = score(s_ref, i, q, i, n, m, True, True)
            return m

        none = jnp.full((8, TILE), NEG, jnp.float32)
        zeros = jnp.zeros((8, TILE), jnp.float32)
        buffers = (even_ref, odd_ref)
        q = load_queries(q_own_ref, q_pair_ref, 0)
        m = score_diagonal(even_ref, 0, q, none)
        for i in range(TILES):
            s_ref, later_ref = buffers[i % 2], buffers[(i + 1) % 2]
            top = jnp.max(m, axis=0, keepdims=True)
            shift = shift_of(top)
            begin = jnp.maximum(lo_ref[i], 0)
            sums = (zeros, jnp.zeros((HEAD_DIM, TILE), jnp.float32))
            if i + 1 < TILES:
                q = load_queries(q_own_ref, q_pair_ref, i + 1)

                def step(masked, g, carry, i=i, q=q, shift=shift, s_ref=s_ref, later_ref=later_ref):
                    m, l, acc = carry
                    for n in range(2):
                        l, acc = mix(refs, s_ref, g, n, shift, l, acc)
                        m = score(later_ref, i + 1, q, g, n, m, masked, False)
                    return m, l, acc

                carry = (none,) + sums
                if i > 0:
                    middle = jnp.clip(hi_ref[i + 1] + 1, begin, i)
                    carry = lax.fori_loop(begin, middle, functools.partial(step, True), carry)
                    carry = lax.fori_loop(middle, i, functools.partial(step, False), carry)
                m, l, acc = step(True, i, carry)
                m = score_diagonal(later_ref, i + 1, q, m)
            else:
                l, acc = lax.fori_loop(
                    begin,
                    i + 1,
                    lambda g, c, s_ref=s_ref, shift=shift: mix_block(refs, s_ref, g, shift, *c),
                    sums,
                )
            l = jnp.sum(l, axis=0, keepdims=True)
            row = lax.broadcasted_iota(jnp.int32, (8, TILE), 0)
            acc_ref[i] = acc
            state_ref[i] = jnp.where(row == 0, l, top)


def prev_kernel(
    int_ref,
    q_own_ref,
    q_pair_ref,
    prev_own_ref,
    prev_pair_ref,
    acc_ref,
    state_ref,
    o_ref,
    first_ref,
    lo_ref,
    hi_ref,
    even_ref,
    odd_ref,
):
    blk, x, slot = int_ref[0], int_ref[1], int_ref[2]

    @pl.when(slot < HEADS)
    def _():
        find_documents(blk, x, int_ref, first_ref, lo_ref, hi_ref)

        def begin_of(i):
            return jnp.where(blk > 0, jnp.clip(lo_ref[i] + TILES, 0, TILES), TILES)

        refs = (prev_own_ref, prev_pair_ref)
        key_rows = key_places(x)

        def score(s_ref, i, q, g, n, m, masked):
            kept = None
            if masked:
                kept = key_rows >= first_ref[i : i + 1, :] - ((g - TILES) * WIDE + n * SPAN)
            return scores_of(refs, s_ref, q, g, n, m, kept)

        def score_first(masked, g, m):
            for n in range(2):
                m = score(even_ref, 0, q, g, n, m, masked)
            return m

        def middle_of(i, begin):
            return jnp.clip(hi_ref[i] + TILES + 1, begin, TILES)

        none = jnp.full((8, TILE), NEG, jnp.float32)
        zeros = jnp.zeros((8, TILE), jnp.float32)
        buffers = (even_ref, odd_ref)
        q = load_queries(q_own_ref, q_pair_ref, 0)
        begin = begin_of(0)
        middle = middle_of(0, begin)
        m = lax.fori_loop(begin, middle, functools.partial(score_first, True), none)
        m = lax.fori_loop(middle, TILES, functools.partial(score_first, False), m)
        for i in range(TILES):
            s_ref, later_ref = buffers[i % 2], buffers[(i + 1) % 2]
            own_l, own_top = state_ref[i, 0:1, :], state_ref[i, 1:2, :]
            top = jnp.maximum(jnp.max(m, axis=0, keepdims=True), own_top)
            shift = shift_of(top)
            scale = jnp.where(own_top > 0.5 * NEG, jnp.exp2(own_top * C - shift), 0.0)
            begin = begin_of(i)
            sums = (zeros, acc_ref[i] * scale)
            if i + 1 < TILES:
                q = load_queries(q_own_ref, q_pair_ref, i + 1)

                def step(masked, g, carry, i=i, q=q, shift=shift, s_ref=s_ref, later_ref=later_ref):
                    m, l, acc = carry
                    for n in range(2):
                        l, acc = mix(refs, s_ref, g, n, shift, l, acc)
                        m = score(later_ref, i + 1, q, g, n, m, masked)
                    return m, l, acc

                middle = middle_of(i + 1, begin)
                carry = (none,) + sums
                carry = lax.fori_loop(begin, middle, functools.partial(step, True), carry)
                m, l, acc = lax.fori_loop(middle, TILES, functools.partial(step, False), carry)
            else:
                l, acc = lax.fori_loop(
                    begin,
                    TILES,
                    lambda g, c, s_ref=s_ref, shift=shift: mix_block(refs, s_ref, g, shift, *c),
                    sums,
                )
            l = jnp.sum(l, axis=0, keepdims=True) + own_l * scale
            some = l > 0.0
            l = jnp.where(some, l, 1.0)
            o = (acc * (1.0 / l)).astype(jnp.bfloat16)
            log = jnp.where(some, shift + jnp.log(l) * LOG2E, NEG)
            high = log.astype(jnp.bfloat16).astype(jnp.float32)
            middle = (log - high).astype(jnp.bfloat16).astype(jnp.float32)
            low = log - high - middle
            row = lax.broadcasted_iota(jnp.int32, (STATS, TILE), 0)
            stats = jnp.where(row == 0, high, jnp.where(row == 1, middle, low))
            stats = stats.astype(jnp.bfloat16)
            for n in range(4):
                part = slice(n * ROWS, (n + 1) * ROWS)
                y, to = 2 * i + (n & 1), (x & 1) ^ (n >> 1)
                o_ref[y, to, :ROWS, :] = o[:, part]
                o_ref[y, to, ROWS:, :] = stats[:, part]


SCRATCH = [
    pltpu.VMEM((8, TILE), jnp.int32),
    pltpu.SMEM((TILES,), jnp.int32),
    pltpu.SMEM((TILES,), jnp.int32),
    pltpu.VMEM((TILES, TILE, TILE), jnp.float32),
    pltpu.VMEM((TILES, TILE, TILE), jnp.float32),
]
SMEM = pl.BlockSpec(memory_space=pltpu.SMEM)
VMEM = pl.BlockSpec(memory_space=pltpu.VMEM)
ACC = (TILES, HEAD_DIM, TILE)


def attend_own(ints, q_own, q_pair, own, first_pair, second_pair):
    return pl.pallas_call(
        own_kernel,
        out_shape=(
            jax.ShapeDtypeStruct(ACC, jnp.float32),
            jax.ShapeDtypeStruct((TILES, 8, TILE), jnp.float32),
        ),
        in_specs=[SMEM] + [VMEM] * 5,
        out_specs=(VMEM, VMEM),
        scratch_shapes=SCRATCH + [pltpu.VMEM((Y, 2 * ROWS, HEAD_DIM), jnp.bfloat16)],
        compiler_params=pltpu.CompilerParams(vmem_limit_bytes=16 << 20),
        cost_estimate=pl.CostEstimate(
            flops=1 << 30, bytes_accessed=4 << 20, transcendentals=2 << 20
        ),
        name="attend_own",
    )(ints, q_own, q_pair, own, first_pair, second_pair)


def attend_prev(ints, q_own, q_pair, prev_own, prev_pair, acc, state):
    return pl.pallas_call(
        prev_kernel,
        out_shape=jax.ShapeDtypeStruct((Y, 2, ROWS + STATS, HEAD_DIM), jnp.bfloat16),
        in_specs=[SMEM] + [VMEM] * 6,
        out_specs=VMEM,
        scratch_shapes=SCRATCH,
        compiler_params=pltpu.CompilerParams(vmem_limit_bytes=16 << 20),
        cost_estimate=pl.CostEstimate(
            flops=1 << 29, bytes_accessed=4 << 20, transcendentals=1 << 20
        ),
        name="attend_prev",
    )(ints, q_own, q_pair, prev_own, prev_pair, acc, state)


def body(queries, keys, values, lengths):
    x = 2 * lax.axis_index("xh") + lax.axis_index("xl")
    place = jnp.stack([lax.axis_index("blk"), x, lax.axis_index("y")]).astype(jnp.int32)
    ints = jnp.concatenate([place, lengths])
    got = lax.all_to_all(pack(queries, keys, values), "y", 0, 0, tiled=True)
    own_queries, own = got[:, :ROWS], got[:, ROWS:]
    axes = ("blk", "xh", "xl")
    pair_queries = lax.ppermute(own_queries, "xl", QUERY_PAIRS)
    pair_first = lax.ppermute(own, axes, KEY_PAIRS[0])
    pair_second = lax.ppermute(own, axes, KEY_PAIRS[1])
    prev_own = lax.ppermute(own, "blk", [(0, 1)])
    pair_first, pair_queries, ints = lax.optimization_barrier((pair_first, pair_queries, ints))
    prev_pair = lax.ppermute(pair_first, "blk", [(0, 1)])
    state = attend_own(ints, own_queries, pair_queries, own, pair_first, pair_second)
    parts = attend_prev(ints, own_queries, pair_queries, prev_own, prev_pair, *state)
    parts = parts.reshape(2 * Y, ROWS + STATS, HEAD_DIM)
    parts = lax.all_to_all(parts, ("y", "xl"), 0, 0, tiled=True)
    return combine(parts.reshape(Y, 2, ROWS + STATS, HEAD_DIM))


def solution(mesh):
    devices = mesh.devices.reshape(2, Y, 2, 2, mesh.devices.shape[2])
    fine = Mesh(devices, ("blk", "y", "xh", "xl", "tp"))
    rows = P(("blk", "y", "xh", "xl"), "tp")
    return jax.shard_map(
        body, mesh=fine, in_specs=(rows, rows, rows, P()), out_specs=rows, check_vma=False
    )
```

```python
import functools
import math

import jax
import jax.numpy as jnp
from jax import lax
from jax.experimental import pallas as pl
from jax.experimental.pallas import tpu as pltpu
from jax.sharding import Mesh, PartitionSpec as P

HEAD_DIM = 128
ROWS = 128
X = 4
Y = 8
HEADS = 5
DOCS = 32
SPAN = X * ROWS
WIDE = 2 * SPAN
WIDE_SHIFT = 10
TILE = 4 * ROWS
HALF = TILE // 2
TILES = Y // 2
GROUP = Y * SPAN
STATS = 16
PLACE = 3
NEG = -1e30
LOG2E = math.log2(math.e)
C = LOG2E / math.sqrt(HEAD_DIM)
KEY_PAIRS = [(x, X - 1 - x) for x in range(X)]
QUERY_PAIRS = [(0, 1), (1, 0)]


def pack_kernel(q_ref, k_ref, v_ref, out_ref):
    for h in range(HEADS):
        cols = slice(h * HEAD_DIM, (h + 1) * HEAD_DIM)
        out_ref[h, :ROWS, :] = q_ref[:, cols].T
        out_ref[h, ROWS : 2 * ROWS, :] = k_ref[:, cols]
        out_ref[h, 2 * ROWS :, :] = v_ref[:, cols].T


def pack(q, k, v):
    return pl.pallas_call(
        pack_kernel,
        out_shape=jax.ShapeDtypeStruct((Y, 2 * ROWS + HEAD_DIM, HEAD_DIM), jnp.bfloat16),
        name="pack",
    )(q, k, v)


def combine_kernel(in_ref, out_ref):
    for h in range(HEADS):
        logs = []
        for n in range(2):
            terms = in_ref[n, h, ROWS:, :].astype(jnp.float32)
            logs.append(terms[0:1] + terms[1:2] + terms[2:3])
        top = jnp.maximum(logs[0], logs[1])
        a, b = jnp.exp2(logs[0] - top), jnp.exp2(logs[1] - top)
        o = in_ref[0, h, :ROWS, :].astype(jnp.float32) * (a / (a + b))
        o += in_ref[1, h, :ROWS, :].astype(jnp.float32) * (b / (a + b))
        out_ref[:, h * HEAD_DIM : (h + 1) * HEAD_DIM] = o.T.astype(jnp.bfloat16)


def combine(parts):
    shape = (2, HEADS, ROWS + STATS, HEAD_DIM)
    return pl.pallas_call(
        combine_kernel,
        grid=(1,),
        out_shape=jax.ShapeDtypeStruct((ROWS, HEADS * HEAD_DIM), jnp.bfloat16),
        in_specs=[pl.BlockSpec(shape, lambda i: (0, 0, 0, 0))],
        out_specs=pl.BlockSpec((ROWS, HEADS * HEAD_DIM), lambda i: (0, 0)),
        name="combine",
    )(parts)


def places(x, shape):
    n = lax.broadcasted_iota(jnp.int32, shape, 1)
    return (
        jnp.where(n < 2 * ROWS, x, x ^ 1) * ROWS
        + (lax.shift_right_logical(n, 7) & 1) * SPAN
        + (n & (ROWS - 1))
    )


def find_documents(blk, x, int_ref, first_ref, lo_ref, hi_ref):
    base = blk * GROUP
    pos = places(x, (8, TILE)) + lax.broadcasted_iota(jnp.int32, (8, TILE), 0) * WIDE
    lowest = jnp.minimum(x, x ^ 1) * ROWS
    highest = SPAN + jnp.maximum(x, x ^ 1) * ROWS + ROWS - 1
    start = -base
    first = jnp.zeros((8, TILE), jnp.int32) - base
    los = [start] * TILES
    his = [start] * TILES
    for j in range(DOCS - 1):
        start = start + int_ref[PLACE + j]
        first = jnp.where(pos >= start, start, first)
        los = [jnp.where(lowest + i * WIDE >= start, start, los[i]) for i in range(TILES)]
        his = [jnp.where(highest + i * WIDE >= start, start, his[i]) for i in range(TILES)]
    first_ref[...] = first
    for i in range(TILES):
        lo_ref[i] = lax.shift_right_arithmetic(los[i], WIDE_SHIFT)
        hi_ref[i] = lax.shift_right_arithmetic(his[i], WIDE_SHIFT)


def key_places(x):
    row = lax.broadcasted_iota(jnp.int32, (HALF, HALF), 0)
    return jnp.where(row < ROWS, x, X - 1 - x) * ROWS + (row & (ROWS - 1))


def load_queries(q_own_ref, q_pair_ref, i):
    return jnp.concatenate(
        [q_own_ref[2 * i], q_own_ref[2 * i + 1], q_pair_ref[2 * i], q_pair_ref[2 * i + 1]],
        axis=1,
    )


def piece(n):
    return slice(n * HALF, (n + 1) * HALF)


def scores_of(refs, s_ref, q, g, n, m, kept, c):
    k = jnp.concatenate([ref[2 * g + n, :ROWS, :] for ref in refs], axis=0)
    s = jnp.dot(k, q[:, piece(c)], preferred_element_type=jnp.float32)
    if kept is not None:
        s = jnp.where(kept, s, NEG)
    s_ref[g, piece(n), piece(c)] = s
    return jnp.maximum(m, jnp.max(s.reshape(HALF // 8, 8, HALF), axis=0))


def mix(refs, s_ref, g, n, c, shift, l, acc):
    p = jnp.exp2(s_ref[g, piece(n), piece(c)] * C - shift[:, piece(c)])
    l = l + jnp.sum(p.reshape(HALF // 8, 8, HALF), axis=0)
    vt = jnp.concatenate([ref[2 * g + n, ROWS:, :] for ref in refs], axis=1)
    acc = acc + jnp.dot(vt, p.astype(jnp.bfloat16), preferred_element_type=jnp.float32)
    return l, acc


def mix_block(refs, s_ref, g, shift, l, acc):
    l, acc = list(l), list(acc)
    for n in range(2):
        for c in range(2):
            l[c], acc[c] = mix(refs, s_ref, g, n, c, shift, l[c], acc[c])
    return tuple(l), tuple(acc)


def sums_and_scores(refs, s_ref, g, shift, score, m, l, acc):
    m, l, acc = list(m), list(l), list(acc)
    for n in range(2):
        for c in range(2):
            l[c], acc[c] = mix(refs, s_ref, g, n, c, shift, l[c], acc[c])
            m[c] = score(n, c, m[c])
    return tuple(m), tuple(l), tuple(acc)


def joined(parts):
    return jnp.concatenate(parts, axis=1)


def shift_of(top):
    return jnp.where(top > 0.5 * NEG, top * C, 0.0)


def own_kernel(
    int_ref,
    q_own_ref,
    q_pair_ref,
    own_ref,
    pair_ref,
    acc_ref,
    state_ref,
    first_ref,
    lo_ref,
    hi_ref,
    even_ref,
    odd_ref,
):
    blk, x, slot = int_ref[0], int_ref[1], int_ref[2]

    @pl.when(slot < HEADS)
    def _():
        find_documents(blk, x, int_ref, first_ref, lo_ref, hi_ref)

        refs = (own_ref, pair_ref)
        key_rows = key_places(x)

        def score(s_ref, i, q, g, masked, diagonal, n, c, m):
            kept = None
            if masked:
                kept = key_rows >= first_ref[i : i + 1, piece(c)] - (g * WIDE + n * SPAN)
                if diagonal:
                    kept &= key_rows <= places(x, (1, TILE))[:, piece(c)] - n * SPAN
            return scores_of(refs, s_ref, q, g, n, m, kept, c)

        def score_diagonal(s_ref, i, q, m):
            m = list(m)
            for n in range(2):
                for c in range(2):
                    m[c] = score(s_ref, i, q, i, True, True, n, c, m[c])
            return tuple(m)

        none = (jnp.full((8, HALF), NEG, jnp.float32),) * 2
        zeros = (jnp.zeros((8, HALF), jnp.float32),) * 2
        buffers = (even_ref, odd_ref)
        q = load_queries(q_own_ref, q_pair_ref, 0)
        m = score_diagonal(even_ref, 0, q, none)
        for i in range(TILES):
            s_ref, later_ref = buffers[i % 2], buffers[(i + 1) % 2]
            top = jnp.max(joined(m), axis=0, keepdims=True)
            shift = shift_of(top)
            begin = jnp.maximum(lo_ref[i], 0)
            sums = (zeros, (jnp.zeros((HEAD_DIM, HALF), jnp.float32),) * 2)
            if i + 1 < TILES:
                q = load_queries(q_own_ref, q_pair_ref, i + 1)

                def step(masked, g, carry, i=i, q=q, shift=shift, s_ref=s_ref, later_ref=later_ref):
                    later = functools.partial(score, later_ref, i + 1, q, g, masked, False)
                    return sums_and_scores(refs, s_ref, g, shift, later, *carry)

                carry = (none,) + sums
                if i > 0:
                    middle = jnp.clip(hi_ref[i + 1] + 1, begin, i)
                    carry = lax.fori_loop(begin, middle, functools.partial(step, True), carry)
                    carry = lax.fori_loop(middle, i, functools.partial(step, False), carry)
                m, l, acc = step(True, i, carry)
                m = score_diagonal(later_ref, i + 1, q, m)
            else:
                l, acc = lax.fori_loop(
                    begin,
                    i + 1,
                    lambda g, c, s_ref=s_ref, shift=shift: mix_block(refs, s_ref, g, shift, *c),
                    sums,
                )
            l = jnp.sum(joined(l), axis=0, keepdims=True)
            row = lax.broadcasted_iota(jnp.int32, (8, TILE), 0)
            acc_ref[i] = joined(acc)
            state_ref[i] = jnp.where(row == 0, l, top)


def prev_kernel(
    int_ref,
    q_own_ref,
    q_pair_ref,
    prev_own_ref,
    prev_pair_ref,
    acc_ref,
    state_ref,
    o_ref,
    first_ref,
    lo_ref,
    hi_ref,
    even_ref,
    odd_ref,
):
    blk, x, slot = int_ref[0], int_ref[1], int_ref[2]

    @pl.when(slot < HEADS)
    def _():
        @pl.when(blk > 0)
        def _():
            find_documents(blk, x, int_ref, first_ref, lo_ref, hi_ref)

        def begin_of(i):
            return jnp.where(blk > 0, jnp.clip(lo_ref[i] + TILES, 0, TILES), TILES)

        refs = (prev_own_ref, prev_pair_ref)
        key_rows = key_places(x)

        def score(s_ref, i, q, g, masked, n, c, m):
            kept = None
            if masked:
                start = first_ref[i : i + 1, piece(c)] - ((g - TILES) * WIDE + n * SPAN)
                kept = key_rows >= start
            return scores_of(refs, s_ref, q, g, n, m, kept, c)

        def score_first(masked, g, m):
            m = list(m)
            for n in range(2):
                for c in range(2):
                    m[c] = score(even_ref, 0, q, g, masked, n, c, m[c])
            return tuple(m)

        def middle_of(i, begin):
            return jnp.clip(hi_ref[i] + TILES + 1, begin, TILES)

        none = (jnp.full((8, HALF), NEG, jnp.float32),) * 2
        zeros = (jnp.zeros((8, HALF), jnp.float32),) * 2
        buffers = (even_ref, odd_ref)
        q = load_queries(q_own_ref, q_pair_ref, 0)
        begin = begin_of(0)
        middle = middle_of(0, begin)
        m = lax.fori_loop(begin, middle, functools.partial(score_first, True), none)
        m = lax.fori_loop(middle, TILES, functools.partial(score_first, False), m)
        for i in range(TILES):
            s_ref, later_ref = buffers[i % 2], buffers[(i + 1) % 2]
            own_l, own_top = state_ref[i, 0:1, :], state_ref[i, 1:2, :]
            top = jnp.maximum(jnp.max(joined(m), axis=0, keepdims=True), own_top)
            shift = shift_of(top)
            scale = jnp.where(own_top > 0.5 * NEG, jnp.exp2(own_top * C - shift), 0.0)
            begin = begin_of(i)
            scaled = acc_ref[i] * scale
            sums = (zeros, (scaled[:, piece(0)], scaled[:, piece(1)]))
            if i + 1 < TILES:
                q = load_queries(q_own_ref, q_pair_ref, i + 1)

                def step(masked, g, carry, i=i, q=q, shift=shift, s_ref=s_ref, later_ref=later_ref):
                    later = functools.partial(score, later_ref, i + 1, q, g, masked)
                    return sums_and_scores(refs, s_ref, g, shift, later, *carry)

                middle = middle_of(i + 1, begin)
                carry = (none,) + sums
                carry = lax.fori_loop(begin, middle, functools.partial(step, True), carry)
                m, l, acc = lax.fori_loop(middle, TILES, functools.partial(step, False), carry)
            else:
                l, acc = lax.fori_loop(
                    begin,
                    TILES,
                    lambda g, c, s_ref=s_ref, shift=shift: mix_block(refs, s_ref, g, shift, *c),
                    sums,
                )
            l = jnp.sum(joined(l), axis=0, keepdims=True) + own_l * scale
            some = l > 0.0
            l = jnp.where(some, l, 1.0)
            o = (joined(acc) * (1.0 / l)).astype(jnp.bfloat16)
            log = jnp.where(some, shift + jnp.log(l) * LOG2E, NEG)
            high = log.astype(jnp.bfloat16).astype(jnp.float32)
            middle = (log - high).astype(jnp.bfloat16).astype(jnp.float32)
            low = log - high - middle
            row = lax.broadcasted_iota(jnp.int32, (STATS, TILE), 0)
            stats = jnp.where(row == 0, high, jnp.where(row == 1, middle, low))
            stats = stats.astype(jnp.bfloat16)
            for n in range(4):
                part = slice(n * ROWS, (n + 1) * ROWS)
                y, to = 2 * i + (n & 1), (x & 1) ^ (n >> 1)
                o_ref[to, y, :ROWS, :] = o[:, part]
                o_ref[to, y, ROWS:, :] = stats[:, part]


SCRATCH = [
    pltpu.VMEM((8, TILE), jnp.int32),
    pltpu.SMEM((TILES,), jnp.int32),
    pltpu.SMEM((TILES,), jnp.int32),
    pltpu.VMEM((TILES, TILE, TILE), jnp.float32),
    pltpu.VMEM((TILES, TILE, TILE), jnp.float32),
]
SMEM = pl.BlockSpec(memory_space=pltpu.SMEM)
VMEM = pl.BlockSpec(memory_space=pltpu.VMEM)
ACC = (TILES, HEAD_DIM, TILE)


def attend_own(ints, q_own, q_pair, own, pair):
    return pl.pallas_call(
        own_kernel,
        out_shape=(
            jax.ShapeDtypeStruct(ACC, jnp.float32),
            jax.ShapeDtypeStruct((TILES, 8, TILE), jnp.float32),
        ),
        in_specs=[SMEM] + [VMEM] * 4,
        out_specs=(VMEM, VMEM),
        scratch_shapes=SCRATCH,
        compiler_params=pltpu.CompilerParams(vmem_limit_bytes=16 << 20),
        cost_estimate=pl.CostEstimate(
            flops=1 << 30, bytes_accessed=4 << 20, transcendentals=2 << 20
        ),
        name="attend_own",
    )(ints, q_own, q_pair, own, pair)


def attend_prev(ints, q_own, q_pair, prev_own, prev_pair, acc, state):
    return pl.pallas_call(
        prev_kernel,
        out_shape=jax.ShapeDtypeStruct((2, Y, ROWS + STATS, HEAD_DIM), jnp.bfloat16),
        in_specs=[SMEM] + [VMEM] * 6,
        out_specs=VMEM,
        scratch_shapes=SCRATCH,
        compiler_params=pltpu.CompilerParams(vmem_limit_bytes=16 << 20),
        cost_estimate=pl.CostEstimate(
            flops=1 << 29, bytes_accessed=4 << 20, transcendentals=1 << 20
        ),
        name="attend_prev",
    )(ints, q_own, q_pair, prev_own, prev_pair, acc, state)


def body(queries, keys, values, lengths):
    x = 2 * lax.axis_index("xh") + lax.axis_index("xl")
    place = jnp.stack([lax.axis_index("blk"), x, lax.axis_index("y")]).astype(jnp.int32)
    ints = jnp.concatenate([place, lengths])
    got = lax.all_to_all(pack(queries, keys, values), "y", 0, 0, tiled=True)
    own_queries, own = got[:, :ROWS], got[:, ROWS:]
    pair = lax.ppermute(own, ("xh", "xl"), KEY_PAIRS)
    pair_queries = lax.ppermute(own_queries, "xl", QUERY_PAIRS)
    prev_own = lax.ppermute(own, "blk", [(0, 1)])
    pair, pair_queries, ints = lax.optimization_barrier((pair, pair_queries, ints))
    prev_pair = lax.ppermute(pair, "blk", [(0, 1)])
    state = attend_own(ints, own_queries, pair_queries, own, pair)
    parts = attend_prev(ints, own_queries, pair_queries, prev_own, prev_pair, *state)
    parts = parts.reshape(2 * Y, ROWS + STATS, HEAD_DIM)
    parts = lax.all_to_all(parts, ("xl", "y"), 0, 0, tiled=True)
    return combine(parts.reshape(2, Y, ROWS + STATS, HEAD_DIM))


def solution(mesh):
    devices = mesh.devices.reshape(2, Y, 2, 2, mesh.devices.shape[2])
    fine = Mesh(devices, ("blk", "y", "xh", "xl", "tp"))
    rows = P(("blk", "y", "xh", "xl"), "tp")
    return jax.shard_map(
        body, mesh=fine, in_specs=(rows, rows, rows, P()), out_specs=rows, check_vma=False
    )
```

```python
import functools
import math

import jax
import jax.numpy as jnp
from jax import lax
from jax.experimental import pallas as pl
from jax.experimental.pallas import tpu as pltpu
from jax.sharding import Mesh, PartitionSpec as P

HEAD_DIM = 128
ROWS = 128
X = 4
Y = 8
HEADS = 5
DOCS = 32
SPAN = X * ROWS
WIDE = 2 * SPAN
WIDE_SHIFT = 10
TILE = 4 * ROWS
HALF = TILE // 2
TILES = Y // 2
GROUP = Y * SPAN
STATS = 16
PLACE = 3
NEG = -1e30
LOG2E = math.log2(math.e)
C = LOG2E / math.sqrt(HEAD_DIM)
KEY_PAIRS = [(x, X - 1 - x) for x in range(X)]
QUERY_PAIRS = [(0, 1), (1, 0)]


def pack_kernel(q_ref, k_ref, v_ref, out_ref):
    for h in range(HEADS):
        cols = slice(h * HEAD_DIM, (h + 1) * HEAD_DIM)
        out_ref[h, :ROWS, :] = q_ref[:, cols].T
        out_ref[h, ROWS : 2 * ROWS, :] = k_ref[:, cols]
        out_ref[h, 2 * ROWS :, :] = v_ref[:, cols].T


def pack(q, k, v):
    return pl.pallas_call(
        pack_kernel,
        out_shape=jax.ShapeDtypeStruct((Y, 2 * ROWS + HEAD_DIM, HEAD_DIM), jnp.bfloat16),
        name="pack",
    )(q, k, v)


def combine_kernel(in_ref, out_ref):
    for h in range(HEADS):
        logs = []
        for n in range(2):
            terms = in_ref[n, h, ROWS:, :].astype(jnp.float32)
            logs.append(terms[0:1] + terms[1:2] + terms[2:3])
        top = jnp.maximum(logs[0], logs[1])
        a, b = jnp.exp2(logs[0] - top), jnp.exp2(logs[1] - top)
        o = in_ref[0, h, :ROWS, :].astype(jnp.float32) * (a / (a + b))
        o += in_ref[1, h, :ROWS, :].astype(jnp.float32) * (b / (a + b))
        out_ref[:, h * HEAD_DIM : (h + 1) * HEAD_DIM] = o.T.astype(jnp.bfloat16)


def combine(parts):
    return pl.pallas_call(
        combine_kernel,
        out_shape=jax.ShapeDtypeStruct((ROWS, HEADS * HEAD_DIM), jnp.bfloat16),
        in_specs=[pl.BlockSpec(memory_space=pltpu.VMEM)],
        name="combine",
    )(parts)


def places(x, shape):
    n = lax.broadcasted_iota(jnp.int32, shape, 1)
    return (
        jnp.where(n < 2 * ROWS, x, x ^ 1) * ROWS
        + (lax.shift_right_logical(n, 7) & 1) * SPAN
        + (n & (ROWS - 1))
    )


def find_documents(blk, x, int_ref, first_ref, lo_ref, hi_ref):
    base = blk * GROUP
    pos = places(x, (8, TILE)) + lax.broadcasted_iota(jnp.int32, (8, TILE), 0) * WIDE
    lowest = jnp.minimum(x, x ^ 1) * ROWS
    highest = SPAN + jnp.maximum(x, x ^ 1) * ROWS + ROWS - 1
    start = -base
    first = jnp.zeros((8, TILE), jnp.int32) - base
    los = [start] * TILES
    his = [start] * TILES
    for j in range(DOCS - 1):
        start = start + int_ref[PLACE + j]
        first = jnp.where(pos >= start, start, first)
        los = [jnp.where(lowest + i * WIDE >= start, start, los[i]) for i in range(TILES)]
        his = [jnp.where(highest + i * WIDE >= start, start, his[i]) for i in range(TILES)]
    first_ref[...] = first
    for i in range(TILES):
        lo_ref[i] = lax.shift_right_arithmetic(los[i], WIDE_SHIFT)
        hi_ref[i] = lax.shift_right_arithmetic(his[i], WIDE_SHIFT)


def key_places(x):
    row = lax.broadcasted_iota(jnp.int32, (HALF, HALF), 0)
    return jnp.where(row < ROWS, x, X - 1 - x) * ROWS + (row & (ROWS - 1))


def load_queries(q_own_ref, q_pair_ref, i):
    return jnp.concatenate(
        [q_own_ref[2 * i], q_own_ref[2 * i + 1], q_pair_ref[2 * i], q_pair_ref[2 * i + 1]],
        axis=1,
    )


def piece(n):
    return slice(n * HALF, (n + 1) * HALF)


def scores_of(refs, s_ref, q, g, n, m, kept, c):
    k = jnp.concatenate([ref[2 * g + n, :ROWS, :] for ref in refs], axis=0)
    s = jnp.dot(k, q[:, piece(c)], preferred_element_type=jnp.float32)
    if kept is not None:
        s = jnp.where(kept, s, NEG)
    s_ref[g, piece(n), piece(c)] = s
    return jnp.maximum(m, jnp.max(s.reshape(HALF // 8, 8, HALF), axis=0))


def mix(refs, s_ref, g, n, c, shift, l, acc):
    p = jnp.exp2(s_ref[g, piece(n), piece(c)] * C - shift[:, piece(c)])
    l = l + jnp.sum(p.reshape(HALF // 8, 8, HALF), axis=0)
    vt = jnp.concatenate([ref[2 * g + n, ROWS:, :] for ref in refs], axis=1)
    acc = acc + jnp.dot(vt, p.astype(jnp.bfloat16), preferred_element_type=jnp.float32)
    return l, acc


def mix_block(refs, s_ref, g, shift, l, acc):
    l, acc = list(l), list(acc)
    for n in range(2):
        for c in range(2):
            l[c], acc[c] = mix(refs, s_ref, g, n, c, shift, l[c], acc[c])
    return tuple(l), tuple(acc)


def sums_and_scores(refs, s_ref, g, shift, score, m, l, acc):
    m, l, acc = list(m), list(l), list(acc)
    for n in range(2):
        for c in range(2):
            l[c], acc[c] = mix(refs, s_ref, g, n, c, shift, l[c], acc[c])
            m[c] = score(n, c, m[c])
    return tuple(m), tuple(l), tuple(acc)


def joined(parts):
    return jnp.concatenate(parts, axis=1)


def shift_of(top):
    return jnp.where(top > 0.5 * NEG, top * C, 0.0)


def own_kernel(
    int_ref,
    q_own_ref,
    q_pair_ref,
    own_ref,
    pair_ref,
    acc_ref,
    state_ref,
    first_ref,
    lo_ref,
    hi_ref,
    even_ref,
    odd_ref,
):
    blk, x, slot = int_ref[0], int_ref[1], int_ref[2]

    @pl.when(slot < HEADS)
    def _():
        find_documents(blk, x, int_ref, first_ref, lo_ref, hi_ref)

        refs = (own_ref, pair_ref)
        key_rows = key_places(x)

        def score(s_ref, i, q, g, masked, diagonal, n, c, m):
            kept = None
            if masked:
                kept = key_rows >= first_ref[i : i + 1, piece(c)] - (g * WIDE + n * SPAN)
                if diagonal:
                    kept &= key_rows <= places(x, (1, TILE))[:, piece(c)] - n * SPAN
            return scores_of(refs, s_ref, q, g, n, m, kept, c)

        def score_diagonal(s_ref, i, q, m):
            m = list(m)
            for n in range(2):
                for c in range(2):
                    m[c] = score(s_ref, i, q, i, True, True, n, c, m[c])
            return tuple(m)

        none = (jnp.full((8, HALF), NEG, jnp.float32),) * 2
        zeros = (jnp.zeros((8, HALF), jnp.float32),) * 2
        buffers = (even_ref, odd_ref)
        q = load_queries(q_own_ref, q_pair_ref, 0)
        m = score_diagonal(even_ref, 0, q, none)
        for i in range(TILES):
            s_ref, later_ref = buffers[i % 2], buffers[(i + 1) % 2]
            top = jnp.max(joined(m), axis=0, keepdims=True)
            shift = shift_of(top)
            begin = jnp.maximum(lo_ref[i], 0)
            sums = (zeros, (jnp.zeros((HEAD_DIM, HALF), jnp.float32),) * 2)
            if i + 1 < TILES:
                q = load_queries(q_own_ref, q_pair_ref, i + 1)

                def step(masked, g, carry, i=i, q=q, shift=shift, s_ref=s_ref, later_ref=later_ref):
                    later = functools.partial(score, later_ref, i + 1, q, g, masked, False)
                    return sums_and_scores(refs, s_ref, g, shift, later, *carry)

                carry = (none,) + sums
                if i > 0:
                    middle = jnp.clip(hi_ref[i + 1] + 1, begin, i)
                    carry = lax.fori_loop(begin, middle, functools.partial(step, True), carry)
                    carry = lax.fori_loop(middle, i, functools.partial(step, False), carry)
                m, l, acc = step(True, i, carry)
                m = score_diagonal(later_ref, i + 1, q, m)
            else:
                l, acc = lax.fori_loop(
                    begin,
                    i + 1,
                    lambda g, c, s_ref=s_ref, shift=shift: mix_block(refs, s_ref, g, shift, *c),
                    sums,
                )
            l = jnp.sum(joined(l), axis=0, keepdims=True)
            row = lax.broadcasted_iota(jnp.int32, (8, TILE), 0)
            acc_ref[i] = joined(acc)
            state_ref[i] = jnp.where(row == 0, l, top)


def prev_kernel(
    int_ref,
    q_own_ref,
    q_pair_ref,
    prev_own_ref,
    prev_pair_ref,
    acc_ref,
    state_ref,
    o_ref,
    first_ref,
    lo_ref,
    hi_ref,
    even_ref,
    odd_ref,
):
    blk, x, slot = int_ref[0], int_ref[1], int_ref[2]

    @pl.when(slot < HEADS)
    def _():
        @pl.when(blk > 0)
        def _():
            find_documents(blk, x, int_ref, first_ref, lo_ref, hi_ref)

        def begin_of(i):
            return jnp.where(blk > 0, jnp.clip(lo_ref[i] + TILES, 0, TILES), TILES)

        refs = (prev_own_ref, prev_pair_ref)
        key_rows = key_places(x)

        def score(s_ref, i, q, g, masked, n, c, m):
            kept = None
            if masked:
                start = first_ref[i : i + 1, piece(c)] - ((g - TILES) * WIDE + n * SPAN)
                kept = key_rows >= start
            return scores_of(refs, s_ref, q, g, n, m, kept, c)

        def score_first(masked, g, m):
            m = list(m)
            for n in range(2):
                for c in range(2):
                    m[c] = score(even_ref, 0, q, g, masked, n, c, m[c])
            return tuple(m)

        def middle_of(i, begin):
            return jnp.clip(hi_ref[i] + TILES + 1, begin, TILES)

        none = (jnp.full((8, HALF), NEG, jnp.float32),) * 2
        zeros = (jnp.zeros((8, HALF), jnp.float32),) * 2
        buffers = (even_ref, odd_ref)
        q = load_queries(q_own_ref, q_pair_ref, 0)
        begin = begin_of(0)
        middle = middle_of(0, begin)
        m = lax.fori_loop(begin, middle, functools.partial(score_first, True), none)
        m = lax.fori_loop(middle, TILES, functools.partial(score_first, False), m)
        for i in range(TILES):
            s_ref, later_ref = buffers[i % 2], buffers[(i + 1) % 2]
            own_l, own_top = state_ref[i, 0:1, :], state_ref[i, 1:2, :]
            top = jnp.maximum(jnp.max(joined(m), axis=0, keepdims=True), own_top)
            shift = shift_of(top)
            scale = jnp.where(own_top > 0.5 * NEG, jnp.exp2(own_top * C - shift), 0.0)
            begin = begin_of(i)
            scaled = acc_ref[i] * scale
            sums = (zeros, (scaled[:, piece(0)], scaled[:, piece(1)]))
            if i + 1 < TILES:
                q = load_queries(q_own_ref, q_pair_ref, i + 1)

                def step(masked, g, carry, i=i, q=q, shift=shift, s_ref=s_ref, later_ref=later_ref):
                    later = functools.partial(score, later_ref, i + 1, q, g, masked)
                    return sums_and_scores(refs, s_ref, g, shift, later, *carry)

                middle = middle_of(i + 1, begin)
                carry = (none,) + sums
                carry = lax.fori_loop(begin, middle, functools.partial(step, True), carry)
                m, l, acc = lax.fori_loop(middle, TILES, functools.partial(step, False), carry)
            else:
                l, acc = lax.fori_loop(
                    begin,
                    TILES,
                    lambda g, c, s_ref=s_ref, shift=shift: mix_block(refs, s_ref, g, shift, *c),
                    sums,
                )
            l = jnp.sum(joined(l), axis=0, keepdims=True) + own_l * scale
            some = l > 0.0
            l = jnp.where(some, l, 1.0)
            o = (joined(acc) * (1.0 / l)).astype(jnp.bfloat16)
            log = jnp.where(some, shift + jnp.log(l) * LOG2E, NEG)
            high = log.astype(jnp.bfloat16).astype(jnp.float32)
            middle = (log - high).astype(jnp.bfloat16).astype(jnp.float32)
            low = log - high - middle
            row = lax.broadcasted_iota(jnp.int32, (STATS, TILE), 0)
            stats = jnp.where(row == 0, high, jnp.where(row == 1, middle, low))
            stats = stats.astype(jnp.bfloat16)
            for n in range(4):
                part = slice(n * ROWS, (n + 1) * ROWS)
                y, to = 2 * i + (n & 1), (x & 1) ^ (n >> 1)
                o_ref[to, y, :ROWS, :] = o[:, part]
                o_ref[to, y, ROWS:, :] = stats[:, part]


SCRATCH = [
    pltpu.VMEM((8, TILE), jnp.int32),
    pltpu.SMEM((TILES,), jnp.int32),
    pltpu.SMEM((TILES,), jnp.int32),
    pltpu.VMEM((TILES, TILE, TILE), jnp.float32),
    pltpu.VMEM((TILES, TILE, TILE), jnp.float32),
]
SMEM = pl.BlockSpec(memory_space=pltpu.SMEM)
VMEM = pl.BlockSpec(memory_space=pltpu.VMEM)
ACC = (TILES, HEAD_DIM, TILE)


def attend_own(ints, q_own, q_pair, own, pair):
    return pl.pallas_call(
        own_kernel,
        out_shape=(
            jax.ShapeDtypeStruct(ACC, jnp.float32),
            jax.ShapeDtypeStruct((TILES, 8, TILE), jnp.float32),
        ),
        in_specs=[SMEM] + [VMEM] * 4,
        out_specs=(VMEM, VMEM),
        scratch_shapes=SCRATCH,
        compiler_params=pltpu.CompilerParams(vmem_limit_bytes=16 << 20),
        cost_estimate=pl.CostEstimate(
            flops=1 << 30, bytes_accessed=4 << 20, transcendentals=2 << 20
        ),
        name="attend_own",
    )(ints, q_own, q_pair, own, pair)


def attend_prev(ints, q_own, q_pair, prev_own, prev_pair, acc, state):
    return pl.pallas_call(
        prev_kernel,
        out_shape=jax.ShapeDtypeStruct((2, Y, ROWS + STATS, HEAD_DIM), jnp.bfloat16),
        in_specs=[SMEM] + [VMEM] * 6,
        scratch_shapes=SCRATCH,
        compiler_params=pltpu.CompilerParams(vmem_limit_bytes=16 << 20),
        cost_estimate=pl.CostEstimate(
            flops=1 << 29, bytes_accessed=4 << 20, transcendentals=1 << 20
        ),
        name="attend_prev",
    )(ints, q_own, q_pair, prev_own, prev_pair, acc, state)


def body(queries, keys, values, lengths):
    x = 2 * lax.axis_index("xh") + lax.axis_index("xl")
    place = jnp.stack([lax.axis_index("blk"), x, lax.axis_index("y")]).astype(jnp.int32)
    ints = jnp.concatenate([place, lengths])
    got = lax.all_to_all(pack(queries, keys, values), "y", 0, 0, tiled=True)
    own_queries, own = got[:, :ROWS], got[:, ROWS:]
    pair = lax.ppermute(own, ("xh", "xl"), KEY_PAIRS)
    pair_queries = lax.ppermute(own_queries, "xl", QUERY_PAIRS)
    prev_own = lax.ppermute(own, "blk", [(0, 1)])
    pair, pair_queries, ints = lax.optimization_barrier((pair, pair_queries, ints))
    prev_pair = lax.ppermute(pair, "blk", [(0, 1)])
    state = attend_own(ints, own_queries, pair_queries, own, pair)
    parts = attend_prev(ints, own_queries, pair_queries, prev_own, prev_pair, *state)
    parts = parts.reshape(2 * Y, ROWS + STATS, HEAD_DIM)
    parts = lax.all_to_all(parts, ("xl", "y"), 0, 0, tiled=True)
    return combine(parts.reshape(2, Y, ROWS + STATS, HEAD_DIM))


def solution(mesh):
    devices = mesh.devices.reshape(2, Y, 2, 2, mesh.devices.shape[2])
    fine = Mesh(devices, ("blk", "y", "xh", "xl", "tp"))
    rows = P(("blk", "y", "xh", "xl"), "tp")
    return jax.shard_map(
        body, mesh=fine, in_specs=(rows, rows, rows, P()), out_specs=rows, check_vma=False
    )
```

```python
import functools
import math

import jax
import jax.numpy as jnp
from jax import lax
from jax.experimental import pallas as pl
from jax.experimental.pallas import tpu as pltpu
from jax.sharding import Mesh, PartitionSpec as P

HEAD_DIM = 128
ROWS = 128
X = 4
Y = 8
HEADS = 5
DOCS = 32
SPAN = X * ROWS
WIDE = 2 * SPAN
WIDE_SHIFT = 10
TILE = 4 * ROWS
HALF = TILE // 2
TILES = Y // 2
GROUP = Y * SPAN
STATS = 16
PLACE = 3
NEG = -1e30
LOG2E = math.log2(math.e)
C = LOG2E / math.sqrt(HEAD_DIM)
KEY_PAIRS = [(x, X - 1 - x) for x in range(X)]
QUERY_PAIRS = [(0, 1), (1, 0)]


def head_columns(h):
    return pl.ds(h * HEAD_DIM, HEAD_DIM)


def pack_kernel(q_ref, k_ref, v_ref, out_ref, in_ref, turned_ref, in_sems, key_sems, out_sems):
    arrive = [
        pltpu.make_async_copy(ref, in_ref.at[n], in_sems.at[n])
        for n, ref in enumerate((q_ref, v_ref))
    ]
    for copy in arrive:
        copy.start()
    leave = [
        pltpu.make_async_copy(
            k_ref.at[:, head_columns(h)], out_ref.at[h, pl.ds(ROWS, ROWS)], key_sems.at[h]
        )
        for h in range(HEADS)
    ]
    for copy in leave:
        copy.start()
    for n in range(2):
        arrive[n].wait()
        for h in range(HEADS):
            turned_ref[n, h] = in_ref[n, :, h * HEAD_DIM : (h + 1) * HEAD_DIM].T
            copy = pltpu.make_async_copy(
                turned_ref.at[n, h],
                out_ref.at[h, pl.ds(2 * n * ROWS, ROWS)],
                out_sems.at[n, h],
            )
            copy.start()
            leave.append(copy)
    for copy in leave:
        copy.wait()


def pack(q, k, v):
    hbm = pl.BlockSpec(memory_space=pltpu.HBM)
    return pl.pallas_call(
        pack_kernel,
        out_shape=jax.ShapeDtypeStruct((Y, 2 * ROWS + HEAD_DIM, HEAD_DIM), jnp.bfloat16),
        in_specs=[hbm] * 3,
        out_specs=hbm,
        scratch_shapes=[
            pltpu.VMEM((2, ROWS, HEADS * HEAD_DIM), jnp.bfloat16),
            pltpu.VMEM((2, HEADS, ROWS, HEAD_DIM), jnp.bfloat16),
            pltpu.SemaphoreType.DMA((2,)),
            pltpu.SemaphoreType.DMA((HEADS,)),
            pltpu.SemaphoreType.DMA((2, HEADS)),
        ],
        name="pack",
    )(q, k, v)


def combine_kernel(in_ref, out_ref, parts_ref, sums_ref, in_sems, out_sems):
    arrive = [
        [
            pltpu.make_async_copy(in_ref.at[n, h], parts_ref.at[n, h], in_sems.at[n, h])
            for n in range(2)
        ]
        for h in range(HEADS)
    ]
    for pair in arrive:
        for copy in pair:
            copy.start()
    leave = []
    for h in range(HEADS):
        logs = []
        for n in range(2):
            arrive[h][n].wait()
            terms = parts_ref[n, h, ROWS:, :].astype(jnp.float32)
            logs.append(terms[0:1] + terms[1:2] + terms[2:3])
        top = jnp.maximum(logs[0], logs[1])
        a, b = jnp.exp2(logs[0] - top), jnp.exp2(logs[1] - top)
        o = parts_ref[0, h, :ROWS, :].astype(jnp.float32) * (a / (a + b))
        o += parts_ref[1, h, :ROWS, :].astype(jnp.float32) * (b / (a + b))
        sums_ref[h] = o.T.astype(jnp.bfloat16)
        copy = pltpu.make_async_copy(
            sums_ref.at[h], out_ref.at[:, head_columns(h)], out_sems.at[h]
        )
        copy.start()
        leave.append(copy)
    for copy in leave:
        copy.wait()


def combine(parts):
    hbm = pl.BlockSpec(memory_space=pltpu.HBM)
    return pl.pallas_call(
        combine_kernel,
        out_shape=jax.ShapeDtypeStruct((ROWS, HEADS * HEAD_DIM), jnp.bfloat16),
        in_specs=[hbm],
        out_specs=hbm,
        scratch_shapes=[
            pltpu.VMEM((2, HEADS, ROWS + STATS, HEAD_DIM), jnp.bfloat16),
            pltpu.VMEM((HEADS, ROWS, HEAD_DIM), jnp.bfloat16),
            pltpu.SemaphoreType.DMA((2, HEADS)),
            pltpu.SemaphoreType.DMA((HEADS,)),
        ],
        name="combine",
    )(parts)


def places(x, shape):
    n = lax.broadcasted_iota(jnp.int32, shape, 1)
    return (
        jnp.where(n < 2 * ROWS, x, x ^ 1) * ROWS
        + (lax.shift_right_logical(n, 7) & 1) * SPAN
        + (n & (ROWS - 1))
    )


def find_documents(blk, x, int_ref, first_ref, lo_ref, hi_ref):
    base = blk * GROUP
    pos = places(x, (8, TILE)) + lax.broadcasted_iota(jnp.int32, (8, TILE), 0) * WIDE
    lowest = jnp.minimum(x, x ^ 1) * ROWS
    highest = SPAN + jnp.maximum(x, x ^ 1) * ROWS + ROWS - 1
    start = -base
    first = jnp.zeros((8, TILE), jnp.int32) - base
    los = [start] * TILES
    his = [start] * TILES
    for j in range(DOCS - 1):
        start = start + int_ref[PLACE + j]
        first = jnp.where(pos >= start, start, first)
        los = [jnp.where(lowest + i * WIDE >= start, start, los[i]) for i in range(TILES)]
        his = [jnp.where(highest + i * WIDE >= start, start, his[i]) for i in range(TILES)]
    first_ref[...] = first
    for i in range(TILES):
        lo_ref[i] = lax.shift_right_arithmetic(los[i], WIDE_SHIFT)
        hi_ref[i] = lax.shift_right_arithmetic(his[i], WIDE_SHIFT)


def key_places(x):
    row = lax.broadcasted_iota(jnp.int32, (HALF, HALF), 0)
    return jnp.where(row < ROWS, x, X - 1 - x) * ROWS + (row & (ROWS - 1))


def load_queries(q_own_ref, q_pair_ref, i):
    return jnp.concatenate(
        [q_own_ref[2 * i], q_own_ref[2 * i + 1], q_pair_ref[2 * i], q_pair_ref[2 * i + 1]],
        axis=1,
    )


def piece(n):
    return slice(n * HALF, (n + 1) * HALF)


def scores_of(refs, s_ref, q, g, n, m, kept, c):
    k = jnp.concatenate([ref[2 * g + n, :ROWS, :] for ref in refs], axis=0)
    s = jnp.dot(k, q[:, piece(c)], preferred_element_type=jnp.float32)
    if kept is not None:
        s = jnp.where(kept, s, NEG)
    s_ref[g, piece(n), piece(c)] = s
    return jnp.maximum(m, jnp.max(s.reshape(HALF // 8, 8, HALF), axis=0))


def mix(refs, s_ref, g, n, c, shift, l, acc):
    p = jnp.exp2(s_ref[g, piece(n), piece(c)] * C - shift[:, piece(c)])
    l = l + jnp.sum(p.reshape(HALF // 8, 8, HALF), axis=0)
    vt = jnp.concatenate([ref[2 * g + n, ROWS:, :] for ref in refs], axis=1)
    acc = acc + jnp.dot(vt, p.astype(jnp.bfloat16), preferred_element_type=jnp.float32)
    return l, acc


def mix_block(refs, s_ref, g, shift, l, acc):
    l, acc = list(l), list(acc)
    for n in range(2):
        for c in range(2):
            l[c], acc[c] = mix(refs, s_ref, g, n, c, shift, l[c], acc[c])
    return tuple(l), tuple(acc)


def sums_and_scores(refs, s_ref, g, shift, score, m, l, acc):
    m, l, acc = list(m), list(l), list(acc)
    for n in range(2):
        for c in range(2):
            l[c], acc[c] = mix(refs, s_ref, g, n, c, shift, l[c], acc[c])
            m[c] = score(n, c, m[c])
    return tuple(m), tuple(l), tuple(acc)


def joined(parts):
    return jnp.concatenate(parts, axis=1)


def shift_of(top):
    return jnp.where(top > 0.5 * NEG, top * C, 0.0)


def own_kernel(
    int_ref,
    q_own_ref,
    q_pair_ref,
    own_ref,
    pair_ref,
    acc_ref,
    state_ref,
    first_ref,
    lo_ref,
    hi_ref,
    even_ref,
    odd_ref,
):
    blk, x, slot = int_ref[0], int_ref[1], int_ref[2]

    @pl.when(slot < HEADS)
    def _():
        find_documents(blk, x, int_ref, first_ref, lo_ref, hi_ref)

        refs = (own_ref, pair_ref)
        key_rows = key_places(x)

        def score(s_ref, i, q, g, masked, diagonal, n, c, m):
            kept = None
            if masked:
                kept = key_rows >= first_ref[i : i + 1, piece(c)] - (g * WIDE + n * SPAN)
                if diagonal:
                    kept &= key_rows <= places(x, (1, TILE))[:, piece(c)] - n * SPAN
            return scores_of(refs, s_ref, q, g, n, m, kept, c)

        def score_diagonal(s_ref, i, q, m):
            m = list(m)
            for n in range(2):
                for c in range(2):
                    m[c] = score(s_ref, i, q, i, True, True, n, c, m[c])
            return tuple(m)

        none = (jnp.full((8, HALF), NEG, jnp.float32),) * 2
        zeros = (jnp.zeros((8, HALF), jnp.float32),) * 2
        buffers = (even_ref, odd_ref)
        q = load_queries(q_own_ref, q_pair_ref, 0)
        m = score_diagonal(even_ref, 0, q, none)
        for i in range(TILES):
            s_ref, later_ref = buffers[i % 2], buffers[(i + 1) % 2]
            top = jnp.max(joined(m), axis=0, keepdims=True)
            shift = shift_of(top)
            begin = jnp.maximum(lo_ref[i], 0)
            sums = (zeros, (jnp.zeros((HEAD_DIM, HALF), jnp.float32),) * 2)
            if i + 1 < TILES:
                q = load_queries(q_own_ref, q_pair_ref, i + 1)

                def step(masked, g, carry, i=i, q=q, shift=shift, s_ref=s_ref, later_ref=later_ref):
                    later = functools.partial(score, later_ref, i + 1, q, g, masked, False)
                    return sums_and_scores(refs, s_ref, g, shift, later, *carry)

                carry = (none,) + sums
                if i > 0:
                    middle = jnp.clip(hi_ref[i + 1] + 1, begin, i)
                    carry = lax.fori_loop(begin, middle, functools.partial(step, True), carry)
                    carry = lax.fori_loop(middle, i, functools.partial(step, False), carry)
                m, l, acc = step(True, i, carry)
                m = score_diagonal(later_ref, i + 1, q, m)
            else:
                l, acc = lax.fori_loop(
                    begin,
                    i + 1,
                    lambda g, c, s_ref=s_ref, shift=shift: mix_block(refs, s_ref, g, shift, *c),
                    sums,
                )
            l = jnp.sum(joined(l), axis=0, keepdims=True)
            row = lax.broadcasted_iota(jnp.int32, (8, TILE), 0)
            acc_ref[i] = joined(acc)
            state_ref[i] = jnp.where(row == 0, l, top)


def prev_kernel(
    int_ref,
    q_own_ref,
    q_pair_ref,
    prev_own_ref,
    prev_pair_ref,
    acc_ref,
    state_ref,
    o_ref,
    first_ref,
    lo_ref,
    hi_ref,
    even_ref,
    odd_ref,
):
    blk, x, slot = int_ref[0], int_ref[1], int_ref[2]

    @pl.when(slot < HEADS)
    def _():
        @pl.when(blk > 0)
        def _():
            find_documents(blk, x, int_ref, first_ref, lo_ref, hi_ref)

        def begin_of(i):
            return jnp.where(blk > 0, jnp.clip(lo_ref[i] + TILES, 0, TILES), TILES)

        refs = (prev_own_ref, prev_pair_ref)
        key_rows = key_places(x)

        def score(s_ref, i, q, g, masked, n, c, m):
            kept = None
            if masked:
                start = first_ref[i : i + 1, piece(c)] - ((g - TILES) * WIDE + n * SPAN)
                kept = key_rows >= start
            return scores_of(refs, s_ref, q, g, n, m, kept, c)

        def score_first(masked, g, m):
            m = list(m)
            for n in range(2):
                for c in range(2):
                    m[c] = score(even_ref, 0, q, g, masked, n, c, m[c])
            return tuple(m)

        def middle_of(i, begin):
            return jnp.clip(hi_ref[i] + TILES + 1, begin, TILES)

        none = (jnp.full((8, HALF), NEG, jnp.float32),) * 2
        zeros = (jnp.zeros((8, HALF), jnp.float32),) * 2
        buffers = (even_ref, odd_ref)
        q = load_queries(q_own_ref, q_pair_ref, 0)
        begin = begin_of(0)
        middle = middle_of(0, begin)
        m = lax.fori_loop(begin, middle, functools.partial(score_first, True), none)
        m = lax.fori_loop(middle, TILES, functools.partial(score_first, False), m)
        for i in range(TILES):
            s_ref, later_ref = buffers[i % 2], buffers[(i + 1) % 2]
            own_l, own_top = state_ref[i, 0:1, :], state_ref[i, 1:2, :]
            top = jnp.maximum(jnp.max(joined(m), axis=0, keepdims=True), own_top)
            shift = shift_of(top)
            scale = jnp.where(own_top > 0.5 * NEG, jnp.exp2(own_top * C - shift), 0.0)
            begin = begin_of(i)
            scaled = acc_ref[i] * scale
            sums = (zeros, (scaled[:, piece(0)], scaled[:, piece(1)]))
            if i + 1 < TILES:
                q = load_queries(q_own_ref, q_pair_ref, i + 1)

                def step(masked, g, carry, i=i, q=q, shift=shift, s_ref=s_ref, later_ref=later_ref):
                    later = functools.partial(score, later_ref, i + 1, q, g, masked)
                    return sums_and_scores(refs, s_ref, g, shift, later, *carry)

                middle = middle_of(i + 1, begin)
                carry = (none,) + sums
                carry = lax.fori_loop(begin, middle, functools.partial(step, True), carry)
                m, l, acc = lax.fori_loop(middle, TILES, functools.partial(step, False), carry)
            else:
                l, acc = lax.fori_loop(
                    begin,
                    TILES,
                    lambda g, c, s_ref=s_ref, shift=shift: mix_block(refs, s_ref, g, shift, *c),
                    sums,
                )
            l = jnp.sum(joined(l), axis=0, keepdims=True) + own_l * scale
            some = l > 0.0
            l = jnp.where(some, l, 1.0)
            o = (joined(acc) * (1.0 / l)).astype(jnp.bfloat16)
            log = jnp.where(some, shift + jnp.log(l) * LOG2E, NEG)
            high = log.astype(jnp.bfloat16).astype(jnp.float32)
            middle = (log - high).astype(jnp.bfloat16).astype(jnp.float32)
            low = log - high - middle
            row = lax.broadcasted_iota(jnp.int32, (STATS, TILE), 0)
            stats = jnp.where(row == 0, high, jnp.where(row == 1, middle, low))
            stats = stats.astype(jnp.bfloat16)
            for n in range(4):
                part = slice(n * ROWS, (n + 1) * ROWS)
                y, to = 2 * i + (n & 1), (x & 1) ^ (n >> 1)
                o_ref[to, y, :ROWS, :] = o[:, part]
                o_ref[to, y, ROWS:, :] = stats[:, part]


SCRATCH = [
    pltpu.VMEM((8, TILE), jnp.int32),
    pltpu.SMEM((TILES,), jnp.int32),
    pltpu.SMEM((TILES,), jnp.int32),
    pltpu.VMEM((TILES, TILE, TILE), jnp.float32),
    pltpu.VMEM((TILES, TILE, TILE), jnp.float32),
]
SMEM = pl.BlockSpec(memory_space=pltpu.SMEM)
VMEM = pl.BlockSpec(memory_space=pltpu.VMEM)
ACC = (TILES, HEAD_DIM, TILE)


def attend_own(ints, q_own, q_pair, own, pair):
    return pl.pallas_call(
        own_kernel,
        out_shape=(
            jax.ShapeDtypeStruct(ACC, jnp.float32),
            jax.ShapeDtypeStruct((TILES, 8, TILE), jnp.float32),
        ),
        in_specs=[SMEM] + [VMEM] * 4,
        out_specs=(VMEM, VMEM),
        scratch_shapes=SCRATCH,
        compiler_params=pltpu.CompilerParams(vmem_limit_bytes=16 << 20),
        cost_estimate=pl.CostEstimate(
            flops=1 << 30, bytes_accessed=4 << 20, transcendentals=2 << 20
        ),
        name="attend_own",
    )(ints, q_own, q_pair, own, pair)


def attend_prev(ints, q_own, q_pair, prev_own, prev_pair, acc, state):
    return pl.pallas_call(
        prev_kernel,
        out_shape=jax.ShapeDtypeStruct((2, Y, ROWS + STATS, HEAD_DIM), jnp.bfloat16),
        in_specs=[SMEM] + [VMEM] * 6,
        out_specs=VMEM,
        scratch_shapes=SCRATCH,
        compiler_params=pltpu.CompilerParams(vmem_limit_bytes=16 << 20),
        cost_estimate=pl.CostEstimate(
            flops=1 << 29, bytes_accessed=4 << 20, transcendentals=1 << 20
        ),
        name="attend_prev",
    )(ints, q_own, q_pair, prev_own, prev_pair, acc, state)


def body(queries, keys, values, lengths):
    x = 2 * lax.axis_index("xh") + lax.axis_index("xl")
    place = jnp.stack([lax.axis_index("blk"), x, lax.axis_index("y")]).astype(jnp.int32)
    ints = jnp.concatenate([place, lengths])
    got = lax.all_to_all(pack(queries, keys, values), "y", 0, 0, tiled=True)
    own_queries, own = got[:, :ROWS], got[:, ROWS:]
    pair = lax.ppermute(own, ("xh", "xl"), KEY_PAIRS)
    pair_queries = lax.ppermute(own_queries, "xl", QUERY_PAIRS)
    prev_own = lax.ppermute(own, "blk", [(0, 1)])
    pair, pair_queries, ints = lax.optimization_barrier((pair, pair_queries, ints))
    prev_pair = lax.ppermute(pair, "blk", [(0, 1)])
    state = attend_own(ints, own_queries, pair_queries, own, pair)
    parts = attend_prev(ints, own_queries, pair_queries, prev_own, prev_pair, *state)
    parts = parts.reshape(2 * Y, ROWS + STATS, HEAD_DIM)
    parts = lax.all_to_all(parts, ("xl", "y"), 0, 0, tiled=True)
    return combine(parts.reshape(2, Y, ROWS + STATS, HEAD_DIM))


def solution(mesh):
    devices = mesh.devices.reshape(2, Y, 2, 2, mesh.devices.shape[2])
    fine = Mesh(devices, ("blk", "y", "xh", "xl", "tp"))
    rows = P(("blk", "y", "xh", "xl"), "tp")
    return jax.shard_map(
        body, mesh=fine, in_specs=(rows, rows, rows, P()), out_specs=rows, check_vma=False
    )
```

```python
import functools
import math

import jax
import jax.numpy as jnp
from jax import lax
from jax.experimental import pallas as pl
from jax.experimental.pallas import tpu as pltpu
from jax.sharding import PartitionSpec as P

HEAD_DIM = 128
ROWS = 128
X = 4
Y = 8
HEADS = 5
DOCS = 32
SPAN = X * ROWS
WIDE = 2 * SPAN
WIDE_SHIFT = 10
TILE = 4 * ROWS
HALF = TILE // 2
TILES = Y // 2
GROUP = Y * SPAN
STATS = 16
PLACE = 3
NEG = -1e30
LOG2E = math.log2(math.e)
C = LOG2E / math.sqrt(HEAD_DIM)
CHIPS = X * Y
KEY_PAIRS = [(n, n ^ 1) for n in range(CHIPS)]
QUERY_PAIRS = [(n, n ^ 3) for n in range(CHIPS)]
COLUMNS = [[y * X + x for y in range(Y)] for x in range(X)]
COLUMN_PAIRS = [COLUMNS[x] + COLUMNS[X - 1 - x] for x in range(X // 2)]


def pack_kernel(q_ref, k_ref, v_ref, out_ref):
    for h in range(HEADS):
        cols = slice(h * HEAD_DIM, (h + 1) * HEAD_DIM)
        out_ref[h, :ROWS, :] = q_ref[:, cols].T
        out_ref[h, ROWS : 2 * ROWS, :] = k_ref[:, cols]
        out_ref[h, 2 * ROWS :, :] = v_ref[:, cols].T


def pack(q, k, v):
    return pl.pallas_call(
        pack_kernel,
        out_shape=jax.ShapeDtypeStruct((Y, 2 * ROWS + HEAD_DIM, HEAD_DIM), jnp.bfloat16),
        name="pack",
    )(q, k, v)


def combine_kernel(in_ref, out_ref):
    for h in range(HEADS):
        logs = []
        for n in range(2):
            terms = in_ref[n, h, ROWS:, :].astype(jnp.float32)
            logs.append(terms[0:1] + terms[1:2] + terms[2:3])
        top = jnp.maximum(logs[0], logs[1])
        a, b = jnp.exp2(logs[0] - top), jnp.exp2(logs[1] - top)
        o = in_ref[0, h, :ROWS, :].astype(jnp.float32) * (a / (a + b))
        o += in_ref[1, h, :ROWS, :].astype(jnp.float32) * (b / (a + b))
        out_ref[:, h * HEAD_DIM : (h + 1) * HEAD_DIM] = o.T.astype(jnp.bfloat16)


def combine(parts):
    shape = (2, HEADS, ROWS + STATS, HEAD_DIM)
    return pl.pallas_call(
        combine_kernel,
        grid=(1,),
        out_shape=jax.ShapeDtypeStruct((ROWS, HEADS * HEAD_DIM), jnp.bfloat16),
        in_specs=[pl.BlockSpec(shape, lambda i: (0, 0, 0, 0))],
        out_specs=pl.BlockSpec((ROWS, HEADS * HEAD_DIM), lambda i: (0, 0)),
        name="combine",
    )(parts)


def places(x, shape):
    n = lax.broadcasted_iota(jnp.int32, shape, 1)
    return (
        jnp.where(n < 2 * ROWS, x, X - 1 - x) * ROWS
        + (lax.shift_right_logical(n, 7) & 1) * SPAN
        + (n & (ROWS - 1))
    )


def find_documents(blk, x, int_ref, first_ref, lo_ref, hi_ref):
    base = blk * GROUP
    pos = places(x, (8, TILE)) + lax.broadcasted_iota(jnp.int32, (8, TILE), 0) * WIDE
    lowest = jnp.minimum(x, X - 1 - x) * ROWS
    highest = SPAN + jnp.maximum(x, X - 1 - x) * ROWS + ROWS - 1
    start = -base
    first = jnp.zeros((8, TILE), jnp.int32) - base
    los = [start] * TILES
    his = [start] * TILES
    for j in range(DOCS - 1):
        start = start + int_ref[PLACE + j]
        first = jnp.where(pos >= start, start, first)
        los = [jnp.where(lowest + i * WIDE >= start, start, los[i]) for i in range(TILES)]
        his = [jnp.where(highest + i * WIDE >= start, start, his[i]) for i in range(TILES)]
    first_ref[...] = first
    for i in range(TILES):
        lo_ref[i] = lax.shift_right_arithmetic(los[i], WIDE_SHIFT)
        hi_ref[i] = lax.shift_right_arithmetic(his[i], WIDE_SHIFT)


def key_places(x):
    row = lax.broadcasted_iota(jnp.int32, (HALF, HALF), 0)
    return jnp.where(row < ROWS, x, x ^ 1) * ROWS + (row & (ROWS - 1))


def load_queries(q_own_ref, q_pair_ref, i):
    return jnp.concatenate(
        [q_own_ref[2 * i], q_own_ref[2 * i + 1], q_pair_ref[2 * i], q_pair_ref[2 * i + 1]],
        axis=1,
    )


def piece(n):
    return slice(n * HALF, (n + 1) * HALF)


def scores_of(refs, s_ref, q, g, n, m, kept, c):
    k = jnp.concatenate([ref[2 * g + n, :ROWS, :] for ref in refs], axis=0)
    s = jnp.dot(k, q[:, piece(c)], preferred_element_type=jnp.float32)
    if kept is not None:
        s = jnp.where(kept, s, NEG)
    s_ref[g, piece(n), piece(c)] = s
    return jnp.maximum(m, jnp.max(s.reshape(HALF // 8, 8, HALF), axis=0))


def mix(refs, s_ref, g, n, c, shift, l, acc):
    p = jnp.exp2(s_ref[g, piece(n), piece(c)] * C - shift[:, piece(c)])
    l = l + jnp.sum(p.reshape(HALF // 8, 8, HALF), axis=0)
    vt = jnp.concatenate([ref[2 * g + n, ROWS:, :] for ref in refs], axis=1)
    acc = acc + jnp.dot(vt, p.astype(jnp.bfloat16), preferred_element_type=jnp.float32)
    return l, acc


def mix_block(refs, s_ref, g, shift, l, acc):
    l, acc = list(l), list(acc)
    for n in range(2):
        for c in range(2):
            l[c], acc[c] = mix(refs, s_ref, g, n, c, shift, l[c], acc[c])
    return tuple(l), tuple(acc)


def sums_and_scores(refs, s_ref, g, shift, score, m, l, acc):
    m, l, acc = list(m), list(l), list(acc)
    for n in range(2):
        for c in range(2):
            l[c], acc[c] = mix(refs, s_ref, g, n, c, shift, l[c], acc[c])
            m[c] = score(n, c, m[c])
    return tuple(m), tuple(l), tuple(acc)


def joined(parts):
    return jnp.concatenate(parts, axis=1)


def shift_of(top):
    return jnp.where(top > 0.5 * NEG, top * C, 0.0)


def own_kernel(
    int_ref,
    q_own_ref,
    q_pair_ref,
    own_ref,
    pair_ref,
    acc_ref,
    state_ref,
    first_ref,
    lo_ref,
    hi_ref,
    even_ref,
    odd_ref,
):
    blk, x, slot = int_ref[0], int_ref[1], int_ref[2]

    @pl.when(slot < HEADS)
    def _():
        find_documents(blk, x, int_ref, first_ref, lo_ref, hi_ref)

        refs = (own_ref, pair_ref)
        key_rows = key_places(x)

        def score(s_ref, i, q, g, masked, diagonal, n, c, m):
            kept = None
            if masked:
                kept = key_rows >= first_ref[i : i + 1, piece(c)] - (g * WIDE + n * SPAN)
                if diagonal:
                    kept &= key_rows <= places(x, (1, TILE))[:, piece(c)] - n * SPAN
            return scores_of(refs, s_ref, q, g, n, m, kept, c)

        def score_diagonal(s_ref, i, q, m):
            m = list(m)
            for n in range(2):
                for c in range(2):
                    m[c] = score(s_ref, i, q, i, True, True, n, c, m[c])
            return tuple(m)

        none = (jnp.full((8, HALF), NEG, jnp.float32),) * 2
        zeros = (jnp.zeros((8, HALF), jnp.float32),) * 2
        buffers = (even_ref, odd_ref)
        q = load_queries(q_own_ref, q_pair_ref, 0)
        m = score_diagonal(even_ref, 0, q, none)
        for i in range(TILES):
            s_ref, later_ref = buffers[i % 2], buffers[(i + 1) % 2]
            top = jnp.max(joined(m), axis=0, keepdims=True)
            shift = shift_of(top)
            begin = jnp.maximum(lo_ref[i], 0)
            sums = (zeros, (jnp.zeros((HEAD_DIM, HALF), jnp.float32),) * 2)
            if i + 1 < TILES:
                q = load_queries(q_own_ref, q_pair_ref, i + 1)

                def step(masked, g, carry, i=i, q=q, shift=shift, s_ref=s_ref, later_ref=later_ref):
                    later = functools.partial(score, later_ref, i + 1, q, g, masked, False)
                    return sums_and_scores(refs, s_ref, g, shift, later, *carry)

                carry = (none,) + sums
                if i > 0:
                    middle = jnp.clip(hi_ref[i + 1] + 1, begin, i)
                    carry = lax.fori_loop(begin, middle, functools.partial(step, True), carry)
                    carry = lax.fori_loop(middle, i, functools.partial(step, False), carry)
                m, l, acc = step(True, i, carry)
                m = score_diagonal(later_ref, i + 1, q, m)
            else:
                l, acc = lax.fori_loop(
                    begin,
                    i + 1,
                    lambda g, c, s_ref=s_ref, shift=shift: mix_block(refs, s_ref, g, shift, *c),
                    sums,
                )
            l = jnp.sum(joined(l), axis=0, keepdims=True)
            row = lax.broadcasted_iota(jnp.int32, (8, TILE), 0)
            acc_ref[i] = joined(acc)
            state_ref[i] = jnp.where(row == 0, l, top)


def prev_kernel(
    int_ref,
    q_own_ref,
    q_pair_ref,
    prev_own_ref,
    prev_pair_ref,
    acc_ref,
    state_ref,
    o_ref,
    first_ref,
    lo_ref,
    hi_ref,
    even_ref,
    odd_ref,
):
    blk, x, slot = int_ref[0], int_ref[1], int_ref[2]

    @pl.when(slot < HEADS)
    def _():
        @pl.when(blk > 0)
        def _():
            find_documents(blk, x, int_ref, first_ref, lo_ref, hi_ref)

        def begin_of(i):
            return jnp.where(blk > 0, jnp.clip(lo_ref[i] + TILES, 0, TILES), TILES)

        refs = (prev_own_ref, prev_pair_ref)
        key_rows = key_places(x)

        def score(s_ref, i, q, g, masked, n, c, m):
            kept = None
            if masked:
                start = first_ref[i : i + 1, piece(c)] - ((g - TILES) * WIDE + n * SPAN)
                kept = key_rows >= start
            return scores_of(refs, s_ref, q, g, n, m, kept, c)

        def score_first(masked, g, m):
            m = list(m)
            for n in range(2):
                for c in range(2):
                    m[c] = score(even_ref, 0, q, g, masked, n, c, m[c])
            return tuple(m)

        def middle_of(i, begin):
            return jnp.clip(hi_ref[i] + TILES + 1, begin, TILES)

        none = (jnp.full((8, HALF), NEG, jnp.float32),) * 2
        zeros = (jnp.zeros((8, HALF), jnp.float32),) * 2
        buffers = (even_ref, odd_ref)
        q = load_queries(q_own_ref, q_pair_ref, 0)
        begin = begin_of(0)
        middle = middle_of(0, begin)
        m = lax.fori_loop(begin, middle, functools.partial(score_first, True), none)
        m = lax.fori_loop(middle, TILES, functools.partial(score_first, False), m)
        for i in range(TILES):
            s_ref, later_ref = buffers[i % 2], buffers[(i + 1) % 2]
            own_l, own_top = state_ref[i, 0:1, :], state_ref[i, 1:2, :]
            top = jnp.maximum(jnp.max(joined(m), axis=0, keepdims=True), own_top)
            shift = shift_of(top)
            scale = jnp.where(own_top > 0.5 * NEG, jnp.exp2(own_top * C - shift), 0.0)
            begin = begin_of(i)
            scaled = acc_ref[i] * scale
            sums = (zeros, (scaled[:, piece(0)], scaled[:, piece(1)]))
            if i + 1 < TILES:
                q = load_queries(q_own_ref, q_pair_ref, i + 1)

                def step(masked, g, carry, i=i, q=q, shift=shift, s_ref=s_ref, later_ref=later_ref):
                    later = functools.partial(score, later_ref, i + 1, q, g, masked)
                    return sums_and_scores(refs, s_ref, g, shift, later, *carry)

                middle = middle_of(i + 1, begin)
                carry = (none,) + sums
                carry = lax.fori_loop(begin, middle, functools.partial(step, True), carry)
                m, l, acc = lax.fori_loop(middle, TILES, functools.partial(step, False), carry)
            else:
                l, acc = lax.fori_loop(
                    begin,
                    TILES,
                    lambda g, c, s_ref=s_ref, shift=shift: mix_block(refs, s_ref, g, shift, *c),
                    sums,
                )
            l = jnp.sum(joined(l), axis=0, keepdims=True) + own_l * scale
            some = l > 0.0
            l = jnp.where(some, l, 1.0)
            o = (joined(acc) * (1.0 / l)).astype(jnp.bfloat16)
            log = jnp.where(some, shift + jnp.log(l) * LOG2E, NEG)
            high = log.astype(jnp.bfloat16).astype(jnp.float32)
            middle = (log - high).astype(jnp.bfloat16).astype(jnp.float32)
            low = log - high - middle
            row = lax.broadcasted_iota(jnp.int32, (STATS, TILE), 0)
            stats = jnp.where(row == 0, high, jnp.where(row == 1, middle, low))
            stats = stats.astype(jnp.bfloat16)
            for n in range(4):
                part = slice(n * ROWS, (n + 1) * ROWS)
                y, to = 2 * i + (n & 1), lax.shift_right_logical(x, 1) ^ (n >> 1)
                o_ref[to, y, :ROWS, :] = o[:, part]
                o_ref[to, y, ROWS:, :] = stats[:, part]


SCRATCH = [
    pltpu.VMEM((8, TILE), jnp.int32),
    pltpu.SMEM((TILES,), jnp.int32),
    pltpu.SMEM((TILES,), jnp.int32),
    pltpu.VMEM((TILES, TILE, TILE), jnp.float32),
    pltpu.VMEM((TILES, TILE, TILE), jnp.float32),
]
SMEM = pl.BlockSpec(memory_space=pltpu.SMEM)
VMEM = pl.BlockSpec(memory_space=pltpu.VMEM)
ACC = (TILES, HEAD_DIM, TILE)


def attend_own(ints, q_own, q_pair, own, pair):
    return pl.pallas_call(
        own_kernel,
        out_shape=(
            jax.ShapeDtypeStruct(ACC, jnp.float32),
            jax.ShapeDtypeStruct((TILES, 8, TILE), jnp.float32),
        ),
        in_specs=[SMEM] + [VMEM] * 4,
        out_specs=(VMEM, VMEM),
        scratch_shapes=SCRATCH,
        compiler_params=pltpu.CompilerParams(vmem_limit_bytes=16 << 20),
        cost_estimate=pl.CostEstimate(
            flops=1 << 30, bytes_accessed=4 << 20, transcendentals=2 << 20
        ),
        name="attend_own",
    )(ints, q_own, q_pair, own, pair)


def attend_prev(ints, q_own, q_pair, prev_own, prev_pair, acc, state):
    return pl.pallas_call(
        prev_kernel,
        out_shape=jax.ShapeDtypeStruct((2, Y, ROWS + STATS, HEAD_DIM), jnp.bfloat16),
        in_specs=[SMEM] + [VMEM] * 6,
        out_specs=VMEM,
        scratch_shapes=SCRATCH,
        compiler_params=pltpu.CompilerParams(vmem_limit_bytes=16 << 20),
        cost_estimate=pl.CostEstimate(
            flops=1 << 29, bytes_accessed=4 << 20, transcendentals=1 << 20
        ),
        name="attend_prev",
    )(ints, q_own, q_pair, prev_own, prev_pair, acc, state)


def body(queries, keys, values, lengths):
    chip = lax.axis_index("ctx")
    place = jnp.stack([lax.axis_index("blk"), chip % X, chip // X]).astype(jnp.int32)
    ints = jnp.concatenate([place, lengths])
    packed = pack(queries, keys, values)
    got = lax.all_to_all(packed, "ctx", 0, 0, tiled=True, axis_index_groups=COLUMNS)
    own_queries, own = got[:, :ROWS], got[:, ROWS:]
    pair = lax.ppermute(own, "ctx", KEY_PAIRS)
    pair_queries = lax.ppermute(own_queries, "ctx", QUERY_PAIRS)
    prev_own = lax.ppermute(own, "blk", [(0, 1)])
    pair, pair_queries, ints = lax.optimization_barrier((pair, pair_queries, ints))
    prev_pair = lax.ppermute(pair, "blk", [(0, 1)])
    state = attend_own(ints, own_queries, pair_queries, own, pair)
    parts = attend_prev(ints, own_queries, pair_queries, prev_own, prev_pair, *state)
    parts = parts.reshape(2 * Y, ROWS + STATS, HEAD_DIM)
    parts = lax.all_to_all(parts, "ctx", 0, 0, tiled=True, axis_index_groups=COLUMN_PAIRS)
    return combine(parts.reshape(2, Y, ROWS + STATS, HEAD_DIM))


def solution(mesh):
    rows = P(("blk", "ctx"), "tp")
    return jax.shard_map(
        body, mesh=mesh, in_specs=(rows, rows, rows, P()), out_specs=rows, check_vma=False
    )
```

```python
import functools
import math

import jax
import jax.numpy as jnp
from jax import lax
from jax.experimental import pallas as pl
from jax.experimental.pallas import tpu as pltpu
from jax.sharding import Mesh, PartitionSpec as P

HEAD_DIM = 128
ROWS = 128
X = 4
Y = 8
HEADS = 5
DOCS = 32
SPAN = X * ROWS
WIDE = 2 * SPAN
WIDE_SHIFT = 10
TILE = 4 * ROWS
HALF = TILE // 2
TILES = Y // 2
GROUP = Y * SPAN
STATS = 16
PLACE = 6
NEG = -1e30
LOG2E = math.log2(math.e)
C = LOG2E / math.sqrt(HEAD_DIM)
CHIPS = X * Y
KEY_PAIRS = [(n, n ^ (1 if n >= CHIPS else 3)) for n in range(2 * CHIPS)]
QUERY_PAIRS = [(n, n ^ (3 if n >= CHIPS else 1)) for n in range(2 * CHIPS)]
PREV_OWN = [(n, CHIPS + n) for n in range(CHIPS)]
PREV_PAIR = [(n, CHIPS + (n ^ 1)) for n in range(CHIPS)]
COLUMNS = [[g * CHIPS + y * X + x for y in range(Y)] for g in range(2) for x in range(X)]
COLUMN_PAIRS = [COLUMNS[a] + COLUMNS[b] for a, b in ((0, 1), (2, 3), (4, 7), (5, 6))]


def pack_kernel(q_ref, k_ref, v_ref, out_ref):
    for h in range(HEADS):
        cols = slice(h * HEAD_DIM, (h + 1) * HEAD_DIM)
        out_ref[h, :ROWS, :] = q_ref[:, cols].T
        out_ref[h, ROWS : 2 * ROWS, :] = k_ref[:, cols]
        out_ref[h, 2 * ROWS :, :] = v_ref[:, cols].T


def pack(q, k, v):
    return pl.pallas_call(
        pack_kernel,
        out_shape=jax.ShapeDtypeStruct((Y, 2 * ROWS + HEAD_DIM, HEAD_DIM), jnp.bfloat16),
        name="pack",
    )(q, k, v)


def combine_kernel(in_ref, out_ref):
    for h in range(HEADS):
        logs = []
        for n in range(2):
            terms = in_ref[n, h, ROWS:, :].astype(jnp.float32)
            logs.append(terms[0:1] + terms[1:2] + terms[2:3])
        top = jnp.maximum(logs[0], logs[1])
        a, b = jnp.exp2(logs[0] - top), jnp.exp2(logs[1] - top)
        o = in_ref[0, h, :ROWS, :].astype(jnp.float32) * (a / (a + b))
        o += in_ref[1, h, :ROWS, :].astype(jnp.float32) * (b / (a + b))
        out_ref[:, h * HEAD_DIM : (h + 1) * HEAD_DIM] = o.T.astype(jnp.bfloat16)


def combine(parts):
    shape = (2, HEADS, ROWS + STATS, HEAD_DIM)
    return pl.pallas_call(
        combine_kernel,
        grid=(1,),
        out_shape=jax.ShapeDtypeStruct((ROWS, HEADS * HEAD_DIM), jnp.bfloat16),
        in_specs=[pl.BlockSpec(shape, lambda i: (0, 0, 0, 0))],
        out_specs=pl.BlockSpec((ROWS, HEADS * HEAD_DIM), lambda i: (0, 0)),
        name="combine",
    )(parts)


def places(x, pair_x, shape):
    n = lax.broadcasted_iota(jnp.int32, shape, 1)
    return (
        jnp.where(n < 2 * ROWS, x, pair_x) * ROWS
        + (lax.shift_right_logical(n, 7) & 1) * SPAN
        + (n & (ROWS - 1))
    )


def find_documents(int_ref, first_ref, lo_ref, hi_ref):
    x, pair_x = int_ref[1], int_ref[3]
    base = int_ref[0] * GROUP
    pos = places(x, pair_x, (8, TILE)) + lax.broadcasted_iota(jnp.int32, (8, TILE), 0) * WIDE
    lowest = jnp.minimum(x, pair_x) * ROWS
    highest = SPAN + jnp.maximum(x, pair_x) * ROWS + ROWS - 1
    start = -base
    first = jnp.zeros((8, TILE), jnp.int32) - base
    los = [start] * TILES
    his = [start] * TILES
    for j in range(DOCS - 1):
        start = start + int_ref[PLACE + j]
        first = jnp.where(pos >= start, start, first)
        los = [jnp.where(lowest + i * WIDE >= start, start, los[i]) for i in range(TILES)]
        his = [jnp.where(highest + i * WIDE >= start, start, his[i]) for i in range(TILES)]
    first_ref[...] = first
    for i in range(TILES):
        lo_ref[i] = lax.shift_right_arithmetic(los[i], WIDE_SHIFT)
        hi_ref[i] = lax.shift_right_arithmetic(his[i], WIDE_SHIFT)


def key_places(x, pair_x):
    row = lax.broadcasted_iota(jnp.int32, (HALF, HALF), 0)
    return jnp.where(row < ROWS, x, pair_x) * ROWS + (row & (ROWS - 1))


def load_queries(q_own_ref, q_pair_ref, i):
    return jnp.concatenate(
        [q_own_ref[2 * i], q_own_ref[2 * i + 1], q_pair_ref[2 * i], q_pair_ref[2 * i + 1]],
        axis=1,
    )


def piece(n):
    return slice(n * HALF, (n + 1) * HALF)


def scores_of(refs, s_ref, q, g, n, m, kept, c):
    k = jnp.concatenate([ref[2 * g + n, :ROWS, :] for ref in refs], axis=0)
    s = jnp.dot(k, q[:, piece(c)], preferred_element_type=jnp.float32)
    if kept is not None:
        s = jnp.where(kept, s, NEG)
    s_ref[g, piece(n), piece(c)] = s
    return jnp.maximum(m, jnp.max(s.reshape(HALF // 8, 8, HALF), axis=0))


def mix(refs, s_ref, g, n, c, shift, l, acc):
    p = jnp.exp2(s_ref[g, piece(n), piece(c)] * C - shift[:, piece(c)])
    l = l + jnp.sum(p.reshape(HALF // 8, 8, HALF), axis=0)
    vt = jnp.concatenate([ref[2 * g + n, ROWS:, :] for ref in refs], axis=1)
    acc = acc + jnp.dot(vt, p.astype(jnp.bfloat16), preferred_element_type=jnp.float32)
    return l, acc


def mix_block(refs, s_ref, g, shift, l, acc):
    l, acc = list(l), list(acc)
    for n in range(2):
        for c in range(2):
            l[c], acc[c] = mix(refs, s_ref, g, n, c, shift, l[c], acc[c])
    return tuple(l), tuple(acc)


def sums_and_scores(refs, s_ref, g, shift, score, m, l, acc):
    m, l, acc = list(m), list(l), list(acc)
    for n in range(2):
        for c in range(2):
            l[c], acc[c] = mix(refs, s_ref, g, n, c, shift, l[c], acc[c])
            m[c] = score(n, c, m[c])
    return tuple(m), tuple(l), tuple(acc)


def joined(parts):
    return jnp.concatenate(parts, axis=1)


def shift_of(top):
    return jnp.where(top > 0.5 * NEG, top * C, 0.0)


def own_kernel(
    int_ref,
    q_own_ref,
    q_pair_ref,
    own_ref,
    pair_ref,
    acc_ref,
    state_ref,
    first_ref,
    lo_ref,
    hi_ref,
    even_ref,
    odd_ref,
):
    blk, x, slot = int_ref[0], int_ref[1], int_ref[2]

    @pl.when(slot < HEADS)
    def _():
        find_documents(int_ref, first_ref, lo_ref, hi_ref)

        refs = (own_ref, pair_ref)
        key_rows = key_places(x, int_ref[4])

        def score(s_ref, i, q, g, masked, diagonal, n, c, m):
            kept = None
            if masked:
                kept = key_rows >= first_ref[i : i + 1, piece(c)] - (g * WIDE + n * SPAN)
                if diagonal:
                    kept &= key_rows <= places(x, int_ref[3], (1, TILE))[:, piece(c)] - n * SPAN
            return scores_of(refs, s_ref, q, g, n, m, kept, c)

        def score_diagonal(s_ref, i, q, m):
            m = list(m)
            for n in range(2):
                for c in range(2):
                    m[c] = score(s_ref, i, q, i, True, True, n, c, m[c])
            return tuple(m)

        none = (jnp.full((8, HALF), NEG, jnp.float32),) * 2
        zeros = (jnp.zeros((8, HALF), jnp.float32),) * 2
        buffers = (even_ref, odd_ref)
        q = load_queries(q_own_ref, q_pair_ref, 0)
        m = score_diagonal(even_ref, 0, q, none)
        for i in range(TILES):
            s_ref, later_ref = buffers[i % 2], buffers[(i + 1) % 2]
            top = jnp.max(joined(m), axis=0, keepdims=True)
            shift = shift_of(top)
            begin = jnp.maximum(lo_ref[i], 0)
            sums = (zeros, (jnp.zeros((HEAD_DIM, HALF), jnp.float32),) * 2)
            if i + 1 < TILES:
                q = load_queries(q_own_ref, q_pair_ref, i + 1)

                def step(masked, g, carry, i=i, q=q, shift=shift, s_ref=s_ref, later_ref=later_ref):
                    later = functools.partial(score, later_ref, i + 1, q, g, masked, False)
                    return sums_and_scores(refs, s_ref, g, shift, later, *carry)

                carry = (none,) + sums
                if i > 0:
                    middle = jnp.clip(hi_ref[i + 1] + 1, begin, i)
                    carry = lax.fori_loop(begin, middle, functools.partial(step, True), carry)
                    carry = lax.fori_loop(middle, i, functools.partial(step, False), carry)
                m, l, acc = step(True, i, carry)
                m = score_diagonal(later_ref, i + 1, q, m)
            else:
                l, acc = lax.fori_loop(
                    begin,
                    i + 1,
                    lambda g, c, s_ref=s_ref, shift=shift: mix_block(refs, s_ref, g, shift, *c),
                    sums,
                )
            l = jnp.sum(joined(l), axis=0, keepdims=True)
            row = lax.broadcasted_iota(jnp.int32, (8, TILE), 0)
            acc_ref[i] = joined(acc)
            state_ref[i] = jnp.where(row == 0, l, top)


def prev_kernel(
    int_ref,
    q_own_ref,
    q_pair_ref,
    prev_own_ref,
    prev_pair_ref,
    acc_ref,
    state_ref,
    o_ref,
    first_ref,
    lo_ref,
    hi_ref,
    even_ref,
    odd_ref,
):
    blk, x, slot = int_ref[0], int_ref[1], int_ref[2]

    @pl.when(slot < HEADS)
    def _():
        @pl.when(blk > 0)
        def _():
            find_documents(int_ref, first_ref, lo_ref, hi_ref)

        def begin_of(i):
            return jnp.where(blk > 0, jnp.clip(lo_ref[i] + TILES, 0, TILES), TILES)

        refs = (prev_own_ref, prev_pair_ref)
        key_rows = key_places(x, int_ref[4])

        def score(s_ref, i, q, g, masked, n, c, m):
            kept = None
            if masked:
                start = first_ref[i : i + 1, piece(c)] - ((g - TILES) * WIDE + n * SPAN)
                kept = key_rows >= start
            return scores_of(refs, s_ref, q, g, n, m, kept, c)

        def score_first(masked, g, m):
            m = list(m)
            for n in range(2):
                for c in range(2):
                    m[c] = score(even_ref, 0, q, g, masked, n, c, m[c])
            return tuple(m)

        def middle_of(i, begin):
            return jnp.clip(hi_ref[i] + TILES + 1, begin, TILES)

        none = (jnp.full((8, HALF), NEG, jnp.float32),) * 2
        zeros = (jnp.zeros((8, HALF), jnp.float32),) * 2
        buffers = (even_ref, odd_ref)
        q = load_queries(q_own_ref, q_pair_ref, 0)
        begin = begin_of(0)
        middle = middle_of(0, begin)
        m = lax.fori_loop(begin, middle, functools.partial(score_first, True), none)
        m = lax.fori_loop(middle, TILES, functools.partial(score_first, False), m)
        for i in range(TILES):
            s_ref, later_ref = buffers[i % 2], buffers[(i + 1) % 2]
            own_l, own_top = state_ref[i, 0:1, :], state_ref[i, 1:2, :]
            top = jnp.maximum(jnp.max(joined(m), axis=0, keepdims=True), own_top)
            shift = shift_of(top)
            scale = jnp.where(own_top > 0.5 * NEG, jnp.exp2(own_top * C - shift), 0.0)
            begin = begin_of(i)
            scaled = acc_ref[i] * scale
            sums = (zeros, (scaled[:, piece(0)], scaled[:, piece(1)]))
            if i + 1 < TILES:
                q = load_queries(q_own_ref, q_pair_ref, i + 1)

                def step(masked, g, carry, i=i, q=q, shift=shift, s_ref=s_ref, later_ref=later_ref):
                    later = functools.partial(score, later_ref, i + 1, q, g, masked)
                    return sums_and_scores(refs, s_ref, g, shift, later, *carry)

                middle = middle_of(i + 1, begin)
                carry = (none,) + sums
                carry = lax.fori_loop(begin, middle, functools.partial(step, True), carry)
                m, l, acc = lax.fori_loop(middle, TILES, functools.partial(step, False), carry)
            else:
                l, acc = lax.fori_loop(
                    begin,
                    TILES,
                    lambda g, c, s_ref=s_ref, shift=shift: mix_block(refs, s_ref, g, shift, *c),
                    sums,
                )
            l = jnp.sum(joined(l), axis=0, keepdims=True) + own_l * scale
            some = l > 0.0
            l = jnp.where(some, l, 1.0)
            o = (joined(acc) * (1.0 / l)).astype(jnp.bfloat16)
            log = jnp.where(some, shift + jnp.log(l) * LOG2E, NEG)
            high = log.astype(jnp.bfloat16).astype(jnp.float32)
            middle = (log - high).astype(jnp.bfloat16).astype(jnp.float32)
            low = log - high - middle
            row = lax.broadcasted_iota(jnp.int32, (STATS, TILE), 0)
            stats = jnp.where(row == 0, high, jnp.where(row == 1, middle, low))
            stats = stats.astype(jnp.bfloat16)
            for n in range(4):
                part = slice(n * ROWS, (n + 1) * ROWS)
                y, to = 2 * i + (n & 1), int_ref[5] ^ (n >> 1)
                o_ref[to, y, :ROWS, :] = o[:, part]
                o_ref[to, y, ROWS:, :] = stats[:, part]


SCRATCH = [
    pltpu.VMEM((8, TILE), jnp.int32),
    pltpu.SMEM((TILES,), jnp.int32),
    pltpu.SMEM((TILES,), jnp.int32),
    pltpu.VMEM((TILES, TILE, TILE), jnp.float32),
    pltpu.VMEM((TILES, TILE, TILE), jnp.float32),
]
SMEM = pl.BlockSpec(memory_space=pltpu.SMEM)
VMEM = pl.BlockSpec(memory_space=pltpu.VMEM)
ACC = (TILES, HEAD_DIM, TILE)


def attend_own(ints, q_own, q_pair, own, pair):
    return pl.pallas_call(
        own_kernel,
        out_shape=(
            jax.ShapeDtypeStruct(ACC, jnp.float32),
            jax.ShapeDtypeStruct((TILES, 8, TILE), jnp.float32),
        ),
        in_specs=[SMEM] + [VMEM] * 4,
        out_specs=(VMEM, VMEM),
        scratch_shapes=SCRATCH,
        compiler_params=pltpu.CompilerParams(vmem_limit_bytes=16 << 20),
        cost_estimate=pl.CostEstimate(
            flops=1 << 30, bytes_accessed=4 << 20, transcendentals=2 << 20
        ),
        name="attend_own",
    )(ints, q_own, q_pair, own, pair)


def attend_prev(ints, q_own, q_pair, prev_own, prev_pair, acc, state):
    return pl.pallas_call(
        prev_kernel,
        out_shape=jax.ShapeDtypeStruct((2, Y, ROWS + STATS, HEAD_DIM), jnp.bfloat16),
        in_specs=[SMEM] + [VMEM] * 6,
        out_specs=VMEM,
        scratch_shapes=SCRATCH,
        compiler_params=pltpu.CompilerParams(vmem_limit_bytes=16 << 20),
        cost_estimate=pl.CostEstimate(
            flops=1 << 29, bytes_accessed=4 << 20, transcendentals=1 << 20
        ),
        name="attend_prev",
    )(ints, q_own, q_pair, prev_own, prev_pair, acc, state)


def body(queries, keys, values, lengths):
    chip = lax.axis_index("tokens")
    blk, x, y = chip // CHIPS, chip % X, chip // X % Y
    first = blk == 0
    pairs = [jnp.where(first, x ^ 1, x ^ 3), jnp.where(first, x ^ 3, x ^ 1)]
    place = jnp.stack([blk, x, y, *pairs, jnp.where(first, x & 1, x // 2)]).astype(jnp.int32)
    ints = jnp.concatenate([place, lengths])
    packed = pack(queries, keys, values)
    got = lax.all_to_all(packed, "tokens", 0, 0, tiled=True, axis_index_groups=COLUMNS)
    own_queries, own = got[:, :ROWS], got[:, ROWS:]
    pair = lax.ppermute(own, "tokens", KEY_PAIRS)
    pair_queries = lax.ppermute(own_queries, "tokens", QUERY_PAIRS)
    prev_own = lax.ppermute(own, "tokens", PREV_OWN)
    later, pair_queries, ints = lax.optimization_barrier((own, pair_queries, ints))
    prev_pair = lax.ppermute(later, "tokens", PREV_PAIR)
    state = attend_own(ints, own_queries, pair_queries, own, pair)
    parts = attend_prev(ints, own_queries, pair_queries, prev_own, prev_pair, *state)
    parts = parts.reshape(2 * Y, ROWS + STATS, HEAD_DIM)
    parts = lax.all_to_all(parts, "tokens", 0, 0, tiled=True, axis_index_groups=COLUMN_PAIRS)
    return combine(parts.reshape(2, Y, ROWS + STATS, HEAD_DIM))


def solution(mesh):
    devices = mesh.devices.reshape(2 * CHIPS, mesh.devices.shape[2])
    rows = P("tokens", "tp")
    return jax.shard_map(
        body,
        mesh=Mesh(devices, ("tokens", "tp")),
        in_specs=(rows, rows, rows, P()),
        out_specs=rows,
        check_vma=False,
    )
```

```python
import functools
import math

import jax
import jax.numpy as jnp
from jax import lax
from jax.experimental import pallas as pl
from jax.experimental.pallas import tpu as pltpu
from jax.sharding import Mesh, PartitionSpec as P

HEAD_DIM = 128
ROWS = 128
X = 4
Y = 8
HEADS = 5
DOCS = 32
SPAN = X * ROWS
WIDE = 2 * SPAN
WIDE_SHIFT = 10
TILE = 4 * ROWS
HALF = TILE // 2
TILES = Y // 2
GROUP = Y * SPAN
STATS = 16
PLACE = 6
NEG = -1e30
LOG2E = math.log2(math.e)
C = LOG2E / math.sqrt(HEAD_DIM)
CHIPS = X * Y
KEY_PAIRS = [(n, n ^ (1 if n >= CHIPS else 3)) for n in range(2 * CHIPS)]
QUERY_PAIRS = [(n, n ^ (3 if n >= CHIPS else 1)) for n in range(2 * CHIPS)]
PREV_OWN = [(n, CHIPS + n) for n in range(CHIPS)]
PREV_PAIR = [(n, CHIPS + (n ^ 1)) for n in range(CHIPS)]
COLUMNS = [[g * CHIPS + y * X + x for y in range(Y)] for g in range(2) for x in range(X)]
COLUMN_PAIRS = [COLUMNS[a] + COLUMNS[b] for a, b in ((0, 1), (2, 3), (4, 7), (5, 6))]


def pack_kernel(q_ref, k_ref, v_ref, out_ref):
    for h in range(HEADS):
        cols = slice(h * HEAD_DIM, (h + 1) * HEAD_DIM)
        out_ref[h, :ROWS, :] = q_ref[:, cols].T
        out_ref[h, ROWS : 2 * ROWS, :] = k_ref[:, cols]
        out_ref[h, 2 * ROWS :, :] = v_ref[:, cols].T


def pack(q, k, v):
    return pl.pallas_call(
        pack_kernel,
        out_shape=jax.ShapeDtypeStruct((Y, 2 * ROWS + HEAD_DIM, HEAD_DIM), jnp.bfloat16),
        name="pack",
    )(q, k, v)


def combine_kernel(in_ref, out_ref):
    for h in range(HEADS):
        logs = []
        for n in range(2):
            terms = in_ref[n, h, ROWS:, :].astype(jnp.float32)
            logs.append(terms[0:1] + terms[1:2] + terms[2:3])
        top = jnp.maximum(logs[0], logs[1])
        a, b = jnp.exp2(logs[0] - top), jnp.exp2(logs[1] - top)
        o = in_ref[0, h, :ROWS, :].astype(jnp.float32) * (a / (a + b))
        o += in_ref[1, h, :ROWS, :].astype(jnp.float32) * (b / (a + b))
        out_ref[:, h * HEAD_DIM : (h + 1) * HEAD_DIM] = o.T.astype(jnp.bfloat16)


def combine(parts):
    shape = (2, HEADS, ROWS + STATS, HEAD_DIM)
    return pl.pallas_call(
        combine_kernel,
        grid=(1,),
        out_shape=jax.ShapeDtypeStruct((ROWS, HEADS * HEAD_DIM), jnp.bfloat16),
        in_specs=[pl.BlockSpec(shape, lambda i: (0, 0, 0, 0))],
        out_specs=pl.BlockSpec((ROWS, HEADS * HEAD_DIM), lambda i: (0, 0)),
        name="combine",
    )(parts)


def places(x, pair_x, shape):
    n = lax.broadcasted_iota(jnp.int32, shape, 1)
    return (
        jnp.where(n < 2 * ROWS, x, pair_x) * ROWS
        + (lax.shift_right_logical(n, 7) & 1) * SPAN
        + (n & (ROWS - 1))
    )


def find_documents(int_ref, first_ref, lo_ref, hi_ref):
    x, pair_x = int_ref[1], int_ref[3]
    base = int_ref[0] * GROUP
    pos = places(x, pair_x, (8, TILE)) + lax.broadcasted_iota(jnp.int32, (8, TILE), 0) * WIDE
    lowest = jnp.minimum(x, pair_x) * ROWS
    highest = SPAN + jnp.maximum(x, pair_x) * ROWS + ROWS - 1
    start = -base
    first = jnp.zeros((8, TILE), jnp.int32) - base
    los = [start] * TILES
    his = [start] * TILES
    for j in range(DOCS - 1):
        start = start + int_ref[PLACE + j]
        first = jnp.where(pos >= start, start, first)
        los = [jnp.where(lowest + i * WIDE >= start, start, los[i]) for i in range(TILES)]
        his = [jnp.where(highest + i * WIDE >= start, start, his[i]) for i in range(TILES)]
    first_ref[...] = first
    for i in range(TILES):
        lo_ref[i] = lax.shift_right_arithmetic(los[i], WIDE_SHIFT)
        hi_ref[i] = lax.shift_right_arithmetic(his[i], WIDE_SHIFT)


def key_places(x, pair_x):
    row = lax.broadcasted_iota(jnp.int32, (HALF, HALF), 0)
    return jnp.where(row < ROWS, x, pair_x) * ROWS + (row & (ROWS - 1))


def load_queries(q_own_ref, q_pair_ref, i):
    return jnp.concatenate(
        [q_own_ref[2 * i], q_own_ref[2 * i + 1], q_pair_ref[2 * i], q_pair_ref[2 * i + 1]],
        axis=1,
    )


def piece(n):
    return slice(n * HALF, (n + 1) * HALF)


def scores_of(refs, s_ref, q, g, n, m, kept, c):
    k = jnp.concatenate([ref[2 * g + n, :ROWS, :] for ref in refs], axis=0)
    s = jnp.dot(k, q[:, piece(c)], preferred_element_type=jnp.float32)
    if kept is not None:
        s = jnp.where(kept, s, NEG)
    s_ref[g, piece(n), piece(c)] = s
    return jnp.maximum(m, jnp.max(s.reshape(HALF // 8, 8, HALF), axis=0))


def mix(refs, s_ref, g, n, c, shift, l, acc):
    p = jnp.exp2(s_ref[g, piece(n), piece(c)] * C - shift[:, piece(c)])
    l = l + jnp.sum(p.reshape(HALF // 8, 8, HALF), axis=0)
    vt = jnp.concatenate([ref[2 * g + n, ROWS:, :] for ref in refs], axis=1)
    acc = acc + jnp.dot(vt, p.astype(jnp.bfloat16), preferred_element_type=jnp.float32)
    return l, acc


def mix_block(refs, s_ref, g, shift, l, acc):
    l, acc = list(l), list(acc)
    for n in range(2):
        for c in range(2):
            l[c], acc[c] = mix(refs, s_ref, g, n, c, shift, l[c], acc[c])
    return tuple(l), tuple(acc)


def sums_and_scores(refs, s_ref, g, shift, score, m, l, acc):
    m, l, acc = list(m), list(l), list(acc)
    for n in range(2):
        for c in range(2):
            l[c], acc[c] = mix(refs, s_ref, g, n, c, shift, l[c], acc[c])
            m[c] = score(n, c, m[c])
    return tuple(m), tuple(l), tuple(acc)


def joined(parts):
    return jnp.concatenate(parts, axis=1)


def shift_of(top):
    return jnp.where(top > 0.5 * NEG, top * C, 0.0)


def own_kernel(
    int_ref,
    q_own_ref,
    q_pair_ref,
    own_ref,
    pair_ref,
    acc_ref,
    state_ref,
    first_ref,
    lo_ref,
    hi_ref,
    even_ref,
    odd_ref,
):
    blk, x, slot = int_ref[0], int_ref[1], int_ref[2]

    @pl.when(slot < HEADS)
    def _():
        find_documents(int_ref, first_ref, lo_ref, hi_ref)

        refs = (own_ref, pair_ref)
        key_rows = key_places(x, int_ref[4])

        def score(s_ref, i, q, g, masked, diagonal, n, c, m):
            kept = None
            if masked:
                kept = key_rows >= first_ref[i : i + 1, piece(c)] - (g * WIDE + n * SPAN)
                if diagonal:
                    kept &= key_rows <= places(x, int_ref[3], (1, TILE))[:, piece(c)] - n * SPAN
            return scores_of(refs, s_ref, q, g, n, m, kept, c)

        def score_diagonal(s_ref, i, q, m):
            m = list(m)
            for n in range(2):
                for c in range(2):
                    m[c] = score(s_ref, i, q, i, True, True, n, c, m[c])
            return tuple(m)

        none = (jnp.full((8, HALF), NEG, jnp.float32),) * 2
        zeros = (jnp.zeros((8, HALF), jnp.float32),) * 2
        buffers = (even_ref, odd_ref)
        q = load_queries(q_own_ref, q_pair_ref, 0)
        m = score_diagonal(even_ref, 0, q, none)
        for i in range(TILES):
            s_ref, later_ref = buffers[i % 2], buffers[(i + 1) % 2]
            top = jnp.max(joined(m), axis=0, keepdims=True)
            shift = shift_of(top)
            begin = jnp.maximum(lo_ref[i], 0)
            sums = (zeros, (jnp.zeros((HEAD_DIM, HALF), jnp.float32),) * 2)
            if i + 1 < TILES:
                q = load_queries(q_own_ref, q_pair_ref, i + 1)

                def step(masked, g, carry, i=i, q=q, shift=shift, s_ref=s_ref, later_ref=later_ref):
                    later = functools.partial(score, later_ref, i + 1, q, g, masked, False)
                    return sums_and_scores(refs, s_ref, g, shift, later, *carry)

                carry = (none,) + sums
                if i > 0:
                    middle = jnp.clip(hi_ref[i + 1] + 1, begin, i)
                    carry = lax.fori_loop(begin, middle, functools.partial(step, True), carry)
                    carry = lax.fori_loop(middle, i, functools.partial(step, False), carry)
                m, l, acc = step(True, i, carry)
                m = score_diagonal(later_ref, i + 1, q, m)
            else:
                l, acc = lax.fori_loop(
                    begin,
                    i + 1,
                    lambda g, c, s_ref=s_ref, shift=shift: mix_block(refs, s_ref, g, shift, *c),
                    sums,
                )
            l = jnp.sum(joined(l), axis=0, keepdims=True)
            row = lax.broadcasted_iota(jnp.int32, (8, TILE), 0)
            acc_ref[i] = joined(acc)
            state_ref[i] = jnp.where(row == 0, l, top)


def prev_kernel(
    int_ref,
    q_own_ref,
    q_pair_ref,
    prev_own_ref,
    prev_pair_ref,
    acc_ref,
    state_ref,
    o_ref,
    first_ref,
    lo_ref,
    hi_ref,
    even_ref,
    odd_ref,
):
    blk, x, slot = int_ref[0], int_ref[1], int_ref[2]

    @pl.when(slot < HEADS)
    def _():
        @pl.when(blk > 0)
        def _():
            find_documents(int_ref, first_ref, lo_ref, hi_ref)

        def begin_of(i):
            return jnp.where(blk > 0, jnp.clip(lo_ref[i] + TILES, 0, TILES), TILES)

        refs = (prev_own_ref, prev_pair_ref)
        key_rows = key_places(x, int_ref[4])

        def score(s_ref, i, q, g, masked, n, c, m):
            kept = None
            if masked:
                start = first_ref[i : i + 1, piece(c)] - ((g - TILES) * WIDE + n * SPAN)
                kept = key_rows >= start
            return scores_of(refs, s_ref, q, g, n, m, kept, c)

        def score_first(masked, g, m):
            m = list(m)
            for n in range(2):
                for c in range(2):
                    m[c] = score(even_ref, 0, q, g, masked, n, c, m[c])
            return tuple(m)

        def middle_of(i, begin):
            return jnp.clip(hi_ref[i] + TILES + 1, begin, TILES)

        none = (jnp.full((8, HALF), NEG, jnp.float32),) * 2
        zeros = (jnp.zeros((8, HALF), jnp.float32),) * 2
        buffers = (even_ref, odd_ref)
        q = load_queries(q_own_ref, q_pair_ref, 0)
        begin = begin_of(0)
        middle = middle_of(0, begin)
        m = lax.fori_loop(begin, middle, functools.partial(score_first, True), none)
        m = lax.fori_loop(middle, TILES, functools.partial(score_first, False), m)
        for i in range(TILES):
            s_ref, later_ref = buffers[i % 2], buffers[(i + 1) % 2]
            own_l, own_top = state_ref[i, 0:1, :], state_ref[i, 1:2, :]
            top = jnp.maximum(jnp.max(joined(m), axis=0, keepdims=True), own_top)
            shift = shift_of(top)
            scale = jnp.where(own_top > 0.5 * NEG, jnp.exp2(own_top * C - shift), 0.0)
            begin = begin_of(i)
            scaled = acc_ref[i] * scale
            sums = (zeros, (scaled[:, piece(0)], scaled[:, piece(1)]))
            if i + 1 < TILES:
                q = load_queries(q_own_ref, q_pair_ref, i + 1)

                def step(masked, g, carry, i=i, q=q, shift=shift, s_ref=s_ref, later_ref=later_ref):
                    later = functools.partial(score, later_ref, i + 1, q, g, masked)
                    return sums_and_scores(refs, s_ref, g, shift, later, *carry)

                middle = middle_of(i + 1, begin)
                carry = (none,) + sums
                carry = lax.fori_loop(begin, middle, functools.partial(step, True), carry)
                m, l, acc = lax.fori_loop(middle, TILES, functools.partial(step, False), carry)
            else:
                l, acc = lax.fori_loop(
                    begin,
                    TILES,
                    lambda g, c, s_ref=s_ref, shift=shift: mix_block(refs, s_ref, g, shift, *c),
                    sums,
                )
            l = jnp.sum(joined(l), axis=0, keepdims=True) + own_l * scale
            some = l > 0.0
            l = jnp.where(some, l, 1.0)
            o = (joined(acc) * (1.0 / l)).astype(jnp.bfloat16)
            log = jnp.where(some, shift + jnp.log(l) * LOG2E, NEG)
            high = log.astype(jnp.bfloat16).astype(jnp.float32)
            middle = (log - high).astype(jnp.bfloat16).astype(jnp.float32)
            low = log - high - middle
            row = lax.broadcasted_iota(jnp.int32, (STATS, TILE), 0)
            stats = jnp.where(row == 0, high, jnp.where(row == 1, middle, low))
            stats = stats.astype(jnp.bfloat16)
            for n in range(4):
                part = slice(n * ROWS, (n + 1) * ROWS)
                y, to = 2 * i + (n & 1), int_ref[5] ^ (n >> 1)
                o_ref[to, y, :ROWS, :] = o[:, part]
                o_ref[to, y, ROWS:, :] = stats[:, part]


SCRATCH = [
    pltpu.VMEM((8, TILE), jnp.int32),
    pltpu.SMEM((TILES,), jnp.int32),
    pltpu.SMEM((TILES,), jnp.int32),
    pltpu.VMEM((TILES, TILE, TILE), jnp.float32),
    pltpu.VMEM((TILES, TILE, TILE), jnp.float32),
]
SMEM = pl.BlockSpec(memory_space=pltpu.SMEM)
VMEM = pl.BlockSpec(memory_space=pltpu.VMEM)
ACC = (TILES, HEAD_DIM, TILE)


def attend_own(ints, q_own, q_pair, own, pair):
    return pl.pallas_call(
        own_kernel,
        out_shape=(
            jax.ShapeDtypeStruct(ACC, jnp.float32),
            jax.ShapeDtypeStruct((TILES, 8, TILE), jnp.float32),
        ),
        in_specs=[SMEM] + [VMEM] * 4,
        out_specs=(VMEM, VMEM),
        scratch_shapes=SCRATCH,
        compiler_params=pltpu.CompilerParams(vmem_limit_bytes=16 << 20),
        cost_estimate=pl.CostEstimate(
            flops=1 << 30, bytes_accessed=4 << 20, transcendentals=2 << 20
        ),
        name="attend_own",
    )(ints, q_own, q_pair, own, pair)


def attend_prev(ints, q_own, q_pair, prev_own, prev_pair, acc, state):
    return pl.pallas_call(
        prev_kernel,
        out_shape=jax.ShapeDtypeStruct((2, Y, ROWS + STATS, HEAD_DIM), jnp.bfloat16),
        in_specs=[SMEM] + [VMEM] * 6,
        out_specs=VMEM,
        scratch_shapes=SCRATCH,
        compiler_params=pltpu.CompilerParams(vmem_limit_bytes=16 << 20),
        cost_estimate=pl.CostEstimate(
            flops=1 << 29, bytes_accessed=4 << 20, transcendentals=1 << 20
        ),
        name="attend_prev",
    )(ints, q_own, q_pair, prev_own, prev_pair, acc, state)


def body(queries, keys, values, lengths):
    chip = lax.axis_index("tokens")
    blk, x, y = chip // CHIPS, chip % X, chip // X % Y
    first = blk == 0
    pairs = [jnp.where(first, x ^ 1, x ^ 3), jnp.where(first, x ^ 3, x ^ 1)]
    place = jnp.stack([blk, x, y, *pairs, jnp.where(first, x & 1, x // 2)]).astype(jnp.int32)
    ints = jnp.concatenate([place, lengths])
    packed = pack(queries, keys, values)
    got = lax.all_to_all(packed, "tokens", 0, 0, tiled=True, axis_index_groups=COLUMNS)
    own_queries, own = got[:, :ROWS], got[:, ROWS:]
    pair = lax.ppermute(own, "tokens", KEY_PAIRS)
    pair_queries = lax.ppermute(own_queries, "tokens", QUERY_PAIRS)
    prev_own = lax.ppermute(own, "tokens", PREV_OWN)
    later, pair, pair_queries, ints = lax.optimization_barrier((own, pair, pair_queries, ints))
    prev_pair = lax.ppermute(later, "tokens", PREV_PAIR)
    state = attend_own(ints, own_queries, pair_queries, own, pair)
    parts = attend_prev(ints, own_queries, pair_queries, prev_own, prev_pair, *state)
    parts = parts.reshape(2 * Y, ROWS + STATS, HEAD_DIM)
    parts = lax.all_to_all(parts, "tokens", 0, 0, tiled=True, axis_index_groups=COLUMN_PAIRS)
    return combine(parts.reshape(2, Y, ROWS + STATS, HEAD_DIM))


def solution(mesh):
    devices = mesh.devices.reshape(2 * CHIPS, mesh.devices.shape[2])
    rows = P("tokens", "tp")
    return jax.shard_map(
        body,
        mesh=Mesh(devices, ("tokens", "tp")),
        in_specs=(rows, rows, rows, P()),
        out_specs=rows,
        check_vma=False,
    )
```

```python
import functools
import math

import jax
import jax.numpy as jnp
from jax import lax
from jax.experimental import pallas as pl
from jax.experimental.pallas import tpu as pltpu
from jax.sharding import Mesh, PartitionSpec as P

HEAD_DIM = 128
ROWS = 128
X = 4
Y = 8
HEADS = 5
DOCS = 32
SPAN = X * ROWS
WIDE = 2 * SPAN
WIDE_SHIFT = 10
TILE = 4 * ROWS
HALF = TILE // 2
TILES = Y // 2
GROUP = Y * SPAN
STATS = 16
PLACE = 6
NEG = -1e30
LOG2E = math.log2(math.e)
C = LOG2E / math.sqrt(HEAD_DIM)
CHIPS = X * Y
KEY_PAIRS = [(n, n ^ (3 if n >= CHIPS else 1)) for n in range(2 * CHIPS)]
QUERY_PAIRS = [(n, n ^ (1 if n >= CHIPS else 3)) for n in range(2 * CHIPS)]
PREV_OWN = [(n, CHIPS + n) for n in range(CHIPS)]
PREV_PAIR = [(n, CHIPS + (n ^ 3)) for n in range(CHIPS)]
COLUMNS = [[g * CHIPS + y * X + x for y in range(Y)] for g in range(2) for x in range(X)]
COLUMN_PAIRS = [COLUMNS[a] + COLUMNS[b] for a, b in ((0, 3), (1, 2), (4, 5), (6, 7))]


def pack_kernel(q_ref, k_ref, v_ref, out_ref):
    for h in range(HEADS):
        cols = slice(h * HEAD_DIM, (h + 1) * HEAD_DIM)
        out_ref[h, :ROWS, :] = q_ref[:, cols].T
        out_ref[h, ROWS : 2 * ROWS, :] = k_ref[:, cols]
        out_ref[h, 2 * ROWS :, :] = v_ref[:, cols].T


def pack(q, k, v):
    return pl.pallas_call(
        pack_kernel,
        out_shape=jax.ShapeDtypeStruct((Y, 2 * ROWS + HEAD_DIM, HEAD_DIM), jnp.bfloat16),
        name="pack",
    )(q, k, v)


def combine_kernel(in_ref, out_ref):
    for h in range(HEADS):
        logs = []
        for n in range(2):
            terms = in_ref[n, h, ROWS:, :].astype(jnp.float32)
            logs.append(terms[0:1] + terms[1:2] + terms[2:3])
        top = jnp.maximum(logs[0], logs[1])
        a, b = jnp.exp2(logs[0] - top), jnp.exp2(logs[1] - top)
        o = in_ref[0, h, :ROWS, :].astype(jnp.float32) * (a / (a + b))
        o += in_ref[1, h, :ROWS, :].astype(jnp.float32) * (b / (a + b))
        out_ref[:, h * HEAD_DIM : (h + 1) * HEAD_DIM] = o.T.astype(jnp.bfloat16)


def combine(parts):
    shape = (2, HEADS, ROWS + STATS, HEAD_DIM)
    return pl.pallas_call(
        combine_kernel,
        grid=(1,),
        out_shape=jax.ShapeDtypeStruct((ROWS, HEADS * HEAD_DIM), jnp.bfloat16),
        in_specs=[pl.BlockSpec(shape, lambda i: (0, 0, 0, 0))],
        out_specs=pl.BlockSpec((ROWS, HEADS * HEAD_DIM), lambda i: (0, 0)),
        name="combine",
    )(parts)


def places(x, pair_x, shape):
    n = lax.broadcasted_iota(jnp.int32, shape, 1)
    return (
        jnp.where(n < 2 * ROWS, x, pair_x) * ROWS
        + (lax.shift_right_logical(n, 7) & 1) * SPAN
        + (n & (ROWS - 1))
    )


def find_documents(int_ref, first_ref, lo_ref, hi_ref):
    x, pair_x = int_ref[1], int_ref[3]
    base = int_ref[0] * GROUP
    pos = places(x, pair_x, (8, TILE)) + lax.broadcasted_iota(jnp.int32, (8, TILE), 0) * WIDE
    lowest = jnp.minimum(x, pair_x) * ROWS
    highest = SPAN + jnp.maximum(x, pair_x) * ROWS + ROWS - 1
    start = -base
    first = jnp.zeros((8, TILE), jnp.int32) - base
    los = [start] * TILES
    his = [start] * TILES
    for j in range(DOCS - 1):
        start = start + int_ref[PLACE + j]
        first = jnp.where(pos >= start, start, first)
        los = [jnp.where(lowest + i * WIDE >= start, start, los[i]) for i in range(TILES)]
        his = [jnp.where(highest + i * WIDE >= start, start, his[i]) for i in range(TILES)]
    first_ref[...] = first
    for i in range(TILES):
        lo_ref[i] = lax.shift_right_arithmetic(los[i], WIDE_SHIFT)
        hi_ref[i] = lax.shift_right_arithmetic(his[i], WIDE_SHIFT)


def key_places(x, pair_x):
    row = lax.broadcasted_iota(jnp.int32, (HALF, HALF), 0)
    return jnp.where(row < ROWS, x, pair_x) * ROWS + (row & (ROWS - 1))


def load_queries(q_own_ref, q_pair_ref, i):
    return jnp.concatenate(
        [q_own_ref[2 * i], q_own_ref[2 * i + 1], q_pair_ref[2 * i], q_pair_ref[2 * i + 1]],
        axis=1,
    )


def piece(n):
    return slice(n * HALF, (n + 1) * HALF)


def scores_of(refs, s_ref, q, g, n, m, kept, c):
    k = jnp.concatenate([ref[2 * g + n, :ROWS, :] for ref in refs], axis=0)
    s = jnp.dot(k, q[:, piece(c)], preferred_element_type=jnp.float32)
    if kept is not None:
        s = jnp.where(kept, s, NEG)
    s_ref[g, piece(n), piece(c)] = s
    return jnp.maximum(m, jnp.max(s.reshape(HALF // 8, 8, HALF), axis=0))


def mix(refs, s_ref, g, n, c, shift, l, acc):
    p = jnp.exp2(s_ref[g, piece(n), piece(c)] * C - shift[:, piece(c)])
    l = l + jnp.sum(p.reshape(HALF // 8, 8, HALF), axis=0)
    vt = jnp.concatenate([ref[2 * g + n, ROWS:, :] for ref in refs], axis=1)
    acc = acc + jnp.dot(vt, p.astype(jnp.bfloat16), preferred_element_type=jnp.float32)
    return l, acc


def mix_block(refs, s_ref, g, shift, l, acc):
    l, acc = list(l), list(acc)
    for n in range(2):
        for c in range(2):
            l[c], acc[c] = mix(refs, s_ref, g, n, c, shift, l[c], acc[c])
    return tuple(l), tuple(acc)


def sums_and_scores(refs, s_ref, g, shift, score, m, l, acc):
    m, l, acc = list(m), list(l), list(acc)
    for n in range(2):
        for c in range(2):
            l[c], acc[c] = mix(refs, s_ref, g, n, c, shift, l[c], acc[c])
            m[c] = score(n, c, m[c])
    return tuple(m), tuple(l), tuple(acc)


def joined(parts):
    return jnp.concatenate(parts, axis=1)


def shift_of(top):
    return jnp.where(top > 0.5 * NEG, top * C, 0.0)


def own_kernel(
    int_ref,
    q_own_ref,
    q_pair_ref,
    own_ref,
    pair_ref,
    acc_ref,
    state_ref,
    first_ref,
    lo_ref,
    hi_ref,
    even_ref,
    odd_ref,
):
    blk, x, slot = int_ref[0], int_ref[1], int_ref[2]

    @pl.when(slot < HEADS)
    def _():
        find_documents(int_ref, first_ref, lo_ref, hi_ref)

        refs = (own_ref, pair_ref)
        key_rows = key_places(x, int_ref[4])

        def score(s_ref, i, q, g, masked, diagonal, n, c, m):
            kept = None
            if masked:
                kept = key_rows >= first_ref[i : i + 1, piece(c)] - (g * WIDE + n * SPAN)
                if diagonal:
                    kept &= key_rows <= places(x, int_ref[3], (1, TILE))[:, piece(c)] - n * SPAN
            return scores_of(refs, s_ref, q, g, n, m, kept, c)

        def score_diagonal(s_ref, i, q, m):
            m = list(m)
            for n in range(2):
                for c in range(2):
                    m[c] = score(s_ref, i, q, i, True, True, n, c, m[c])
            return tuple(m)

        none = (jnp.full((8, HALF), NEG, jnp.float32),) * 2
        zeros = (jnp.zeros((8, HALF), jnp.float32),) * 2
        buffers = (even_ref, odd_ref)
        q = load_queries(q_own_ref, q_pair_ref, 0)
        m = score_diagonal(even_ref, 0, q, none)
        for i in range(TILES):
            s_ref, later_ref = buffers[i % 2], buffers[(i + 1) % 2]
            top = jnp.max(joined(m), axis=0, keepdims=True)
            shift = shift_of(top)
            begin = jnp.maximum(lo_ref[i], 0)
            sums = (zeros, (jnp.zeros((HEAD_DIM, HALF), jnp.float32),) * 2)
            if i + 1 < TILES:
                q = load_queries(q_own_ref, q_pair_ref, i + 1)

                def step(masked, g, carry, i=i, q=q, shift=shift, s_ref=s_ref, later_ref=later_ref):
                    later = functools.partial(score, later_ref, i + 1, q, g, masked, False)
                    return sums_and_scores(refs, s_ref, g, shift, later, *carry)

                carry = (none,) + sums
                if i > 0:
                    middle = jnp.clip(hi_ref[i + 1] + 1, begin, i)
                    carry = lax.fori_loop(begin, middle, functools.partial(step, True), carry)
                    carry = lax.fori_loop(middle, i, functools.partial(step, False), carry)
                m, l, acc = step(True, i, carry)
                m = score_diagonal(later_ref, i + 1, q, m)
            else:
                l, acc = lax.fori_loop(
                    begin,
                    i + 1,
                    lambda g, c, s_ref=s_ref, shift=shift: mix_block(refs, s_ref, g, shift, *c),
                    sums,
                )
            l = jnp.sum(joined(l), axis=0, keepdims=True)
            row = lax.broadcasted_iota(jnp.int32, (8, TILE), 0)
            acc_ref[i] = joined(acc)
            state_ref[i] = jnp.where(row == 0, l, top)


def prev_kernel(
    int_ref,
    q_own_ref,
    q_pair_ref,
    prev_own_ref,
    prev_pair_ref,
    acc_ref,
    state_ref,
    o_ref,
    first_ref,
    lo_ref,
    hi_ref,
    even_ref,
    odd_ref,
):
    blk, x, slot = int_ref[0], int_ref[1], int_ref[2]

    @pl.when(slot < HEADS)
    def _():
        @pl.when(blk > 0)
        def _():
            find_documents(int_ref, first_ref, lo_ref, hi_ref)

        def begin_of(i):
            return jnp.where(blk > 0, jnp.clip(lo_ref[i] + TILES, 0, TILES), TILES)

        refs = (prev_own_ref, prev_pair_ref)
        key_rows = key_places(x, int_ref[4])

        def score(s_ref, i, q, g, masked, n, c, m):
            kept = None
            if masked:
                start = first_ref[i : i + 1, piece(c)] - ((g - TILES) * WIDE + n * SPAN)
                kept = key_rows >= start
            return scores_of(refs, s_ref, q, g, n, m, kept, c)

        def score_first(masked, g, m):
            m = list(m)
            for n in range(2):
                for c in range(2):
                    m[c] = score(even_ref, 0, q, g, masked, n, c, m[c])
            return tuple(m)

        def middle_of(i, begin):
            return jnp.clip(hi_ref[i] + TILES + 1, begin, TILES)

        none = (jnp.full((8, HALF), NEG, jnp.float32),) * 2
        zeros = (jnp.zeros((8, HALF), jnp.float32),) * 2
        buffers = (even_ref, odd_ref)
        q = load_queries(q_own_ref, q_pair_ref, 0)
        begin = begin_of(0)
        middle = middle_of(0, begin)
        m = lax.fori_loop(begin, middle, functools.partial(score_first, True), none)
        m = lax.fori_loop(middle, TILES, functools.partial(score_first, False), m)
        for i in range(TILES):
            s_ref, later_ref = buffers[i % 2], buffers[(i + 1) % 2]
            own_l, own_top = state_ref[i, 0:1, :], state_ref[i, 1:2, :]
            top = jnp.maximum(jnp.max(joined(m), axis=0, keepdims=True), own_top)
            shift = shift_of(top)
            scale = jnp.where(own_top > 0.5 * NEG, jnp.exp2(own_top * C - shift), 0.0)
            begin = begin_of(i)
            scaled = acc_ref[i] * scale
            sums = (zeros, (scaled[:, piece(0)], scaled[:, piece(1)]))
            if i + 1 < TILES:
                q = load_queries(q_own_ref, q_pair_ref, i + 1)

                def step(masked, g, carry, i=i, q=q, shift=shift, s_ref=s_ref, later_ref=later_ref):
                    later = functools.partial(score, later_ref, i + 1, q, g, masked)
                    return sums_and_scores(refs, s_ref, g, shift, later, *carry)

                middle = middle_of(i + 1, begin)
                carry = (none,) + sums
                carry = lax.fori_loop(begin, middle, functools.partial(step, True), carry)
                m, l, acc = lax.fori_loop(middle, TILES, functools.partial(step, False), carry)
            else:
                l, acc = lax.fori_loop(
                    begin,
                    TILES,
                    lambda g, c, s_ref=s_ref, shift=shift: mix_block(refs, s_ref, g, shift, *c),
                    sums,
                )
            l = jnp.sum(joined(l), axis=0, keepdims=True) + own_l * scale
            some = l > 0.0
            l = jnp.where(some, l, 1.0)
            o = (joined(acc) * (1.0 / l)).astype(jnp.bfloat16)
            log = jnp.where(some, shift + jnp.log(l) * LOG2E, NEG)
            high = log.astype(jnp.bfloat16).astype(jnp.float32)
            middle = (log - high).astype(jnp.bfloat16).astype(jnp.float32)
            low = log - high - middle
            row = lax.broadcasted_iota(jnp.int32, (STATS, TILE), 0)
            stats = jnp.where(row == 0, high, jnp.where(row == 1, middle, low))
            stats = stats.astype(jnp.bfloat16)
            for n in range(4):
                part = slice(n * ROWS, (n + 1) * ROWS)
                y, to = 2 * i + (n & 1), int_ref[5] ^ (n >> 1)
                o_ref[to, y, :ROWS, :] = o[:, part]
                o_ref[to, y, ROWS:, :] = stats[:, part]


SCRATCH = [
    pltpu.VMEM((8, TILE), jnp.int32),
    pltpu.SMEM((TILES,), jnp.int32),
    pltpu.SMEM((TILES,), jnp.int32),
    pltpu.VMEM((TILES, TILE, TILE), jnp.float32),
    pltpu.VMEM((TILES, TILE, TILE), jnp.float32),
]
SMEM = pl.BlockSpec(memory_space=pltpu.SMEM)
VMEM = pl.BlockSpec(memory_space=pltpu.VMEM)
ACC = (TILES, HEAD_DIM, TILE)


def attend_own(ints, q_own, q_pair, own, pair):
    return pl.pallas_call(
        own_kernel,
        out_shape=(
            jax.ShapeDtypeStruct(ACC, jnp.float32),
            jax.ShapeDtypeStruct((TILES, 8, TILE), jnp.float32),
        ),
        in_specs=[SMEM] + [VMEM] * 4,
        out_specs=(VMEM, VMEM),
        scratch_shapes=SCRATCH,
        compiler_params=pltpu.CompilerParams(vmem_limit_bytes=16 << 20),
        cost_estimate=pl.CostEstimate(
            flops=1 << 30, bytes_accessed=4 << 20, transcendentals=2 << 20
        ),
        name="attend_own",
    )(ints, q_own, q_pair, own, pair)


def attend_prev(ints, q_own, q_pair, prev_own, prev_pair, acc, state):
    return pl.pallas_call(
        prev_kernel,
        out_shape=jax.ShapeDtypeStruct((2, Y, ROWS + STATS, HEAD_DIM), jnp.bfloat16),
        in_specs=[SMEM] + [VMEM] * 6,
        out_specs=VMEM,
        scratch_shapes=SCRATCH,
        compiler_params=pltpu.CompilerParams(vmem_limit_bytes=16 << 20),
        cost_estimate=pl.CostEstimate(
            flops=1 << 29, bytes_accessed=4 << 20, transcendentals=1 << 20
        ),
        name="attend_prev",
    )(ints, q_own, q_pair, prev_own, prev_pair, acc, state)


def body(queries, keys, values, lengths):
    chip = lax.axis_index("tokens")
    blk, x, y = chip // CHIPS, chip % X, chip // X % Y
    first = blk == 0
    pairs = [jnp.where(first, x ^ 3, x ^ 1), jnp.where(first, x ^ 1, x ^ 3)]
    place = jnp.stack([blk, x, y, *pairs, jnp.where(first, x // 2, x & 1)]).astype(jnp.int32)
    ints = jnp.concatenate([place, lengths])
    packed = pack(queries, keys, values)
    got = lax.all_to_all(packed, "tokens", 0, 0, tiled=True, axis_index_groups=COLUMNS)
    own_queries, own = got[:, :ROWS], got[:, ROWS:]
    pair = lax.ppermute(own, "tokens", KEY_PAIRS)
    pair_queries = lax.ppermute(own_queries, "tokens", QUERY_PAIRS)
    prev_own = lax.ppermute(own, "tokens", PREV_OWN)
    later, pair_queries, ints = lax.optimization_barrier((own, pair_queries, ints))
    prev_pair = lax.ppermute(later, "tokens", PREV_PAIR)
    state = attend_own(ints, own_queries, pair_queries, own, pair)
    parts = attend_prev(ints, own_queries, pair_queries, prev_own, prev_pair, *state)
    parts = parts.reshape(2 * Y, ROWS + STATS, HEAD_DIM)
    parts = lax.all_to_all(parts, "tokens", 0, 0, tiled=True, axis_index_groups=COLUMN_PAIRS)
    return combine(parts.reshape(2, Y, ROWS + STATS, HEAD_DIM))


def solution(mesh):
    devices = mesh.devices.reshape(2 * CHIPS, mesh.devices.shape[2])
    rows = P("tokens", "tp")
    return jax.shard_map(
        body,
        mesh=Mesh(devices, ("tokens", "tp")),
        in_specs=(rows, rows, rows, P()),
        out_specs=rows,
        check_vma=False,
    )
```
